32 devices in a mesh: dp: 4 (over z), row: 4 (over y, x), col: 2 (over core).
Axes of the slice: x: 2, y: 2, z: 4, core: 2. Of those that a mesh axis runs over, the one named last changes fastest.
Arguments:
- tokens: bfloat16 [6304, 512], P(('dp', 'row'), 'col'), may hold values from -6 to 6
- norm_gain: float32 [2, 2, 512], P(None, None, 'col'), may hold values from 0.5 to 1.5
- norm_shift: float32 [2, 2, 512], P(None, None, 'col'), may hold values from -3 to 3
- w_qkv: bfloat16 [2, 512, 3, 512], P(None, 'col', None, 'row'), may hold values from -0.25 to 0.25
- w_proj: bfloat16 [2, 512, 512], P(None, 'row', 'col'), may hold values from -0.75 to 0.75
- w_router: bfloat16 [2, 512, 32], P(None, 'col'), may hold values from -0.25 to 0.25
- w_in: bfloat16 [2, 32, 512, 2048], P(None, None, 'col', 'row'), may hold values from -0.25 to 0.25
- w_out: bfloat16 [2, 32, 2048, 512], P(None, None, 'row', 'col'), may hold values from -2 to 2
- expert_ids: int32 [2, 6304, 2], P(None, 'dp'), may hold values from 0 to 31, as said below
- slot_ids: int32 [2, 6304, 2], P(None, 'dp'), may hold values from 0 to 123, as said below
- cotangent: bfloat16 [6304, 512], P(('dp', 'row'), 'col'), may hold values from -6 to 6
Outputs:
- output: bfloat16 [6304, 512], P(('dp', 'row'), 'col')
- grad_input: float32 [6304, 512], P(('dp', 'row'), 'col')
- grad_qkv: float32 [2, 512, 3, 512], P(None, 'col', None, 'row')
- grad_proj: float32 [2, 512, 512], P(None, 'row', 'col')
- grad_router: float32 [2, 512, 32], P(None, 'col')
- grad_in: float32 [2, 32, 512, 2048], P(None, 'dp', 'col', 'row')
- grad_out: float32 [2, 32, 2048, 512], P(None, 'dp', 'row', 'col')
- grad_gain: float32 [2, 2, 512], P(None, None, 'col')
- grad_shift: float32 [2, 2, 512], P(None, None, 'col')
The draws below stay inside these ranges and needn't reach their ends.
Inputs may be any that keep to these rules, and one draw needn't show every extreme that they name: `expert_ids`: in each layer and each group of 1576 consecutive tokens, a token's two experts differ, no expert is named by more than 124 tokens, and some expert is named by exactly 124 tokens. `slot_ids`: in each layer, group and expert, the tokens that name the expert have different slots.
All inputs are finite; a program needn't handle non-finite values.
Results may differ from the reference program's by a relative error of at most 0.015.
Values may be sent and summed in bfloat16 or wider, within the bound.
No kernel may reach another device: no remote copies, remote signals or barrier semaphores. Data moves between devices by JAX's collectives and lax.ppermute only.
A program may use at most 256 MiB of HBM per device.

```python
import jax
import jax.numpy as jnp
from jax import lax

D = 512
HEADS = 8
HDIM = 64
H = 2048
EXPERTS = 32
TOP = 2
SEQ = 197
LAYERS = 2
IMG_G = 8
TOKENS = 6304
CAP = 124


def route_table(key):
    base = jax.random.fold_in(key, 29)
    group_rows = IMG_G * SEQ
    groups = TOKENS // group_rows
    half_count = EXPERTS // 2

    def one_side(side_key, labels):
        order_key, token_key = jax.random.split(side_key)
        others = jax.random.permutation(order_key, half_count * CAP - CAP).astype(jnp.int32) + CAP
        chosen = jnp.concatenate([jnp.arange(CAP, dtype=jnp.int32), others])[:group_rows]
        chosen = chosen[jax.random.permutation(token_key, group_rows)]
        return (labels[chosen // CAP], chosen % CAP)

    def one_group(group_key):
        label_key, first_key, second_key = jax.random.split(group_key, 3)
        labels = jax.random.permutation(label_key, EXPERTS).astype(jnp.int32)
        first_experts, first_slots = one_side(first_key, labels[:half_count])
        second_experts, second_slots = one_side(second_key, labels[half_count:])
        return (jnp.stack([first_experts, second_experts], axis=1), jnp.stack([first_slots, second_slots], axis=1))
    group_keys = jax.random.split(base, LAYERS * groups)
    expert_rows, slot_rows = jax.vmap(one_group)(group_keys)
    return (expert_rows.reshape(LAYERS, TOKENS, TOP), slot_rows.reshape(LAYERS, TOKENS, TOP))


def draw_expert_ids(key, part):
    return route_table(key)[0]


def draw_slot_ids(key, part):
    return route_table(key)[1]


def block_scale(key, extent, cuts, least, top_value):
    def one(position, shards_of):
        steps = jax.random.uniform(jax.random.fold_in(jax.random.fold_in(key, 6), position), (shards_of,), jnp.float32, least / len(cuts), top_value / len(cuts))
        return jnp.repeat(jnp.exp(steps), extent[position] // shards_of).reshape((-1,) + (1,) * (len(extent) - position - 1))

    gain = one(*cuts[0])
    for cut in cuts[1:]:
        gain = gain * one(*cut)
    return gain


def normal_values(own_key, extent, deviation, limit, cuts=(), kind=jnp.bfloat16):
    factor_of = block_scale(own_key, extent, cuts, -0.22, 0.18) if cuts else 1.0
    values = jax.random.normal(own_key, extent, jnp.float32) * deviation * factor_of
    return jnp.minimum(jnp.maximum(values, -limit), limit).astype(kind)


def setup_inputs(seed: int = 0) -> dict:
    keys = jax.random.split(jax.random.key(seed), 12)
    tokens = normal_values(keys[0], (TOKENS, D), 1.0, 6.0, ((0, 16), (1, 2)))
    norm_gain = jnp.clip(1.0 + 0.1 * jax.random.normal(keys[1], (LAYERS, 2, D), jnp.float32), 0.5, 1.5)
    norm_shift = normal_values(keys[2], (LAYERS, 2, D), 0.5, 3.0, ((2, 2),), jnp.float32)
    w_qkv = normal_values(keys[3], (LAYERS, D, 3, D), D ** -0.5, 0.25, ((1, 2), (3, 4)))
    w_proj = normal_values(keys[4], (LAYERS, D, D), (D // 8) ** -0.5, 0.75, ((1, 4), (2, 2)))
    w_router = normal_values(keys[5], (LAYERS, D, EXPERTS), D ** -0.5, 0.25, ((1, 2),))
    w_in = normal_values(keys[6], (LAYERS, EXPERTS, D, H), D ** -0.5, 0.25, ((2, 2), (3, 4)))
    w_out = normal_values(keys[7], (LAYERS, EXPERTS, H, D), (max(1, H * 4 // (EXPERTS * EXPERTS))) ** -0.5, 2.0, ((2, 4), (3, 2)))
    expert_ids = draw_expert_ids(jax.random.fold_in(keys[11], 71), 0)
    slot_ids = draw_slot_ids(jax.random.fold_in(keys[11], 71), 0)
    cotangent = normal_values(keys[10], (TOKENS, D), 1.0, 6.0, ((0, 16), (1, 2)))
    return {"tokens": tokens, "norm_gain": norm_gain, "norm_shift": norm_shift, "w_qkv": w_qkv, "w_proj": w_proj, "w_router": w_router, "w_in": w_in, "w_out": w_out, "expert_ids": expert_ids, "slot_ids": slot_ids, "cotangent": cotangent}


EPSILON = 1e-06
PRECISE = lax.Precision.HIGHEST

@jax.custom_vjp
def low(v):
    return lax.optimization_barrier(v.astype(jnp.bfloat16)).astype(jnp.float32)

@jax.custom_vjp
def low_back(v):
    return v

def low_keep(v):
    return (low(v), None)

def low_pass(kept, grad):
    return (grad,)

def back_keep(v):
    return (v, None)

def back_low(kept, grad):
    return (low(grad),)
low.defvjp(low_keep, low_pass)
low_back.defvjp(back_keep, back_low)

def layer_norm(values, gain_row, shift_row):
    center = lax.optimization_barrier(jnp.mean(values, axis=-1, keepdims=True))
    spread = lax.optimization_barrier(jnp.mean(jnp.square(values - center), axis=-1, keepdims=True))
    return (values - center) * lax.rsqrt(spread + EPSILON) * gain_row + shift_row

def softmax_rows(values):
    shifted = jnp.exp(values - lax.optimization_barrier(jnp.max(values, axis=-1, keepdims=True)))
    return shifted / lax.optimization_barrier(jnp.sum(shifted, axis=-1, keepdims=True))

def attend(block):
    query_part, key_part, value_part = (block[:, :, 0], block[:, :, 1], block[:, :, 2])
    scores = low_back(jnp.einsum('bqhd,bkhd->bhqk', query_part, key_part, precision=PRECISE) * HDIM ** (-0.5))
    weights = low(softmax_rows(scores))
    mixed_heads = jnp.einsum('bhqk,bkhd->bqhd', weights, value_part, precision=PRECISE)
    return low_back(low(mixed_heads))

def slot_table(flat_group):
    owners = jnp.broadcast_to(jnp.arange(IMG_G * SEQ, dtype=jnp.int32)[:, None], flat_group.shape)
    empty = jnp.full((EXPERTS * CAP,), IMG_G * SEQ, jnp.int32)
    return empty.at[flat_group.reshape(-1)].set(owners.reshape(-1))

def experts(normed_group, gate_group, flat_group, owner_group, weight_in, weight_out):
    padded = jnp.concatenate([normed_group, jnp.zeros((1, D), jnp.float32)], axis=0)
    buffer = padded[owner_group].reshape(EXPERTS, CAP, D)
    hidden = low_back(jnp.einsum('ecd,edf->ecf', buffer, weight_in, precision=PRECISE))
    active = low(jax.nn.gelu(hidden))
    slot_out = low_back(jnp.einsum('ecf,efd->ecd', active, weight_out, precision=PRECISE)).reshape(EXPERTS * CAP, D)
    return lax.optimization_barrier(jnp.sum(gate_group[:, :, None] * slot_out[flat_group], axis=1))

def whole_layer(stream, gain_pair, shift_pair, weight_qkv, weight_proj, weight_router, weight_in, weight_out, choices, flat_slots, slot_owner):
    normed = low(layer_norm(stream, gain_pair[0], shift_pair[0]))
    packed = low_back(low(jnp.einsum('td,dcf->tcf', normed, weight_qkv, precision=PRECISE)))
    blocks = packed.reshape(-1, IMG_G, SEQ, 3, HEADS, HDIM)
    mixed_heads = lax.map(jax.checkpoint(attend), blocks).reshape(-1, D)
    stream = stream + low_back(jnp.dot(mixed_heads, weight_proj, precision=PRECISE))
    normed = low(layer_norm(stream, gain_pair[1], shift_pair[1]))
    router = softmax_rows(low_back(jnp.dot(normed, weight_router, precision=PRECISE)))
    gate_values = jnp.take_along_axis(router, choices, axis=1)

    def one_group(pieces):
        return experts(pieces[0], pieces[1], pieces[2], pieces[3], weight_in, weight_out)
    group_rows = IMG_G * SEQ
    branch = lax.map(jax.checkpoint(one_group), (normed.reshape(-1, group_rows, D), gate_values.reshape(-1, group_rows, TOP), flat_slots, slot_owner))
    return stream + low_back(branch.reshape(-1, D))

def reference(tokens, norm_gain, norm_shift, w_qkv, w_proj, w_router, w_in, w_out, expert_ids, slot_ids, cotangent):
    group_rows = IMG_G * SEQ
    groups = TOKENS // group_rows
    flat_all = (expert_ids * CAP + slot_ids).astype(jnp.int32).reshape(LAYERS, groups, group_rows, TOP)
    owner_all = jax.vmap(jax.vmap(slot_table))(flat_all)

    def forward(stream, gain_all, shift_all, weights_qkv, weights_proj, weights_router, weights_in, weights_out):
        for layer_index in range(LAYERS):
            stream = whole_layer(stream, gain_all[layer_index], shift_all[layer_index], weights_qkv[layer_index], weights_proj[layer_index], weights_router[layer_index], weights_in[layer_index], weights_out[layer_index], expert_ids[layer_index], flat_all[layer_index], owner_all[layer_index])
        return stream
    primals = (tokens.astype(jnp.float32), norm_gain.astype(jnp.float32), norm_shift.astype(jnp.float32), w_qkv.astype(jnp.float32), w_proj.astype(jnp.float32), w_router.astype(jnp.float32), w_in.astype(jnp.float32), w_out.astype(jnp.float32))
    result, pullback = jax.vjp(forward, *primals)
    gradients = pullback(cotangent.astype(jnp.float32))
    return (result.astype(jnp.bfloat16), gradients[0], gradients[3], gradients[4], gradients[5], gradients[6], gradients[7], gradients[1], gradients[2])
```

```python
import functools

import jax
import jax.numpy as jnp
from jax import lax
from jax.experimental import pallas as pl
from jax.experimental.pallas import tpu as pltpu
from jax.sharding import PartitionSpec as P

HDIM = 64
SEQ = 197


EPSILON = 1e-06


def gather_rows(values):
    return lax.all_gather(values, "row", axis=0, tiled=True)


def sum_rows(values):
    return lax.psum_scatter(values, "row", scatter_dimension=0, tiled=True)


def gather_halves(values):
    return lax.all_gather(values, "col", axis=0, tiled=True)


def sum_halves(values):
    return lax.psum_scatter(values, "col", scatter_dimension=0, tiled=True)


def row_totals(first, second):
    return lax.psum((first, second), "col")


def softmax_rows(values):
    shifted = jnp.exp(values - jnp.max(values, axis=-1, keepdims=True))
    return shifted / jnp.sum(shifted, axis=-1, keepdims=True)


def norm_forward(stream, gain_row, shift_row):
    feature_count = stream.shape[1] * lax.axis_size("col")
    total, squares = row_totals(jnp.sum(stream, axis=1), jnp.sum(stream * stream, axis=1))
    center = total / feature_count
    inverse = lax.rsqrt(squares / feature_count - center * center + EPSILON)
    normal = (stream - center[:, None]) * inverse[:, None]
    return (normal * gain_row + shift_row, normal, inverse)


def norm_backward(upstream, normal, inverse, gain_row):
    feature_count = upstream.shape[1] * lax.axis_size("col")
    scaled = upstream * gain_row
    first, second = row_totals(jnp.sum(scaled, axis=1), jnp.sum(scaled * normal, axis=1))
    result_grad = inverse[:, None] * (
        scaled - first[:, None] / feature_count - normal * (second[:, None] / feature_count)
    )
    return (result_grad, jnp.sum(upstream * normal, axis=0), jnp.sum(upstream, axis=0))


def split_heads(packed):
    row_count = packed.shape[0]
    heads_here = packed.shape[1] // (3 * HDIM)
    parts = packed.reshape(row_count // SEQ, SEQ, 3, heads_here, HDIM)
    return (parts[:, :, 0], parts[:, :, 1], parts[:, :, 2])


def attend_forward(packed):
    query_part, key_part, value_part = split_heads(packed)
    scores = jnp.einsum(
        "bqhd,bkhd->bhqk", query_part, key_part, preferred_element_type=jnp.float32
    ) * HDIM ** (-0.5)
    highest = jnp.max(scores, axis=-1, keepdims=True)
    powers = jnp.exp(scores - highest)
    totals = jnp.sum(powers, axis=-1, keepdims=True)
    weights = (powers / totals).astype(jnp.bfloat16)
    mixed_heads = jnp.einsum(
        "bhqk,bkhd->bqhd", weights, value_part, preferred_element_type=jnp.float32
    )
    return (
        mixed_heads.reshape(packed.shape[0], -1).astype(jnp.bfloat16),
        highest + jnp.log(totals),
    )


def attend_backward(packed, logsum, grad_mixed):
    query_part, key_part, value_part = split_heads(packed)
    scale = HDIM ** (-0.5)
    scores = (
        jnp.einsum("bqhd,bkhd->bhqk", query_part, key_part, preferred_element_type=jnp.float32)
        * scale
    )
    probs_full = jnp.exp(scores - logsum)
    upstream = grad_mixed.reshape(query_part.shape)
    grad_probs = jnp.einsum(
        "bqhd,bkhd->bhqk", upstream, value_part, preferred_element_type=jnp.float32
    )
    grad_values = jnp.einsum(
        "bhqk,bqhd->bkhd",
        probs_full.astype(jnp.bfloat16),
        upstream,
        preferred_element_type=jnp.float32,
    )
    grad_scores = (
        probs_full * (grad_probs - jnp.sum(probs_full * grad_probs, axis=-1, keepdims=True))
    ).astype(jnp.bfloat16)
    grad_query = (
        jnp.einsum("bhqk,bkhd->bqhd", grad_scores, key_part, preferred_element_type=jnp.float32)
        * scale
    )
    grad_keys = (
        jnp.einsum("bhqk,bqhd->bkhd", grad_scores, query_part, preferred_element_type=jnp.float32)
        * scale
    )
    stacked = jnp.stack([grad_query, grad_keys, grad_values], axis=2)
    return stacked.reshape(packed.shape[0], -1).astype(jnp.bfloat16)


def attention_forward(stream, gain_row, shift_row, weight_qkv, weight_proj):
    normed, normal, inverse = norm_forward(stream, gain_row, shift_row)
    normed_all = gather_rows(normed.astype(jnp.bfloat16))
    packed = sum_halves(jnp.dot(normed_all, weight_qkv, preferred_element_type=jnp.float32)).astype(
        jnp.bfloat16
    )
    mixed_heads, logsum = attend_forward(packed)
    mixed_all = gather_halves(mixed_heads)
    branch = sum_rows(jnp.dot(mixed_all, weight_proj, preferred_element_type=jnp.float32))
    saved = {
        "normal": normal,
        "inverse": inverse,
        "normed_all": normed_all,
        "packed": packed,
        "logsum": logsum,
        "mixed_all": mixed_all,
    }
    return (stream + branch, saved)


def attention_backward(upstream, saved, weight_qkv, weight_proj):
    grad_all = gather_rows(upstream.astype(jnp.bfloat16))
    grad_mixed = sum_halves(
        jnp.einsum("te,de->td", grad_all, weight_proj, preferred_element_type=jnp.float32)
    ).astype(jnp.bfloat16)
    grad_w_proj = jnp.einsum(
        "td,te->de", saved["mixed_all"], grad_all, preferred_element_type=jnp.float32
    )
    grad_packed = attend_backward(saved["packed"], saved["logsum"], grad_mixed)
    grad_packed_all = gather_halves(grad_packed)
    grad_part = jnp.einsum(
        "tf,df->td", grad_packed_all, weight_qkv, preferred_element_type=jnp.float32
    )
    grad_w_qkv = jnp.einsum(
        "td,tf->df", saved["normed_all"], grad_packed_all, preferred_element_type=jnp.float32
    )
    return (sum_rows(grad_part), grad_w_qkv, grad_w_proj)


def second_product(active, buffer_shape, weight_out):
    active_all = gather_halves(active).reshape(buffer_shape[0], buffer_shape[1], -1)
    slot_out = jnp.einsum(
        "ecf,efd->ecd", active_all, weight_out, preferred_element_type=jnp.float32
    )
    return (active_all, slot_out.reshape(-1, slot_out.shape[2]))


def expert_forward(
    stream, gain_row, shift_row, choice_ids, slot_rows, weight_router, weight_in, weight_out
):
    normed, normal, inverse = norm_forward(stream, gain_row, shift_row)
    normed_all = gather_rows(normed.astype(jnp.bfloat16))
    row_count = normed_all.shape[0]
    expert_count = weight_in.shape[0]
    capacity = 2 * ((5 * row_count + 4 * expert_count - 1) // (4 * expert_count))
    logits = lax.psum(jnp.dot(normed_all, weight_router, preferred_element_type=jnp.float32), "col")
    router = softmax_rows(logits)
    onehot = (
        choice_ids[:, :, None] == lax.broadcasted_iota(jnp.int32, (1, 1, expert_count), 2)
    ).astype(jnp.float32)
    gate_values = jnp.sum(onehot * router[:, None, :], axis=2)
    flat_slots = choice_ids * capacity + slot_rows
    owners = jnp.broadcast_to(
        lax.broadcasted_iota(jnp.int32, (row_count, 1), 0), flat_slots.shape
    ).reshape(-1)
    slot_owner = (
        jnp.full((expert_count * capacity,), row_count, jnp.int32)
        .at[flat_slots.reshape(-1)]
        .set(owners)
    )
    slot_assign = (
        jnp.full((expert_count * capacity,), 2 * row_count, jnp.int32)
        .at[flat_slots.reshape(-1)]
        .set(lax.iota(jnp.int32, 2 * row_count))
    )
    padded = jnp.concatenate(
        [normed_all, jnp.zeros((1, normed_all.shape[1]), jnp.bfloat16)], axis=0
    )
    buffer = padded[slot_owner].reshape(expert_count, capacity, -1)
    hidden_part = jnp.einsum("ecd,edf->ecf", buffer, weight_in, preferred_element_type=jnp.float32)
    hidden = sum_halves(hidden_part.reshape(buffer.shape[0] * buffer.shape[1], -1))
    active = jax.nn.gelu(hidden).astype(jnp.bfloat16)
    active_all, slot_out = second_product(active, buffer.shape, weight_out)
    branch_part = jnp.sum(gate_values[:, :, None] * slot_out[flat_slots], axis=1)
    saved = {
        "normal": normal,
        "inverse": inverse,
        "normed_all": normed_all,
        "router": router,
        "onehot": onehot,
        "gate_values": gate_values,
        "flat_slots": flat_slots,
        "slot_owner": slot_owner,
        "slot_assign": slot_assign,
        "buffer": buffer,
        "hidden": hidden,
        "active": active,
    }
    saved["active_all"] = active_all
    saved["slot_out"] = slot_out
    return (stream + sum_rows(branch_part), saved)


def expert_backward(upstream, saved, weight_router, weight_in, weight_out):
    buffer = saved["buffer"]
    expert_count = weight_in.shape[0]
    capacity = saved["slot_owner"].shape[0] // expert_count
    active_all = saved["active_all"]
    slot_out = saved["slot_out"]
    flat_slots = saved["flat_slots"]
    grad_all = gather_rows(upstream.astype(jnp.bfloat16))
    gate_part = jnp.sum(grad_all.astype(jnp.float32)[:, None, :] * slot_out[flat_slots], axis=2)
    grad_gates = lax.psum(gate_part, ("row", "col"))
    padded_grad = jnp.concatenate(
        [grad_all, jnp.zeros((1, grad_all.shape[1]), jnp.bfloat16)], axis=0
    )
    slot_gate = jnp.concatenate([saved["gate_values"].reshape(-1), jnp.zeros((1,), jnp.float32)])[
        saved["slot_assign"]
    ]
    grad_slot = (
        (slot_gate[:, None] * padded_grad[saved["slot_owner"]])
        .astype(jnp.bfloat16)
        .reshape(expert_count, capacity, -1)
    )
    grad_active_part = jnp.einsum(
        "ecd,efd->ecf", grad_slot, weight_out, preferred_element_type=jnp.float32
    )
    grad_w_out = jnp.einsum(
        "ecf,ecd->efd", active_all, grad_slot, preferred_element_type=jnp.float32
    )
    grad_active = sum_halves(grad_active_part.reshape(buffer.shape[0] * buffer.shape[1], -1))
    gelu_pull = jax.vjp(jax.nn.gelu, saved["hidden"])[1]
    grad_hidden = gelu_pull(grad_active)[0].astype(jnp.bfloat16)
    grad_hidden_all = gather_halves(grad_hidden).reshape(buffer.shape[0], buffer.shape[1], -1)
    grad_buffer = jnp.einsum(
        "ecf,edf->ecd", grad_hidden_all, weight_in, preferred_element_type=jnp.float32
    )
    grad_w_in = jnp.einsum(
        "ecd,ecf->edf", buffer, grad_hidden_all, preferred_element_type=jnp.float32
    )
    grad_buffer = grad_buffer.reshape(expert_count * capacity, -1)
    router = saved["router"]
    grad_probs = jnp.sum(grad_gates[:, :, None] * saved["onehot"], axis=1)
    grad_logits = (
        router * (grad_probs - jnp.sum(router * grad_probs, axis=1, keepdims=True))
    ).astype(jnp.bfloat16)
    grad_w_router = jnp.einsum(
        "td,te->de", saved["normed_all"], grad_logits, preferred_element_type=jnp.float32
    )
    router_back = jnp.einsum(
        "te,de->td", grad_logits, weight_router, preferred_element_type=jnp.float32
    )
    leading = (lax.axis_index("row") == 0).astype(jnp.float32)
    grad_part = jnp.sum(grad_buffer[flat_slots], axis=1) + leading * router_back
    return (sum_rows(grad_part), grad_w_router, grad_w_in, grad_w_out)


def per_device(
    tokens,
    norm_gain,
    norm_shift,
    w_qkv,
    w_proj,
    w_router,
    w_in,
    w_out,
    expert_ids,
    slot_ids,
    cotangent,
):
    layer_count = w_qkv.shape[0]
    stream = tokens.astype(jnp.float32)
    attention_saved = []
    expert_saved = []
    for layer_index in range(layer_count):
        weight_qkv = w_qkv[layer_index].reshape(w_qkv.shape[1], -1)
        stream, kept_one = attention_forward(
            stream,
            norm_gain[layer_index, 0],
            norm_shift[layer_index, 0],
            weight_qkv,
            w_proj[layer_index],
        )
        stream, kept_two = expert_forward(
            stream,
            norm_gain[layer_index, 1],
            norm_shift[layer_index, 1],
            expert_ids[layer_index],
            slot_ids[layer_index],
            w_router[layer_index],
            w_in[layer_index],
            w_out[layer_index],
        )
        attention_saved.append(kept_one)
        expert_saved.append(kept_two)
    output = stream.astype(jnp.bfloat16)
    grad_stream = cotangent.astype(jnp.float32)
    qkv_grads = [None] * layer_count
    proj_grads = [None] * layer_count
    router_grads = [None] * layer_count
    in_grads = [None] * layer_count
    out_grads = [None] * layer_count
    gain_grads = [None] * layer_count
    shift_grads = [None] * layer_count
    for layer_index in reversed(range(layer_count)):
        weight_qkv = w_qkv[layer_index].reshape(w_qkv.shape[1], -1)
        kept_two = expert_saved[layer_index]
        grad_normed, router_grads[layer_index], grad_w_in, grad_w_out = expert_backward(
            grad_stream, kept_two, w_router[layer_index], w_in[layer_index], w_out[layer_index]
        )
        grad_w_in, grad_w_out = (
            lax.psum_scatter(grad_w_in, "dp", scatter_dimension=0, tiled=True),
            lax.psum_scatter(grad_w_out, "dp", scatter_dimension=0, tiled=True),
        )
        in_grads[layer_index] = grad_w_in
        out_grads[layer_index] = grad_w_out
        grad_inner, gain_two, shift_two = norm_backward(
            grad_normed, kept_two["normal"], kept_two["inverse"], norm_gain[layer_index, 1]
        )
        grad_stream = grad_stream + grad_inner
        kept_one = attention_saved[layer_index]
        grad_normed, grad_w_qkv, proj_grads[layer_index] = attention_backward(
            grad_stream, kept_one, weight_qkv, w_proj[layer_index]
        )
        qkv_grads[layer_index] = grad_w_qkv.reshape(w_qkv.shape[1:])
        grad_inner, gain_one, shift_one = norm_backward(
            grad_normed, kept_one["normal"], kept_one["inverse"], norm_gain[layer_index, 0]
        )
        grad_stream = grad_stream + grad_inner
        gain_grads[layer_index] = jnp.stack([gain_one, gain_two])
        shift_grads[layer_index] = jnp.stack([shift_one, shift_two])
    grad_qkv, grad_proj, grad_router = lax.psum(
        (jnp.stack(qkv_grads), jnp.stack(proj_grads), jnp.stack(router_grads)), "dp"
    )
    grad_gain, grad_shift = lax.psum((jnp.stack(gain_grads), jnp.stack(shift_grads)), ("dp", "row"))
    grad_in = jnp.stack(in_grads)
    grad_out = jnp.stack(out_grads)
    return (
        output,
        grad_stream,
        grad_qkv,
        grad_proj,
        grad_router,
        grad_in,
        grad_out,
        grad_gain,
        grad_shift,
    )


def exchange(values, axis, offset):
    count = lax.axis_size(axis)
    return lax.ppermute(values, axis, [(place, place ^ offset) for place in range(count)])


def contract(left, right, left_dim, right_dim):
    return lax.dot_general(
        left, right, (((left_dim,), (right_dim,)), ((), ())), preferred_element_type=jnp.float32
    )


def layer_norm_parts(values):
    center = jnp.mean(values, axis=1, keepdims=True)
    shifted = values - center
    spread = jnp.mean(shifted * shifted, axis=1, keepdims=True)
    inverse = lax.rsqrt(spread + EPSILON)
    return (shifted * inverse, inverse)


def layer_norm_pull(upstream, normal, inverse, gain_row):
    scaled = upstream * gain_row
    first = jnp.mean(scaled, axis=1, keepdims=True)
    second = jnp.mean(scaled * normal, axis=1, keepdims=True)
    return inverse * (scaled - first - normal * second)


def gelu_parts(values):
    factor = (2.0 / jnp.pi) ** 0.5
    squares = values * values
    curve = jnp.tanh(values * (factor + (factor * 0.044715) * squares))
    half = 0.5 + 0.5 * curve
    slope = half + (0.5 * values) * (1.0 - curve * curve) * (
        factor + (3.0 * factor * 0.044715) * squares
    )
    return (values * half, slope)


def head_probs(query_head, key_pair, valid):
    scores = contract(query_head, key_pair, 1, 1) * HDIM ** (-0.5)
    scores = jnp.where(valid, scores, -1e30)
    powers = jnp.exp(scores - jnp.max(scores, axis=1, keepdims=True))
    return powers / jnp.sum(powers, axis=1, keepdims=True)


def assemble_weights(place_ref, block_refs, full_ref, rows, features):
    half = features // 2
    strip = features // rows
    for position, block_ref in enumerate(block_refs):
        other, offset = divmod(position, rows)
        side = lax.bitwise_xor(place_ref[2], other)
        top = pl.multiple_of(side * half, half)
        for part in range(3):
            full_ref[pl.ds(top, half), pl.ds(part * features + offset * strip, strip)] = block_ref[
                :, pl.ds(part * strip, strip)
            ]
        for piece in range(half // strip):
            left = pl.multiple_of(3 * features + side * half + piece * strip, strip)
            full_ref[pl.ds(offset * strip, strip), pl.ds(left, strip)] = block_ref[
                pl.ds(piece * strip, strip), pl.ds(3 * strip, strip)
            ]


def attention_forward_kernel(rows, place_ref, *refs):
    block_refs = refs[: 2 * rows]
    norm_ref, stream_ref = refs[2 * rows : 2 * rows + 2]
    part_refs = refs[2 * rows + 2 : -6]
    start_ref, middle_ref, first_ref, packed_ref, mixed_ref, second_ref, full_ref = refs[-7:]
    part_refs = refs[2 * rows + 2 : -7]
    features = stream_ref.shape[1]
    padded = stream_ref.shape[0]
    assemble_weights(place_ref, block_refs, full_ref, rows, features)
    stream = stream_ref[...].astype(jnp.float32)
    for part_ref in part_refs:
        stream = stream + part_ref[...].astype(jnp.float32)
    start_ref[...] = stream
    normal, _ = layer_norm_parts(stream)
    normed = (normal * norm_ref[0:1] + norm_ref[2:3]).astype(jnp.bfloat16)
    first_ref[...] = normed
    for part in range(3):
        columns = pl.ds(part * features, features)
        packed_ref[:, columns] = contract(normed, full_ref[:, columns], 1, 0).astype(jnp.bfloat16)
    valid = lax.broadcasted_iota(jnp.int32, (padded, padded), 1) < SEQ
    lower = lax.broadcasted_iota(jnp.int32, (padded, 2 * HDIM), 1) < HDIM
    for pair in range(features // (2 * HDIM)):
        query = packed_ref[:, pl.ds(pair * 2 * HDIM, 2 * HDIM)]
        keys = packed_ref[:, pl.ds(features + pair * 2 * HDIM, 2 * HDIM)]
        values = packed_ref[:, pl.ds(2 * features + pair * 2 * HDIM, 2 * HDIM)]
        blank = jnp.zeros_like(query)
        results = []
        for query_head in (jnp.where(lower, query, blank), jnp.where(lower, blank, query)):
            probs = head_probs(query_head, keys, valid).astype(jnp.bfloat16)
            results.append(contract(probs, values, 1, 0))
        mixed_ref[:, pl.ds(pair * 2 * HDIM, 2 * HDIM)] = jnp.where(
            lower, results[0], results[1]
        ).astype(jnp.bfloat16)
    stream = stream + contract(mixed_ref[...], full_ref[:, pl.ds(3 * features, features)], 1, 0)
    middle_ref[...] = stream
    normal, _ = layer_norm_parts(stream)
    second_ref[...] = (normal * norm_ref[1:2] + norm_ref[3:4]).astype(jnp.bfloat16)


def attention_backward_kernel(rows, place_ref, *refs):
    (
        full_ref,
        norm_ref,
        start_ref,
        middle_ref,
        first_ref,
        packed_ref,
        mixed_ref,
        grad_ref,
        router_ref,
    ) = refs[:9]
    part_refs = refs[9:-5]
    result_ref, branch_ref, blocks_ref, gpacked_ref, gmixed_ref = refs[-5:]
    features = start_ref.shape[1]
    padded = start_ref.shape[0]
    upstream = part_refs[0][...].astype(jnp.float32)
    for part_ref in part_refs[1:]:
        upstream = upstream + part_ref[...].astype(jnp.float32)
    normal, inverse = layer_norm_parts(middle_ref[...])
    gain_two = jnp.sum(upstream * normal, axis=0, keepdims=True)
    shift_two = jnp.sum(upstream, axis=0, keepdims=True)
    grad_middle = grad_ref[...].astype(jnp.float32) + layer_norm_pull(
        upstream, normal, inverse, norm_ref[1:2]
    )
    grad_attn = grad_middle.astype(jnp.bfloat16)
    gmixed_ref[...] = contract(
        grad_attn, full_ref[:, pl.ds(3 * features, features)], 1, 1
    ).astype(jnp.bfloat16)
    valid = lax.broadcasted_iota(jnp.int32, (padded, padded), 1) < SEQ
    lower = lax.broadcasted_iota(jnp.int32, (padded, 2 * HDIM), 1) < HDIM
    scale = HDIM ** (-0.5)
    for pair in range(features // (2 * HDIM)):
        spans = [pl.ds(part * features + pair * 2 * HDIM, 2 * HDIM) for part in range(3)]
        query, keys, values = [packed_ref[:, span] for span in spans]
        gmixed = gmixed_ref[:, spans[0]]
        blank = jnp.zeros_like(query)
        found = []
        for side in range(2):
            keep = lower if side == 0 else jnp.logical_not(lower)
            probs = head_probs(jnp.where(keep, query, blank), keys, valid)
            grad_probs = contract(jnp.where(keep, gmixed, blank), values, 1, 1)
            grad_values = contract(probs.astype(jnp.bfloat16), gmixed, 0, 0)
            grad_scores = (
                probs * (grad_probs - jnp.sum(probs * grad_probs, axis=1, keepdims=True))
            ).astype(jnp.bfloat16)
            grad_query = contract(grad_scores, keys, 1, 0) * scale
            grad_keys = contract(grad_scores, query, 0, 0) * scale
            found.append((grad_query, grad_keys, grad_values))
        for part in range(3):
            gpacked_ref[:, spans[part]] = jnp.where(lower, found[0][part], found[1][part]).astype(
                jnp.bfloat16
            )
    upstream = contract(gpacked_ref[...], full_ref[:, pl.ds(0, 3 * features)], 1, 1)
    normal, inverse = layer_norm_parts(start_ref[...])
    gain_one = jnp.sum(upstream * normal, axis=0, keepdims=True)
    shift_one = jnp.sum(upstream, axis=0, keepdims=True)
    result = grad_middle + layer_norm_pull(upstream, normal, inverse, norm_ref[0:1])
    result_ref[...] = result
    branch_ref[...] = result.astype(jnp.bfloat16)
    half = features // 2
    strip = features // rows
    extra = jnp.concatenate(
        [
            router_ref[...],
            gain_one,
            gain_two,
            shift_one,
            shift_two,
            jnp.zeros((blocks_ref.shape[1] - 4 * strip - router_ref.shape[0] - 4, features), jnp.float32),
        ],
        axis=0,
    ).astype(jnp.bfloat16)
    grad_proj = contract(mixed_ref[...], grad_attn, 0, 0).astype(jnp.bfloat16)
    for offset in range(rows):
        spot = lax.bitwise_xor(place_ref[1], offset) * 2
        for side in range(2):
            columns = slice(side * half, (side + 1) * half)
            blocks_ref[spot + side, pl.ds(3 * strip, strip), :] = grad_proj[
                offset * strip : (offset + 1) * strip, columns
            ]
            blocks_ref[spot + side, pl.ds(4 * strip, extra.shape[0]), :] = extra[:, columns]
    for part in range(3):
        grad_part = contract(
            gpacked_ref[:, pl.ds(part * features, features)], first_ref[...], 0, 0
        ).astype(jnp.bfloat16)
        for offset in range(rows):
            spot = lax.bitwise_xor(place_ref[1], offset) * 2
            for side in range(2):
                blocks_ref[spot + side, pl.ds(part * strip, strip), :] = grad_part[
                    offset * strip : (offset + 1) * strip, side * half : (side + 1) * half
                ]


def dispatch_kernel(room, codes_ref, *refs):
    groups = codes_ref.shape[1]
    block_refs, out_refs = refs[:-groups], refs[-groups:]
    padded = block_refs[0].shape[0]
    rows_of = lax.broadcasted_iota(jnp.int32, (room, padded), 0)
    for group in range(groups):
        total = jnp.zeros((room, block_refs[0].shape[1]), jnp.float32)
        for image, block_ref in enumerate(block_refs):
            picks = (codes_ref[image, group : group + 1, :] == rows_of).astype(jnp.float32)
            total = total + contract(picks.astype(jnp.bfloat16), block_ref[...], 1, 0)
        out_refs[group][...] = total.astype(jnp.bfloat16)


def combine_kernel(rows, codes_ref, *refs):
    slot_refs, out_refs = refs[: codes_ref.shape[1]], refs[codes_ref.shape[1] :]
    room = slot_refs[0].shape[0]
    padded = out_refs[0].shape[0]
    lanes = lax.broadcasted_iota(jnp.int32, (padded, room), 1)
    for image in range(rows):
        total = jnp.zeros(out_refs[0].shape, jnp.float32)
        for source, slot_ref in enumerate(slot_refs):
            codes = codes_ref[pl.ds(image * padded, padded), source : source + 1]
            picks = (codes == lanes).astype(jnp.float32)
            total = total + contract(picks.astype(jnp.bfloat16), slot_ref[...], 1, 0)
        out_refs[image][...] = total.astype(jnp.bfloat16)


def expert_router(place_ref, buffer, wrouter):
    router = softmax_rows(contract(buffer, wrouter, 1, 1))
    chosen = lax.broadcasted_iota(jnp.int32, router.shape, 1) == place_ref[3]
    gate = jnp.sum(jnp.where(chosen, router, 0.0), axis=1, keepdims=True)
    return (router, chosen, gate)


def expert_forward_kernel(groups, place_ref, wrouter_ref, win_ref, wout_ref, *refs):
    buffer = jnp.concatenate([ref[...] for ref in refs[:groups]], axis=0)
    room = refs[0].shape[0]
    half = buffer.shape[1] // 2
    _, _, gate = expert_router(place_ref, buffer, wrouter_ref[...])
    sums = [jnp.zeros((buffer.shape[0], half), jnp.float32) for _ in range(2)]
    for quarter in range(win_ref.shape[0] // 2):
        hidden = contract(buffer[:, :half], win_ref[2 * quarter], 1, 0) + contract(
            buffer[:, half:], win_ref[2 * quarter + 1], 1, 0
        )
        active = gelu_parts(hidden)[0].astype(jnp.bfloat16)
        for side in range(2):
            sums[side] = sums[side] + contract(active, wout_ref[2 * quarter + side], 1, 0)
    for group in range(groups):
        span = slice(group * room, (group + 1) * room)
        for side in range(2):
            refs[groups + group][:, pl.ds(side * half, half)] = (
                gate[span] * sums[side][span]
            ).astype(jnp.bfloat16)


def expert_full_kernel(groups, with_output, place_ref, wrouter_ref, win_ref, wout_ref, *refs):
    buffer = jnp.concatenate([ref[...] for ref in refs[:groups]], axis=0)
    grads = jnp.concatenate([ref[...] for ref in refs[groups : 2 * groups]], axis=0)
    back_refs = refs[2 * groups : 3 * groups]
    out_refs = refs[3 * groups : -3]
    gin_ref, gout_ref, grouter_ref = refs[-3:]
    room = refs[0].shape[0]
    half = buffer.shape[1] // 2
    router, chosen, gate = expert_router(place_ref, buffer, wrouter_ref[...])
    grad_slot = (gate * grads.astype(jnp.float32)).astype(jnp.bfloat16)
    flipped = buffer.T
    sums = [jnp.zeros((buffer.shape[0], half), jnp.float32) for _ in range(2)]
    backs = [jnp.zeros((buffer.shape[0], half), jnp.float32) for _ in range(2)]
    grad_gate = jnp.zeros((buffer.shape[0], 1), jnp.float32)
    for quarter in range(win_ref.shape[0] // 2):
        hidden = contract(buffer[:, :half], win_ref[2 * quarter], 1, 0) + contract(
            buffer[:, half:], win_ref[2 * quarter + 1], 1, 0
        )
        value, slope = gelu_parts(hidden)
        active = value.astype(jnp.bfloat16)
        if with_output:
            for side in range(2):
                sums[side] = sums[side] + contract(active, wout_ref[2 * quarter + side], 1, 0)
        pulled = contract(grads[:, :half], wout_ref[2 * quarter], 1, 1) + contract(
            grads[:, half:], wout_ref[2 * quarter + 1], 1, 1
        )
        grad_gate = grad_gate + jnp.sum(
            pulled * active.astype(jnp.float32), axis=1, keepdims=True
        )
        grad_hidden = (gate * pulled * slope).astype(jnp.bfloat16)
        turned = active.T
        for side in range(2):
            block = 2 * quarter + side
            span = slice(side * half, (side + 1) * half)
            backs[side] = backs[side] + contract(grad_hidden, win_ref[block], 1, 1)
            gin_ref[block] = contract(flipped[span], grad_hidden, 1, 0).astype(jnp.bfloat16)
            gout_ref[block] = contract(turned, grad_slot[:, span], 1, 0).astype(jnp.bfloat16)
    grad_logits = (
        router * (jnp.where(chosen, grad_gate, 0.0) - gate * grad_gate)
    ).astype(jnp.bfloat16)
    grouter_ref[...] = contract(grad_logits, buffer, 0, 0)
    router_back = contract(grad_logits, wrouter_ref[...], 1, 0)
    for group in range(groups):
        span = slice(group * room, (group + 1) * room)
        for side in range(2):
            columns = slice(side * half, (side + 1) * half)
            back_refs[group][:, columns] = (
                backs[side][span] + router_back[span, columns]
            ).astype(jnp.bfloat16)
            if with_output:
                out_refs[group][:, columns] = (gate[span] * sums[side][span]).astype(jnp.bfloat16)


SMALL = pl.BlockSpec(memory_space=pltpu.SMEM)
LOCAL = pl.BlockSpec(memory_space=pltpu.VMEM)


def run_kernel(body, place, operands, results, scratch=()):
    specs = [LOCAL] * len(operands)
    arguments = list(operands)
    if place is not None:
        specs = [SMALL] + specs
        arguments = [place] + arguments
    return pl.pallas_call(
        body,
        in_specs=specs,
        out_specs=[LOCAL] * len(results),
        out_shape=[jax.ShapeDtypeStruct(shape, kind) for shape, kind in results],
        scratch_shapes=list(scratch),
        compiler_params=pltpu.CompilerParams(vmem_limit_bytes=48 * 1024 * 1024),
    )(*arguments)


def gather_group(values):
    near = [values]
    for offset in range(1, lax.axis_size("row")):
        near.append(exchange(values, "row", offset))
    return near + [exchange(piece, "col", 1) for piece in near]


def scatter_pieces(pieces, axis):
    return [
        piece if offset == 0 else exchange(piece, axis, offset)
        for offset, piece in enumerate(pieces)
    ]


def group_device(
    tokens,
    norm_gain,
    norm_shift,
    w_qkv,
    w_proj,
    w_router,
    w_in,
    w_out,
    expert_ids,
    slot_ids,
    cotangent,
):
    low = jnp.bfloat16
    groups, rows = lax.axis_size("dp"), lax.axis_size("row")
    members = 2 * rows
    at_dp, at_row, at_col = [lax.axis_index(name) for name in ("dp", "row", "col")]
    layer_count = w_qkv.shape[0]
    expert_count = w_in.shape[1]
    half = tokens.shape[1]
    features = 2 * half
    strip = features // rows
    padded = -(-SEQ // 16) * 16
    owner = at_dp * members + at_row * 2 + at_col
    place = jnp.stack([at_dp, at_row, at_col, owner]).astype(jnp.int32)

    def join(mine, other):
        return jnp.where(
            at_col == 0,
            jnp.concatenate([mine, other], axis=-1),
            jnp.concatenate([other, mine], axis=-1),
        )

    small = jnp.concatenate(
        [
            jnp.concatenate([norm_gain, norm_shift], axis=1).reshape(-1, half),
            w_router.transpose(0, 2, 1).reshape(-1, half).astype(jnp.float32),
        ],
        axis=0,
    )
    small = join(small, exchange(small, "col", 1))
    norms = small[: 4 * layer_count].reshape(layer_count, 4, features)
    routers = small[4 * layer_count :].reshape(layer_count, expert_count, features).astype(low)
    both = jnp.stack([tokens, cotangent]).reshape(2, 2, SEQ, half)
    mine = lax.dynamic_index_in_dim(both, at_col, 1, keepdims=False)
    other = exchange(lax.dynamic_index_in_dim(both, 1 - at_col, 1, keepdims=False), "col", 1)
    both = jnp.pad(join(mine, other), ((0, 0), (0, padded - SEQ), (0, 0)))

    attention_blocks = []
    for layer in range(layer_count):
        block = jnp.concatenate(
            [
                w_qkv[layer].reshape(half, -1),
                jnp.concatenate(
                    [
                        w_proj[layer][:, piece * strip : (piece + 1) * strip]
                        for piece in range(half // strip)
                    ],
                    axis=0,
                ),
            ],
            axis=1,
        )
        attention_blocks.append(gather_group(block))

    weights_in, weights_out = [], []
    for layer in range(layer_count):
        for store, source in ((weights_in, w_in), (weights_out, w_out)):
            local = lax.dynamic_slice_in_dim(source[layer], at_dp * members, members, 0)
            store.append(
                lax.all_to_all(local, ("row", "col"), split_axis=0, concat_axis=0, tiled=True)
            )

    capacity = 2 * ((5 * members * SEQ + 4 * expert_count - 1) // (4 * expert_count))
    room = -(-capacity // 16) * 16
    images = jnp.stack(
        [(at_row ^ offset) * 2 + (at_col ^ side) for side in range(2) for offset in range(rows)]
    )
    named = jnp.stack(
        [
            (at_dp ^ offset) * members + at_row * 2 + (at_col ^ side)
            for side in range(2)
            for offset in range(groups)
        ]
    )
    chosen = jnp.take(expert_ids.reshape(layer_count, members, SEQ, -1), images, axis=1)
    slots = jnp.take(slot_ids.reshape(layer_count, members, SEQ, -1), images, axis=1)
    codes = jnp.max(
        jnp.where(chosen[..., None] == named, slots[..., None], -1), axis=3
    )
    codes = jnp.pad(codes, ((0, 0), (0, 0), (0, padded - SEQ), (0, 0)), constant_values=-1)
    send_codes = codes[..., :groups].transpose(0, 1, 3, 2)
    back_codes = codes[:, :rows].reshape(layer_count, rows * padded, 2 * groups)

    token_block = ((padded, features), low)
    slot_block = ((room, features), low)

    def send_out(layer, values):
        blocks = run_kernel(
            functools.partial(dispatch_kernel, room),
            None,
            [send_codes[layer]] + gather_group(values),
            [slot_block] * groups,
        )
        return scatter_pieces(blocks, "dp")

    def bring_back(layer, blocks):
        blocks = scatter_pieces(blocks, "dp")
        blocks = blocks + [exchange(piece, "col", 1) for piece in blocks]
        pieces = run_kernel(
            functools.partial(combine_kernel, rows),
            None,
            [back_codes[layer]] + blocks,
            [token_block] * rows,
        )
        return scatter_pieces(pieces, "row")

    stream, parts = both[0], []
    kept, buffers = [], []
    branches = send_out(layer_count - 1, both[1])
    grad_parts = None
    for layer in range(layer_count):
        saved = run_kernel(
            functools.partial(attention_forward_kernel, rows),
            place,
            attention_blocks[layer] + [norms[layer], stream] + parts,
            [
                ((padded, features), jnp.float32),
                ((padded, features), jnp.float32),
                token_block,
                ((padded, 3 * features), low),
                token_block,
                token_block,
                ((features, 4 * features), low),
            ],
        )
        kept.append(saved)
        buffer = send_out(layer, saved[5])
        buffers.append(buffer)
        stream = saved[1]
        if layer < layer_count - 1:
            result = run_kernel(
                functools.partial(expert_forward_kernel, groups),
                place,
                [routers[layer], weights_in[layer], weights_out[layer]] + buffer,
                [slot_block] * groups,
            )
            parts = bring_back(layer, result)
    grad = both[1]
    results = {}
    for layer in reversed(range(layer_count)):
        last = layer == layer_count - 1
        found = run_kernel(
            functools.partial(expert_full_kernel, groups, last),
            place,
            [routers[layer], weights_in[layer], weights_out[layer]] + buffers[layer] + branches,
            [slot_block] * (2 * groups if last else groups)
            + [
                ((members, half, w_in.shape[3]), low),
                ((members, w_out.shape[2], half), low),
                ((expert_count, features), jnp.float32),
            ],
        )
        grad_parts = bring_back(layer, list(found[:groups]))
        if last:
            parts = bring_back(layer, list(found[groups : 2 * groups]))
        grad_in, grad_out = [
            lax.all_to_all(piece, ("row", "col"), split_axis=0, concat_axis=0, tiled=True)
            for piece in found[-3:-1]
        ]
        saved = kept[layer]
        height = -(-(4 * strip + expert_count + 4) // 16) * 16
        grad, branch, blocks = run_kernel(
            functools.partial(attention_backward_kernel, rows),
            place,
            [saved[6], norms[layer], saved[0], saved[1], saved[2], saved[3], saved[4], grad]
            + [found[-1]]
            + grad_parts,
            [
                ((padded, features), jnp.float32),
                token_block,
                ((members, height, half), low),
            ],
            [pltpu.VMEM((padded, 3 * features), low), pltpu.VMEM((padded, features), low)],
        )
        blocks = lax.all_to_all(blocks, ("row", "col"), split_axis=0, concat_axis=0, tiled=True)
        shared = lax.psum(jnp.sum(blocks.astype(jnp.float32), axis=0), "dp")
        results[layer] = (grad_in, grad_out, shared)
        if layer > 0:
            branches = send_out(layer - 1, branch)
    for part in parts:
        stream = stream + part.astype(jnp.float32)

    def split(values):
        pieces = values[:SEQ].reshape(SEQ, 2, half)
        mine = lax.dynamic_index_in_dim(pieces, at_col, 1, keepdims=False)
        other = exchange(lax.dynamic_index_in_dim(pieces, 1 - at_col, 1, keepdims=False), "col", 1)
        return jnp.where(
            at_col == 0,
            jnp.concatenate([mine, other], axis=0),
            jnp.concatenate([other, mine], axis=0),
        )

    output = split(stream.astype(low))
    grad_input = split(grad)
    ordered = [results[layer] for layer in range(layer_count)]
    grad_in = jnp.stack([found[0] for found in ordered]).astype(jnp.float32)
    grad_out = jnp.stack([found[1] for found in ordered]).astype(jnp.float32)
    shared = jnp.stack([found[2] for found in ordered])
    grad_qkv = (
        shared[:, : 3 * strip].reshape(layer_count, 3, strip, half).transpose(0, 3, 1, 2)
    )
    grad_proj = shared[:, 3 * strip : 4 * strip]
    grad_router = shared[:, 4 * strip : 4 * strip + expert_count].transpose(0, 2, 1)
    tail = shared[:, 4 * strip + expert_count : 4 * strip + expert_count + 4]
    return (
        output,
        grad_input,
        grad_qkv,
        grad_proj,
        grad_router,
        grad_in,
        grad_out,
        tail[:, :2],
        tail[:, 2:],
    )


def fits_groups(mesh, tokens, w_in):
    groups, rows, sides = mesh.shape["dp"], mesh.shape["row"], mesh.shape["col"]
    powers = all(size & (size - 1) == 0 for size in (groups, rows))
    return (
        sides == 2
        and powers
        and tokens.shape[0] == groups * rows * sides * SEQ
        and w_in.shape[1] == groups * rows * sides
    )


def solution(mesh):
    in_specs = (
        P(("dp", "row"), "col"),
        P(None, None, "col"),
        P(None, None, "col"),
        P(None, "col", None, "row"),
        P(None, "row", "col"),
        P(None, "col", None),
        P(None, None, "col", "row"),
        P(None, None, "row", "col"),
        P(None, "dp", None),
        P(None, "dp", None),
        P(("dp", "row"), "col"),
    )
    out_specs = (
        P(("dp", "row"), "col"),
        P(("dp", "row"), "col"),
        P(None, "col", None, "row"),
        P(None, "row", "col"),
        P(None, "col", None),
        P(None, "dp", "col", "row"),
        P(None, "dp", "row", "col"),
        P(None, None, "col"),
        P(None, None, "col"),
    )

    def program(*arguments):
        fits = fits_groups(mesh, arguments[0], arguments[6])
        return jax.shard_map(
            group_device if fits else per_device,
            mesh=mesh,
            in_specs=in_specs,
            out_specs=out_specs,
            check_vma=False,
        )(*arguments)

    return program
```

```python
import functools

import jax
import jax.numpy as jnp
from jax import lax
from jax.experimental import pallas as pl
from jax.experimental.pallas import tpu as pltpu
from jax.sharding import PartitionSpec as P

HDIM = 64
SEQ = 197


EPSILON = 1e-06


def gather_rows(values):
    return lax.all_gather(values, "row", axis=0, tiled=True)


def sum_rows(values):
    return lax.psum_scatter(values, "row", scatter_dimension=0, tiled=True)


def gather_halves(values):
    return lax.all_gather(values, "col", axis=0, tiled=True)


def sum_halves(values):
    return lax.psum_scatter(values, "col", scatter_dimension=0, tiled=True)


def row_totals(first, second):
    return lax.psum((first, second), "col")


def softmax_rows(values):
    shifted = jnp.exp(values - jnp.max(values, axis=-1, keepdims=True))
    return shifted / jnp.sum(shifted, axis=-1, keepdims=True)


def norm_forward(stream, gain_row, shift_row):
    feature_count = stream.shape[1] * lax.axis_size("col")
    total, squares = row_totals(jnp.sum(stream, axis=1), jnp.sum(stream * stream, axis=1))
    center = total / feature_count
    inverse = lax.rsqrt(squares / feature_count - center * center + EPSILON)
    normal = (stream - center[:, None]) * inverse[:, None]
    return (normal * gain_row + shift_row, normal, inverse)


def norm_backward(upstream, normal, inverse, gain_row):
    feature_count = upstream.shape[1] * lax.axis_size("col")
    scaled = upstream * gain_row
    first, second = row_totals(jnp.sum(scaled, axis=1), jnp.sum(scaled * normal, axis=1))
    result_grad = inverse[:, None] * (
        scaled - first[:, None] / feature_count - normal * (second[:, None] / feature_count)
    )
    return (result_grad, jnp.sum(upstream * normal, axis=0), jnp.sum(upstream, axis=0))


def split_heads(packed):
    row_count = packed.shape[0]
    heads_here = packed.shape[1] // (3 * HDIM)
    parts = packed.reshape(row_count // SEQ, SEQ, 3, heads_here, HDIM)
    return (parts[:, :, 0], parts[:, :, 1], parts[:, :, 2])


def attend_forward(packed):
    query_part, key_part, value_part = split_heads(packed)
    scores = jnp.einsum(
        "bqhd,bkhd->bhqk", query_part, key_part, preferred_element_type=jnp.float32
    ) * HDIM ** (-0.5)
    highest = jnp.max(scores, axis=-1, keepdims=True)
    powers = jnp.exp(scores - highest)
    totals = jnp.sum(powers, axis=-1, keepdims=True)
    weights = (powers / totals).astype(jnp.bfloat16)
    mixed_heads = jnp.einsum(
        "bhqk,bkhd->bqhd", weights, value_part, preferred_element_type=jnp.float32
    )
    return (
        mixed_heads.reshape(packed.shape[0], -1).astype(jnp.bfloat16),
        highest + jnp.log(totals),
    )


def attend_backward(packed, logsum, grad_mixed):
    query_part, key_part, value_part = split_heads(packed)
    scale = HDIM ** (-0.5)
    scores = (
        jnp.einsum("bqhd,bkhd->bhqk", query_part, key_part, preferred_element_type=jnp.float32)
        * scale
    )
    probs_full = jnp.exp(scores - logsum)
    upstream = grad_mixed.reshape(query_part.shape)
    grad_probs = jnp.einsum(
        "bqhd,bkhd->bhqk", upstream, value_part, preferred_element_type=jnp.float32
    )
    grad_values = jnp.einsum(
        "bhqk,bqhd->bkhd",
        probs_full.astype(jnp.bfloat16),
        upstream,
        preferred_element_type=jnp.float32,
    )
    grad_scores = (
        probs_full * (grad_probs - jnp.sum(probs_full * grad_probs, axis=-1, keepdims=True))
    ).astype(jnp.bfloat16)
    grad_query = (
        jnp.einsum("bhqk,bkhd->bqhd", grad_scores, key_part, preferred_element_type=jnp.float32)
        * scale
    )
    grad_keys = (
        jnp.einsum("bhqk,bqhd->bkhd", grad_scores, query_part, preferred_element_type=jnp.float32)
        * scale
    )
    stacked = jnp.stack([grad_query, grad_keys, grad_values], axis=2)
    return stacked.reshape(packed.shape[0], -1).astype(jnp.bfloat16)


def attention_forward(stream, gain_row, shift_row, weight_qkv, weight_proj):
    normed, normal, inverse = norm_forward(stream, gain_row, shift_row)
    normed_all = gather_rows(normed.astype(jnp.bfloat16))
    packed = sum_halves(jnp.dot(normed_all, weight_qkv, preferred_element_type=jnp.float32)).astype(
        jnp.bfloat16
    )
    mixed_heads, logsum = attend_forward(packed)
    mixed_all = gather_halves(mixed_heads)
    branch = sum_rows(jnp.dot(mixed_all, weight_proj, preferred_element_type=jnp.float32))
    saved = {
        "normal": normal,
        "inverse": inverse,
        "normed_all": normed_all,
        "packed": packed,
        "logsum": logsum,
        "mixed_all": mixed_all,
    }
    return (stream + branch, saved)


def attention_backward(upstream, saved, weight_qkv, weight_proj):
    grad_all = gather_rows(upstream.astype(jnp.bfloat16))
    grad_mixed = sum_halves(
        jnp.einsum("te,de->td", grad_all, weight_proj, preferred_element_type=jnp.float32)
    ).astype(jnp.bfloat16)
    grad_w_proj = jnp.einsum(
        "td,te->de", saved["mixed_all"], grad_all, preferred_element_type=jnp.float32
    )
    grad_packed = attend_backward(saved["packed"], saved["logsum"], grad_mixed)
    grad_packed_all = gather_halves(grad_packed)
    grad_part = jnp.einsum(
        "tf,df->td", grad_packed_all, weight_qkv, preferred_element_type=jnp.float32
    )
    grad_w_qkv = jnp.einsum(
        "td,tf->df", saved["normed_all"], grad_packed_all, preferred_element_type=jnp.float32
    )
    return (sum_rows(grad_part), grad_w_qkv, grad_w_proj)


def second_product(active, buffer_shape, weight_out):
    active_all = gather_halves(active).reshape(buffer_shape[0], buffer_shape[1], -1)
    slot_out = jnp.einsum(
        "ecf,efd->ecd", active_all, weight_out, preferred_element_type=jnp.float32
    )
    return (active_all, slot_out.reshape(-1, slot_out.shape[2]))


def expert_forward(
    stream, gain_row, shift_row, choice_ids, slot_rows, weight_router, weight_in, weight_out
):
    normed, normal, inverse = norm_forward(stream, gain_row, shift_row)
    normed_all = gather_rows(normed.astype(jnp.bfloat16))
    row_count = normed_all.shape[0]
    expert_count = weight_in.shape[0]
    capacity = 2 * ((5 * row_count + 4 * expert_count - 1) // (4 * expert_count))
    logits = lax.psum(jnp.dot(normed_all, weight_router, preferred_element_type=jnp.float32), "col")
    router = softmax_rows(logits)
    onehot = (
        choice_ids[:, :, None] == lax.broadcasted_iota(jnp.int32, (1, 1, expert_count), 2)
    ).astype(jnp.float32)
    gate_values = jnp.sum(onehot * router[:, None, :], axis=2)
    flat_slots = choice_ids * capacity + slot_rows
    owners = jnp.broadcast_to(
        lax.broadcasted_iota(jnp.int32, (row_count, 1), 0), flat_slots.shape
    ).reshape(-1)
    slot_owner = (
        jnp.full((expert_count * capacity,), row_count, jnp.int32)
        .at[flat_slots.reshape(-1)]
        .set(owners)
    )
    slot_assign = (
        jnp.full((expert_count * capacity,), 2 * row_count, jnp.int32)
        .at[flat_slots.reshape(-1)]
        .set(lax.iota(jnp.int32, 2 * row_count))
    )
    padded = jnp.concatenate(
        [normed_all, jnp.zeros((1, normed_all.shape[1]), jnp.bfloat16)], axis=0
    )
    buffer = padded[slot_owner].reshape(expert_count, capacity, -1)
    hidden_part = jnp.einsum("ecd,edf->ecf", buffer, weight_in, preferred_element_type=jnp.float32)
    hidden = sum_halves(hidden_part.reshape(buffer.shape[0] * buffer.shape[1], -1))
    active = jax.nn.gelu(hidden).astype(jnp.bfloat16)
    active_all, slot_out = second_product(active, buffer.shape, weight_out)
    branch_part = jnp.sum(gate_values[:, :, None] * slot_out[flat_slots], axis=1)
    saved = {
        "normal": normal,
        "inverse": inverse,
        "normed_all": normed_all,
        "router": router,
        "onehot": onehot,
        "gate_values": gate_values,
        "flat_slots": flat_slots,
        "slot_owner": slot_owner,
        "slot_assign": slot_assign,
        "buffer": buffer,
        "hidden": hidden,
        "active": active,
    }
    saved["active_all"] = active_all
    saved["slot_out"] = slot_out
    return (stream + sum_rows(branch_part), saved)


def expert_backward(upstream, saved, weight_router, weight_in, weight_out):
    buffer = saved["buffer"]
    expert_count = weight_in.shape[0]
    capacity = saved["slot_owner"].shape[0] // expert_count
    active_all = saved["active_all"]
    slot_out = saved["slot_out"]
    flat_slots = saved["flat_slots"]
    grad_all = gather_rows(upstream.astype(jnp.bfloat16))
    gate_part = jnp.sum(grad_all.astype(jnp.float32)[:, None, :] * slot_out[flat_slots], axis=2)
    grad_gates = lax.psum(gate_part, ("row", "col"))
    padded_grad = jnp.concatenate(
        [grad_all, jnp.zeros((1, grad_all.shape[1]), jnp.bfloat16)], axis=0
    )
    slot_gate = jnp.concatenate([saved["gate_values"].reshape(-1), jnp.zeros((1,), jnp.float32)])[
        saved["slot_assign"]
    ]
    grad_slot = (
        (slot_gate[:, None] * padded_grad[saved["slot_owner"]])
        .astype(jnp.bfloat16)
        .reshape(expert_count, capacity, -1)
    )
    grad_active_part = jnp.einsum(
        "ecd,efd->ecf", grad_slot, weight_out, preferred_element_type=jnp.float32
    )
    grad_w_out = jnp.einsum(
        "ecf,ecd->efd", active_all, grad_slot, preferred_element_type=jnp.float32
    )
    grad_active = sum_halves(grad_active_part.reshape(buffer.shape[0] * buffer.shape[1], -1))
    gelu_pull = jax.vjp(jax.nn.gelu, saved["hidden"])[1]
    grad_hidden = gelu_pull(grad_active)[0].astype(jnp.bfloat16)
    grad_hidden_all = gather_halves(grad_hidden).reshape(buffer.shape[0], buffer.shape[1], -1)
    grad_buffer = jnp.einsum(
        "ecf,edf->ecd", grad_hidden_all, weight_in, preferred_element_type=jnp.float32
    )
    grad_w_in = jnp.einsum(
        "ecd,ecf->edf", buffer, grad_hidden_all, preferred_element_type=jnp.float32
    )
    grad_buffer = grad_buffer.reshape(expert_count * capacity, -1)
    router = saved["router"]
    grad_probs = jnp.sum(grad_gates[:, :, None] * saved["onehot"], axis=1)
    grad_logits = (
        router * (grad_probs - jnp.sum(router * grad_probs, axis=1, keepdims=True))
    ).astype(jnp.bfloat16)
    grad_w_router = jnp.einsum(
        "td,te->de", saved["normed_all"], grad_logits, preferred_element_type=jnp.float32
    )
    router_back = jnp.einsum(
        "te,de->td", grad_logits, weight_router, preferred_element_type=jnp.float32
    )
    leading = (lax.axis_index("row") == 0).astype(jnp.float32)
    grad_part = jnp.sum(grad_buffer[flat_slots], axis=1) + leading * router_back
    return (sum_rows(grad_part), grad_w_router, grad_w_in, grad_w_out)


def per_device(
    tokens,
    norm_gain,
    norm_shift,
    w_qkv,
    w_proj,
    w_router,
    w_in,
    w_out,
    expert_ids,
    slot_ids,
    cotangent,
):
    layer_count = w_qkv.shape[0]
    stream = tokens.astype(jnp.float32)
    attention_saved = []
    expert_saved = []
    for layer_index in range(layer_count):
        weight_qkv = w_qkv[layer_index].reshape(w_qkv.shape[1], -1)
        stream, kept_one = attention_forward(
            stream,
            norm_gain[layer_index, 0],
            norm_shift[layer_index, 0],
            weight_qkv,
            w_proj[layer_index],
        )
        stream, kept_two = expert_forward(
            stream,
            norm_gain[layer_index, 1],
            norm_shift[layer_index, 1],
            expert_ids[layer_index],
            slot_ids[layer_index],
            w_router[layer_index],
            w_in[layer_index],
            w_out[layer_index],
        )
        attention_saved.append(kept_one)
        expert_saved.append(kept_two)
    output = stream.astype(jnp.bfloat16)
    grad_stream = cotangent.astype(jnp.float32)
    qkv_grads = [None] * layer_count
    proj_grads = [None] * layer_count
    router_grads = [None] * layer_count
    in_grads = [None] * layer_count
    out_grads = [None] * layer_count
    gain_grads = [None] * layer_count
    shift_grads = [None] * layer_count
    for layer_index in reversed(range(layer_count)):
        weight_qkv = w_qkv[layer_index].reshape(w_qkv.shape[1], -1)
        kept_two = expert_saved[layer_index]
        grad_normed, router_grads[layer_index], grad_w_in, grad_w_out = expert_backward(
            grad_stream, kept_two, w_router[layer_index], w_in[layer_index], w_out[layer_index]
        )
        grad_w_in, grad_w_out = (
            lax.psum_scatter(grad_w_in, "dp", scatter_dimension=0, tiled=True),
            lax.psum_scatter(grad_w_out, "dp", scatter_dimension=0, tiled=True),
        )
        in_grads[layer_index] = grad_w_in
        out_grads[layer_index] = grad_w_out
        grad_inner, gain_two, shift_two = norm_backward(
            grad_normed, kept_two["normal"], kept_two["inverse"], norm_gain[layer_index, 1]
        )
        grad_stream = grad_stream + grad_inner
        kept_one = attention_saved[layer_index]
        grad_normed, grad_w_qkv, proj_grads[layer_index] = attention_backward(
            grad_stream, kept_one, weight_qkv, w_proj[layer_index]
        )
        qkv_grads[layer_index] = grad_w_qkv.reshape(w_qkv.shape[1:])
        grad_inner, gain_one, shift_one = norm_backward(
            grad_normed, kept_one["normal"], kept_one["inverse"], norm_gain[layer_index, 0]
        )
        grad_stream = grad_stream + grad_inner
        gain_grads[layer_index] = jnp.stack([gain_one, gain_two])
        shift_grads[layer_index] = jnp.stack([shift_one, shift_two])
    grad_qkv, grad_proj, grad_router = lax.psum(
        (jnp.stack(qkv_grads), jnp.stack(proj_grads), jnp.stack(router_grads)), "dp"
    )
    grad_gain, grad_shift = lax.psum((jnp.stack(gain_grads), jnp.stack(shift_grads)), ("dp", "row"))
    grad_in = jnp.stack(in_grads)
    grad_out = jnp.stack(out_grads)
    return (
        output,
        grad_stream,
        grad_qkv,
        grad_proj,
        grad_router,
        grad_in,
        grad_out,
        grad_gain,
        grad_shift,
    )


def exchange(values, axis, offset):
    count = lax.axis_size(axis)
    return lax.ppermute(values, axis, [(place, place ^ offset) for place in range(count)])


def contract(left, right, left_dim, right_dim):
    return lax.dot_general(
        left, right, (((left_dim,), (right_dim,)), ((), ())), preferred_element_type=jnp.float32
    )


def layer_norm_parts(values):
    center = jnp.mean(values, axis=1, keepdims=True)
    shifted = values - center
    spread = jnp.mean(shifted * shifted, axis=1, keepdims=True)
    inverse = lax.rsqrt(spread + EPSILON)
    return (shifted * inverse, inverse)


def layer_norm_pull(upstream, normal, inverse, gain_row):
    scaled = upstream * gain_row
    first = jnp.mean(scaled, axis=1, keepdims=True)
    second = jnp.mean(scaled * normal, axis=1, keepdims=True)
    return inverse * (scaled - first - normal * second)


def gelu_parts(values):
    factor = (2.0 / jnp.pi) ** 0.5
    squares = values * values
    curve = jnp.tanh(values * (factor + (factor * 0.044715) * squares))
    half = 0.5 + 0.5 * curve
    slope = half + (0.5 * values) * (1.0 - curve * curve) * (
        factor + (3.0 * factor * 0.044715) * squares
    )
    return (values * half, slope)


def head_probs(query_head, key_pair, valid):
    scores = contract(query_head, key_pair, 1, 1) * HDIM ** (-0.5)
    scores = jnp.where(valid, scores, -1e30)
    powers = jnp.exp(scores - jnp.max(scores, axis=1, keepdims=True))
    return powers / jnp.sum(powers, axis=1, keepdims=True)


def assemble_weights(place_ref, block_refs, full_ref, rows, features):
    half = features // 2
    strip = features // rows
    for position, block_ref in enumerate(block_refs):
        other, offset = divmod(position, rows)
        side = lax.bitwise_xor(place_ref[2], other)
        top = pl.multiple_of(side * half, half)
        for part in range(3):
            full_ref[pl.ds(top, half), pl.ds(part * features + offset * strip, strip)] = block_ref[
                :, pl.ds(part * strip, strip)
            ]
        for piece in range(half // strip):
            left = pl.multiple_of(3 * features + side * half + piece * strip, strip)
            full_ref[pl.ds(offset * strip, strip), pl.ds(left, strip)] = block_ref[
                pl.ds(piece * strip, strip), pl.ds(3 * strip, strip)
            ]


def attention_forward_kernel(rows, place_ref, *refs):
    block_refs = refs[: 2 * rows]
    norm_ref, stream_ref = refs[2 * rows : 2 * rows + 2]
    start_ref, middle_ref, first_ref, packed_ref, mixed_ref, second_ref, full_ref = refs[-7:]
    part_refs = refs[2 * rows + 2 : -7]
    features = stream_ref.shape[1]
    padded = stream_ref.shape[0]
    assemble_weights(place_ref, block_refs, full_ref, rows, features)
    send(full_ref)
    stream = stream_ref[...].astype(jnp.float32)
    for part_ref in part_refs:
        stream = stream + part_ref[...].astype(jnp.float32)
    start_ref[...] = stream
    send(start_ref)
    normal, _ = layer_norm_parts(stream)
    normed = (normal * norm_ref[0:1] + norm_ref[2:3]).astype(jnp.bfloat16)
    first_ref[...] = normed
    send(first_ref)
    for part in range(3):
        columns = pl.ds(part * features, features)
        packed_ref[:, columns] = contract(normed, full_ref[:, columns], 1, 0).astype(jnp.bfloat16)
    send(packed_ref)
    valid = lax.broadcasted_iota(jnp.int32, (padded, padded), 1) < SEQ
    lower = lax.broadcasted_iota(jnp.int32, (padded, 2 * HDIM), 1) < HDIM
    for pair in range(features // (2 * HDIM)):
        query = packed_ref[:, pl.ds(pair * 2 * HDIM, 2 * HDIM)]
        keys = packed_ref[:, pl.ds(features + pair * 2 * HDIM, 2 * HDIM)]
        values = packed_ref[:, pl.ds(2 * features + pair * 2 * HDIM, 2 * HDIM)]
        blank = jnp.zeros_like(query)
        results = []
        for query_head in (jnp.where(lower, query, blank), jnp.where(lower, blank, query)):
            probs = head_probs(query_head, keys, valid).astype(jnp.bfloat16)
            results.append(contract(probs, values, 1, 0))
        mixed_ref[:, pl.ds(pair * 2 * HDIM, 2 * HDIM)] = jnp.where(
            lower, results[0], results[1]
        ).astype(jnp.bfloat16)
    send(mixed_ref)
    stream = stream + contract(mixed_ref[...], full_ref[:, pl.ds(3 * features, features)], 1, 0)
    middle_ref[...] = stream
    send(middle_ref)
    normal, _ = layer_norm_parts(stream)
    second_ref[...] = (normal * norm_ref[1:2] + norm_ref[3:4]).astype(jnp.bfloat16)


def attention_backward_kernel(rows, place_ref, *refs):
    (
        full_ref,
        norm_ref,
        start_ref,
        middle_ref,
        first_ref,
        packed_ref,
        mixed_ref,
        grad_ref,
        router_ref,
    ) = refs[:9]
    part_refs = refs[9:-5]
    result_ref, branch_ref, blocks_ref, gpacked_ref, gmixed_ref = refs[-5:]
    features = start_ref.shape[1]
    padded = start_ref.shape[0]
    upstream = part_refs[0][...].astype(jnp.float32)
    for part_ref in part_refs[1:]:
        upstream = upstream + part_ref[...].astype(jnp.float32)
    normal, inverse = layer_norm_parts(middle_ref[...])
    gain_two = jnp.sum(upstream * normal, axis=0, keepdims=True)
    shift_two = jnp.sum(upstream, axis=0, keepdims=True)
    grad_middle = grad_ref[...].astype(jnp.float32) + layer_norm_pull(
        upstream, normal, inverse, norm_ref[1:2]
    )
    grad_attn = grad_middle.astype(jnp.bfloat16)
    gmixed_ref[...] = contract(
        grad_attn, full_ref[:, pl.ds(3 * features, features)], 1, 1
    ).astype(jnp.bfloat16)
    valid = lax.broadcasted_iota(jnp.int32, (padded, padded), 1) < SEQ
    lower = lax.broadcasted_iota(jnp.int32, (padded, 2 * HDIM), 1) < HDIM
    scale = HDIM ** (-0.5)
    for pair in range(features // (2 * HDIM)):
        spans = [pl.ds(part * features + pair * 2 * HDIM, 2 * HDIM) for part in range(3)]
        query, keys, values = [packed_ref[:, span] for span in spans]
        gmixed = gmixed_ref[:, spans[0]]
        blank = jnp.zeros_like(query)
        found = []
        for side in range(2):
            keep = lower if side == 0 else jnp.logical_not(lower)
            probs = head_probs(jnp.where(keep, query, blank), keys, valid)
            grad_probs = contract(jnp.where(keep, gmixed, blank), values, 1, 1)
            grad_values = contract(probs.astype(jnp.bfloat16), gmixed, 0, 0)
            grad_scores = (
                probs * (grad_probs - jnp.sum(probs * grad_probs, axis=1, keepdims=True))
            ).astype(jnp.bfloat16)
            grad_query = contract(grad_scores, keys, 1, 0) * scale
            grad_keys = contract(grad_scores, query, 0, 0) * scale
            found.append((grad_query, grad_keys, grad_values))
        for part in range(3):
            gpacked_ref[:, spans[part]] = jnp.where(lower, found[0][part], found[1][part]).astype(
                jnp.bfloat16
            )
    upstream = contract(gpacked_ref[...], full_ref[:, pl.ds(0, 3 * features)], 1, 1)
    normal, inverse = layer_norm_parts(start_ref[...])
    gain_one = jnp.sum(upstream * normal, axis=0, keepdims=True)
    shift_one = jnp.sum(upstream, axis=0, keepdims=True)
    result = grad_middle + layer_norm_pull(upstream, normal, inverse, norm_ref[0:1])
    result_ref[...] = result
    branch_ref[...] = result.astype(jnp.bfloat16)
    half = features // 2
    strip = features // rows
    extra = jnp.concatenate(
        [
            router_ref[...],
            gain_one,
            gain_two,
            shift_one,
            shift_two,
            jnp.zeros((blocks_ref.shape[2] - 4 * strip - router_ref.shape[0] - 4, features), jnp.float32),
        ],
        axis=0,
    ).astype(jnp.bfloat16)
    grad_proj = contract(mixed_ref[...], grad_attn, 0, 0).astype(jnp.bfloat16)
    for offset in range(rows):
        for side in range(2):
            columns = slice(side * half, (side + 1) * half)
            blocks_ref[side, offset, pl.ds(3 * strip, strip), :] = grad_proj[
                offset * strip : (offset + 1) * strip, columns
            ]
            blocks_ref[side, offset, pl.ds(4 * strip, extra.shape[0]), :] = extra[:, columns]
    for part in range(3):
        grad_part = contract(
            gpacked_ref[:, pl.ds(part * features, features)], first_ref[...], 0, 0
        ).astype(jnp.bfloat16)
        for offset in range(rows):
            for side in range(2):
                blocks_ref[side, offset, pl.ds(part * strip, strip), :] = grad_part[
                    offset * strip : (offset + 1) * strip, side * half : (side + 1) * half
                ]


def dispatch_kernel(room, codes_ref, *refs):
    groups = codes_ref.shape[1]
    block_refs, out_refs = refs[:-groups], refs[-groups:]
    padded = block_refs[0].shape[0]
    rows_of = lax.broadcasted_iota(jnp.int32, (room, padded), 0)
    for group in range(groups):
        total = jnp.zeros((room, block_refs[0].shape[1]), jnp.float32)
        for image, block_ref in enumerate(block_refs):
            picks = (codes_ref[image, group : group + 1, :] == rows_of).astype(jnp.float32)
            total = total + contract(picks.astype(jnp.bfloat16), block_ref[...], 1, 0)
        out_refs[group][...] = total.astype(jnp.bfloat16)


def combine_kernel(rows, codes_ref, *refs):
    slot_refs, out_refs = refs[: codes_ref.shape[1]], refs[codes_ref.shape[1] :]
    room = slot_refs[0].shape[0]
    padded = out_refs[0].shape[0]
    lanes = lax.broadcasted_iota(jnp.int32, (padded, room), 1)
    for image in range(rows):
        total = jnp.zeros(out_refs[0].shape, jnp.float32)
        for source, slot_ref in enumerate(slot_refs):
            codes = codes_ref[pl.ds(image * padded, padded), source : source + 1]
            picks = (codes == lanes).astype(jnp.float32)
            total = total + contract(picks.astype(jnp.bfloat16), slot_ref[...], 1, 0)
        out_refs[image][...] = total.astype(jnp.bfloat16)


def expert_router(place_ref, buffer, wrouter):
    router = softmax_rows(contract(buffer, wrouter, 1, 1))
    chosen = lax.broadcasted_iota(jnp.int32, router.shape, 1) == place_ref[3]
    gate = jnp.sum(jnp.where(chosen, router, 0.0), axis=1, keepdims=True)
    return (router, chosen, gate)


def expert_forward_kernel(groups, place_ref, wrouter_ref, win_ref, wout_ref, *refs):
    buffer = jnp.concatenate([ref[...] for ref in refs[:groups]], axis=0)
    room = refs[0].shape[0]
    half = buffer.shape[1] // 2
    _, _, gate = expert_router(place_ref, buffer, wrouter_ref[...])
    sums = [jnp.zeros((buffer.shape[0], half), jnp.float32) for _ in range(2)]
    for quarter in range(win_ref.shape[0] // 2):
        hidden = contract(buffer[:, :half], win_ref[2 * quarter], 1, 0) + contract(
            buffer[:, half:], win_ref[2 * quarter + 1], 1, 0
        )
        active = gelu_parts(hidden)[0].astype(jnp.bfloat16)
        for side in range(2):
            sums[side] = sums[side] + contract(active, wout_ref[2 * quarter + side], 1, 0)
    for group in range(groups):
        span = slice(group * room, (group + 1) * room)
        for side in range(2):
            refs[groups + group][:, pl.ds(side * half, half)] = (
                gate[span] * sums[side][span]
            ).astype(jnp.bfloat16)


def expert_full_kernel(groups, with_output, place_ref, wrouter_ref, win_ref, wout_ref, *refs):
    buffer = jnp.concatenate([ref[...] for ref in refs[:groups]], axis=0)
    grads = jnp.concatenate([ref[...] for ref in refs[groups : 2 * groups]], axis=0)
    back_refs = refs[2 * groups : 3 * groups]
    out_refs = refs[3 * groups : -3]
    gin_ref, gout_ref, grouter_ref = refs[-3:]
    room = refs[0].shape[0]
    half = buffer.shape[1] // 2
    router, chosen, gate = expert_router(place_ref, buffer, wrouter_ref[...])
    grad_slot = (gate * grads.astype(jnp.float32)).astype(jnp.bfloat16)
    flipped = buffer.T
    sums = [jnp.zeros((buffer.shape[0], half), jnp.float32) for _ in range(2)]
    backs = [jnp.zeros((buffer.shape[0], half), jnp.float32) for _ in range(2)]
    grad_gate = jnp.zeros((buffer.shape[0], 1), jnp.float32)
    for quarter in range(win_ref.shape[0] // 2):
        hidden = contract(buffer[:, :half], win_ref[2 * quarter], 1, 0) + contract(
            buffer[:, half:], win_ref[2 * quarter + 1], 1, 0
        )
        value, slope = gelu_parts(hidden)
        active = value.astype(jnp.bfloat16)
        if with_output:
            for side in range(2):
                sums[side] = sums[side] + contract(active, wout_ref[2 * quarter + side], 1, 0)
        pulled = contract(grads[:, :half], wout_ref[2 * quarter], 1, 1) + contract(
            grads[:, half:], wout_ref[2 * quarter + 1], 1, 1
        )
        grad_gate = grad_gate + jnp.sum(
            pulled * active.astype(jnp.float32), axis=1, keepdims=True
        )
        grad_hidden = (gate * pulled * slope).astype(jnp.bfloat16)
        turned = active.T
        for side in range(2):
            block = 2 * quarter + side
            span = slice(side * half, (side + 1) * half)
            backs[side] = backs[side] + contract(grad_hidden, win_ref[block], 1, 1)
            gin_ref[block] = contract(flipped[span], grad_hidden, 1, 0).astype(jnp.bfloat16)
            gout_ref[block] = contract(turned, grad_slot[:, span], 1, 0).astype(jnp.bfloat16)
    grad_logits = (
        router * (jnp.where(chosen, grad_gate, 0.0) - gate * grad_gate)
    ).astype(jnp.bfloat16)
    grouter_ref[...] = contract(grad_logits, buffer, 0, 0)
    router_back = contract(grad_logits, wrouter_ref[...], 1, 0)
    for group in range(groups):
        span = slice(group * room, (group + 1) * room)
        for side in range(2):
            columns = slice(side * half, (side + 1) * half)
            back_refs[group][:, columns] = (
                backs[side][span] + router_back[span, columns]
            ).astype(jnp.bfloat16)
            if with_output:
                out_refs[group][:, columns] = (gate[span] * sums[side][span]).astype(jnp.bfloat16)


SMALL = pl.BlockSpec(memory_space=pltpu.SMEM)
LOCAL = pl.BlockSpec(memory_space=pltpu.VMEM)
FAR = pl.BlockSpec(memory_space=pltpu.HBM)


def widen_kernel(narrow_ref, *refs):
    refs[-1][0, 0] = narrow_ref[0].astype(jnp.float32)


def widen_grads(layer, layer_count, narrow, previous):
    members, *block = narrow.shape
    anywhere = pl.BlockSpec(memory_space=pl.ANY)
    return pl.pallas_call(
        widen_kernel,
        name="widen",
        grid=(members,),
        in_specs=[pl.BlockSpec((1, *block), lambda step: (step, 0, 0))]
        + [anywhere] * len(previous),
        out_specs=pl.BlockSpec((1, 1, *block), lambda step: (layer, step, 0, 0)),
        out_shape=jax.ShapeDtypeStruct((layer_count, members, *block), jnp.float32),
        input_output_aliases={1: 0} if previous else {},
        compiler_params=pltpu.CompilerParams(vmem_limit_bytes=4 * 1024 * 1024),
    )(narrow, *previous)


class Staged:
    def __init__(self, ref, move=None):
        self.ref, self.move = ref, move
        self.shape, self.dtype = ref.shape, ref.dtype

    def __getitem__(self, index):
        if self.move is not None:
            self.move.wait()
            self.move = None
        return self.ref[index]


class Sent:
    def __init__(self, ref, move):
        self.ref, self.move, self.moving = ref, move, False
        self.shape, self.dtype = ref.shape, ref.dtype

    def __getitem__(self, index):
        return self.ref[index]

    def __setitem__(self, index, values):
        self.ref[index] = values

    def send(self):
        if not self.moving:
            self.move.start()
            self.moving = True


def send(ref):
    if isinstance(ref, Sent):
        ref.send()


def staged_body(body, fixed_count, operand_count, far, *refs):
    fixed, refs = refs[:fixed_count], refs[fixed_count:]
    sources, refs = refs[:operand_count], refs[operand_count:]
    targets, refs = list(refs[: len(far)]), refs[len(far) :]
    copies, refs = refs[:operand_count], refs[operand_count:]
    made, refs = refs[: sum(far)], refs[sum(far) :]
    marks, scratch = refs[0], refs[1:]
    staged = []
    for place, (source, copy) in enumerate(zip(sources, copies)):
        move = pltpu.make_async_copy(source, copy, marks.at[place])
        move.start()
        staged.append(Staged(copy, move))
    made = list(made)
    for place, apart in enumerate(far):
        if apart:
            near = made.pop(0)
            move = pltpu.make_async_copy(near, targets[place], marks.at[operand_count + place])
            targets[place] = Sent(near, move)
    body(*fixed, *staged, *targets, *scratch)
    for piece in staged:
        if piece.move is not None:
            piece.move.wait()
    for target in targets:
        if isinstance(target, Sent):
            target.send()
    for target in targets:
        if isinstance(target, Sent):
            target.move.wait()


def run_kernel(title, body, place, operands, results, work, scratch=(), room=16, far=()):
    fixed = [] if place is None else [place]
    arguments = fixed + [pltpu.with_memory_space_constraint(piece, pltpu.HBM) for piece in operands]
    apart = [place in far for place in range(len(results))]
    return pl.pallas_call(
        functools.partial(staged_body, body, len(fixed), len(operands), apart),
        name=title,
        in_specs=[SMALL] * len(fixed) + [FAR] * len(operands),
        out_specs=[FAR if away else LOCAL for away in apart],
        out_shape=[
            pltpu.HBM(shape, kind) if away else jax.ShapeDtypeStruct(shape, kind)
            for away, (shape, kind) in zip(apart, results)
        ],
        scratch_shapes=[pltpu.VMEM(piece.shape, piece.dtype) for piece in operands]
        + [pltpu.VMEM(shape, kind) for away, (shape, kind) in zip(apart, results) if away]
        + [pltpu.SemaphoreType.DMA((len(operands) + len(results),))]
        + list(scratch),
        compiler_params=pltpu.CompilerParams(vmem_limit_bytes=room * 1024 * 1024),
        cost_estimate=pl.CostEstimate(
            flops=work,
            bytes_accessed=sum(piece.size * piece.dtype.itemsize for piece in arguments),
            transcendentals=0,
        ),
    )(*arguments)


def after(values, *earlier):
    return lax.optimization_barrier((values, *earlier))[0]


def gather_group(values):
    near = [values]
    for offset in range(1, lax.axis_size("row")):
        near.append(exchange(values, "row", offset))
    return near + [exchange(piece, "col", 1) for piece in near]


def scatter_pieces(pieces, axis):
    return [
        piece if offset == 0 else exchange(piece, axis, offset)
        for offset, piece in enumerate(pieces)
    ]


def add_pieces(pieces):
    total = pieces[0].astype(jnp.float32)
    for piece in pieces[1:]:
        total = total + piece.astype(jnp.float32)
    return total


def sum_chip(blocks, at_col):
    mine = lax.dynamic_index_in_dim(blocks, at_col, 0, keepdims=False)
    other = exchange(lax.dynamic_index_in_dim(blocks, 1 - at_col, 0, keepdims=False), "col", 1)
    return add_pieces([mine, other]).astype(blocks.dtype)


def sum_groups(plane):
    groups, at_dp = lax.axis_size("dp"), lax.axis_index("dp")
    part = plane.shape[0] // groups
    pieces = [
        lax.dynamic_slice_in_dim(plane, (at_dp ^ offset) * part, part, 0)
        for offset in range(groups)
    ]
    owned = add_pieces(scatter_pieces(pieces, "dp")).astype(plane.dtype)
    result = jnp.zeros(plane.shape, jnp.float32)
    for offset in range(groups):
        piece = owned if offset == 0 else exchange(owned, "dp", offset)
        result = lax.dynamic_update_slice_in_dim(
            result, piece.astype(jnp.float32), (at_dp ^ offset) * part, 0
        )
    return result


def group_device(
    tokens,
    norm_gain,
    norm_shift,
    w_qkv,
    w_proj,
    w_router,
    w_in,
    w_out,
    expert_ids,
    slot_ids,
    cotangent,
):
    low = jnp.bfloat16
    groups, rows = lax.axis_size("dp"), lax.axis_size("row")
    members = 2 * rows
    at_dp, at_row, at_col = [lax.axis_index(name) for name in ("dp", "row", "col")]
    layer_count = w_qkv.shape[0]
    expert_count = w_in.shape[1]
    half = tokens.shape[1]
    features = 2 * half
    strip = features // rows
    padded = -(-SEQ // 16) * 16
    owner = at_dp * members + at_row * 2 + at_col
    place = jnp.stack([at_dp, at_row, at_col, owner]).astype(jnp.int32)

    def join(mine, other):
        return jnp.where(
            at_col == 0,
            jnp.concatenate([mine, other], axis=-1),
            jnp.concatenate([other, mine], axis=-1),
        )

    small = jnp.concatenate(
        [
            jnp.concatenate([norm_gain, norm_shift], axis=1).reshape(-1, half),
            w_router.transpose(0, 2, 1).reshape(-1, half).astype(jnp.float32),
        ],
        axis=0,
    )
    small = join(small, exchange(small, "col", 1))
    norms = small[: 4 * layer_count].reshape(layer_count, 4, features)
    routers = small[4 * layer_count :].reshape(layer_count, expert_count, features).astype(low)
    both = jnp.stack([tokens, cotangent]).reshape(2, 2, SEQ, half)
    mine = lax.dynamic_index_in_dim(both, at_col, 1, keepdims=False)
    other = exchange(lax.dynamic_index_in_dim(both, 1 - at_col, 1, keepdims=False), "col", 1)
    both = jnp.pad(join(mine, other), ((0, 0), (0, padded - SEQ), (0, 0)))

    def fetch_attention(layer, *earlier):
        block = jnp.concatenate(
            [
                w_qkv[layer].reshape(half, -1),
                jnp.concatenate(
                    [
                        w_proj[layer][:, piece * strip : (piece + 1) * strip]
                        for piece in range(half // strip)
                    ],
                    axis=0,
                ),
            ],
            axis=1,
        )
        return gather_group(after(block, *earlier) if earlier else block)

    def own_experts(layer, source):
        own = lax.dynamic_slice(
            source, (layer, at_dp * members, 0, 0), (1, members, *source.shape[2:])
        )
        return own[0]

    def fetch_weights(own, *earlier):
        return lax.all_to_all(
            after(own, *earlier), ("row", "col"), split_axis=0, concat_axis=0, tiled=True
        )

    capacity = 2 * ((5 * members * SEQ + 4 * expert_count - 1) // (4 * expert_count))
    room = -(-capacity // 16) * 16
    images = jnp.stack(
        [(at_row ^ offset) * 2 + (at_col ^ side) for side in range(2) for offset in range(rows)]
    )
    named = jnp.stack(
        [
            (at_dp ^ offset) * members + at_row * 2 + (at_col ^ side)
            for side in range(2)
            for offset in range(groups)
        ]
    )
    chosen = jnp.take(expert_ids.reshape(layer_count, members, SEQ, -1), images, axis=1)
    slots = jnp.take(slot_ids.reshape(layer_count, members, SEQ, -1), images, axis=1)
    codes = jnp.max(
        jnp.where(chosen[..., None] == named, slots[..., None], -1), axis=3
    )
    codes = jnp.pad(codes, ((0, 0), (0, 0), (0, padded - SEQ), (0, 0)), constant_values=-1)
    send_codes = codes[..., :groups].transpose(0, 1, 3, 2)
    back_codes = codes[:, :rows].reshape(layer_count, rows * padded, 2 * groups)

    token_block = ((padded, features), low)
    slot_block = ((room, features), low)

    def dispatch(layer, images):
        return run_kernel(
            "dispatch",
            functools.partial(dispatch_kernel, room),
            None,
            [send_codes[layer]] + images,
            [slot_block] * groups,
            2 * members * padded * groups * room * features,
        )

    def bring_back(blocks):
        blocks = scatter_pieces(blocks, "dp")
        return blocks + [exchange(piece, "col", 1) for piece in blocks]

    def combine(layer, blocks):
        return run_kernel(
            "combine",
            functools.partial(combine_kernel, rows),
            None,
            [back_codes[layer]] + blocks,
            [token_block] * rows,
            4 * rows * padded * groups * room * features,
        )

    def split(values):
        pieces = values[:SEQ].reshape(SEQ, 2, half)
        mine = lax.dynamic_index_in_dim(pieces, at_col, 1, keepdims=False)
        other = exchange(lax.dynamic_index_in_dim(pieces, 1 - at_col, 1, keepdims=False), "col", 1)
        return jnp.where(
            at_col == 0,
            jnp.concatenate([mine, other], axis=0),
            jnp.concatenate([other, mine], axis=0),
        )

    def after_all(pieces, *earlier):
        return [after(piece, *earlier) for piece in pieces]

    work = 4 * groups * room * members * half * w_in.shape[3]
    stream, parts = both[0], []
    kept, buffers, weights = [], [], []
    attention_blocks = fetch_attention(0)
    ready = attention_blocks[1:rows]
    for layer in range(layer_count):
        last = layer == layer_count - 1
        weight_in = fetch_weights(own_experts(layer, w_in), *ready)
        own_out = own_experts(layer, w_out)
        upstream = []
        if last:
            upstream = gather_group(after(both[1], *parts[1:]))
        saved = run_kernel(
            "attention_forward",
            functools.partial(attention_forward_kernel, rows),
            place,
            attention_blocks + [norms[layer], stream] + parts,
            [
                ((padded, features), jnp.float32),
                ((padded, features), jnp.float32),
                token_block,
                ((padded, 3 * features), low),
                token_block,
                token_block,
                ((features, 4 * features), low),
            ],
            16 * padded * features * features,
            far=(0, 1, 2, 3, 4, 6),
        )
        kept.append(saved)
        stream = saved[1]
        images = gather_group(saved[5])
        weight_out = fetch_weights(own_out, *images[1:rows], *upstream[1:rows])
        weights.append([weight_in, weight_out])
        buffers.append(scatter_pieces(dispatch(layer, images), "dp"))
        if last:
            branches = scatter_pieces(dispatch(layer, upstream), "dp")
        else:
            result = run_kernel(
                "expert_forward",
                functools.partial(expert_forward_kernel, groups),
                place,
                [routers[layer]] + weights[layer] + buffers[layer],
                [slot_block] * groups,
                work,
            )
            ready = [result[0]]
            attention_blocks = fetch_attention(layer + 1, result[0])
            parts = scatter_pieces(combine(layer, bring_back(result)), "row")
    grad = both[1]
    shared = [None] * layer_count
    grad_in, grad_out, sooner = [], [], []
    for layer in reversed(range(layer_count)):
        last = layer == layer_count - 1
        found = run_kernel(
            "expert_full",
            functools.partial(expert_full_kernel, groups, last),
            place,
            [routers[layer]] + weights[layer] + buffers[layer] + branches,
            [slot_block] * (2 * groups if last else groups)
            + [
                (weights[layer][0].shape, low),
                (weights[layer][1].shape, low),
                ((expert_count, features), jnp.float32),
            ],
            3 * work,
            room=24,
        )
        blocks = bring_back(list(found[:groups]))
        pieces = combine(layer, after_all(blocks, *grad_out, *sooner))
        if last:
            moved_in = fetch_weights(found[-3])
            pieces = after_all(pieces, moved_in)
        grad_parts = scatter_pieces(pieces, "row")
        if not last:
            moved_in = fetch_weights(found[-3], *grad_parts[1:])
        if last:
            outputs = bring_back(after_all(list(found[groups : 2 * groups]), pieces[0]))
        saved = kept[layer]
        height = -(-(4 * strip + expert_count + 4) // (16 * groups)) * (16 * groups)
        grad, branch, blocks = run_kernel(
            "attention_backward",
            functools.partial(attention_backward_kernel, rows),
            place,
            [saved[6], norms[layer], saved[0], saved[1], saved[2], saved[3], saved[4], grad]
            + [found[-1]]
            + grad_parts,
            [
                ((padded, features), jnp.float32),
                token_block,
                ((2, rows, height, half), low),
            ],
            32 * padded * features * features,
            [pltpu.VMEM((padded, 3 * features), low), pltpu.VMEM((padded, features), low)],
        )
        chip = sum_chip(blocks, at_col)
        if layer > 0:
            images = gather_group(after(branch, *outputs) if last else branch)
            moved_out = fetch_weights(found[-2], *images[1:rows])
            grad_in = [widen_grads(layer, layer_count, moved_in, grad_in)]
            branches = scatter_pieces(dispatch(layer - 1, images), "dp")
            earlier = list(grad_in)
            if last:
                outputs = combine(layer, outputs)
                earlier = earlier + list(outputs)
                parts = scatter_pieces(after_all(outputs, moved_out), "row")
            branches = after_all(branches, *earlier)
            arrived = scatter_pieces(after_all(list(chip), moved_out), "row")
            grad_out = [widen_grads(layer, layer_count, moved_out, grad_out)]
            sooner = arrived[1:] + parts[1:]
            for part in parts:
                stream = stream + part.astype(jnp.float32)
            parts = []
        else:
            grad_in = [widen_grads(layer, layer_count, moved_in, grad_in)]
            arrived = scatter_pieces(after_all(list(chip), *shared[1:]), "row")
            moved_out = fetch_weights(found[-2], *arrived[1:])
            output = split(stream.astype(low))
            arrived = after_all(arrived, *grad_in, output)
            grad_out = [widen_grads(layer, layer_count, moved_out, grad_out)]
        shared[layer] = sum_groups(add_pieces(arrived).astype(low))
    grad_input = split(grad)
    shared = jnp.stack(shared)
    grad_qkv = (
        shared[:, : 3 * strip].reshape(layer_count, 3, strip, half).transpose(0, 3, 1, 2)
    )
    grad_proj = shared[:, 3 * strip : 4 * strip]
    grad_router = shared[:, 4 * strip : 4 * strip + expert_count].transpose(0, 2, 1)
    tail = shared[:, 4 * strip + expert_count : 4 * strip + expert_count + 4]
    return (
        output,
        grad_input,
        grad_qkv,
        grad_proj,
        grad_router,
        grad_in[0],
        grad_out[0],
        tail[:, :2],
        tail[:, 2:],
    )


def fits_groups(mesh, tokens, w_in):
    groups, rows, sides = mesh.shape["dp"], mesh.shape["row"], mesh.shape["col"]
    powers = all(size & (size - 1) == 0 for size in (groups, rows))
    return (
        sides == 2
        and powers
        and tokens.shape[0] == groups * rows * sides * SEQ
        and w_in.shape[1] == groups * rows * sides
    )


def solution(mesh):
    in_specs = (
        P(("dp", "row"), "col"),
        P(None, None, "col"),
        P(None, None, "col"),
        P(None, "col", None, "row"),
        P(None, "row", "col"),
        P(None, "col", None),
        P(None, None, "col", "row"),
        P(None, None, "row", "col"),
        P(None, "dp", None),
        P(None, "dp", None),
        P(("dp", "row"), "col"),
    )
    out_specs = (
        P(("dp", "row"), "col"),
        P(("dp", "row"), "col"),
        P(None, "col", None, "row"),
        P(None, "row", "col"),
        P(None, "col", None),
        P(None, "dp", "col", "row"),
        P(None, "dp", "row", "col"),
        P(None, None, "col"),
        P(None, None, "col"),
    )

    def program(*arguments):
        fits = fits_groups(mesh, arguments[0], arguments[6])
        return jax.shard_map(
            group_device if fits else per_device,
            mesh=mesh,
            in_specs=in_specs,
            out_specs=out_specs,
            check_vma=False,
        )(*arguments)

    return program
```

```python
import functools

import jax
import jax.numpy as jnp
from jax import lax
from jax.experimental import pallas as pl
from jax.experimental.pallas import tpu as pltpu
from jax.sharding import PartitionSpec as P

HDIM = 64
SEQ = 197


EPSILON = 1e-06


def gather_rows(values):
    return lax.all_gather(values, "row", axis=0, tiled=True)


def sum_rows(values):
    return lax.psum_scatter(values, "row", scatter_dimension=0, tiled=True)


def gather_halves(values):
    return lax.all_gather(values, "col", axis=0, tiled=True)


def sum_halves(values):
    return lax.psum_scatter(values, "col", scatter_dimension=0, tiled=True)


def row_totals(first, second):
    return lax.psum((first, second), "col")


def softmax_rows(values):
    shifted = jnp.exp(values - jnp.max(values, axis=-1, keepdims=True))
    return shifted / jnp.sum(shifted, axis=-1, keepdims=True)


def norm_forward(stream, gain_row, shift_row):
    feature_count = stream.shape[1] * lax.axis_size("col")
    total, squares = row_totals(jnp.sum(stream, axis=1), jnp.sum(stream * stream, axis=1))
    center = total / feature_count
    inverse = lax.rsqrt(squares / feature_count - center * center + EPSILON)
    normal = (stream - center[:, None]) * inverse[:, None]
    return (normal * gain_row + shift_row, normal, inverse)


def norm_backward(upstream, normal, inverse, gain_row):
    feature_count = upstream.shape[1] * lax.axis_size("col")
    scaled = upstream * gain_row
    first, second = row_totals(jnp.sum(scaled, axis=1), jnp.sum(scaled * normal, axis=1))
    result_grad = inverse[:, None] * (
        scaled - first[:, None] / feature_count - normal * (second[:, None] / feature_count)
    )
    return (result_grad, jnp.sum(upstream * normal, axis=0), jnp.sum(upstream, axis=0))


def split_heads(packed):
    row_count = packed.shape[0]
    heads_here = packed.shape[1] // (3 * HDIM)
    parts = packed.reshape(row_count // SEQ, SEQ, 3, heads_here, HDIM)
    return (parts[:, :, 0], parts[:, :, 1], parts[:, :, 2])


def attend_forward(packed):
    query_part, key_part, value_part = split_heads(packed)
    scores = jnp.einsum(
        "bqhd,bkhd->bhqk", query_part, key_part, preferred_element_type=jnp.float32
    ) * HDIM ** (-0.5)
    highest = jnp.max(scores, axis=-1, keepdims=True)
    powers = jnp.exp(scores - highest)
    totals = jnp.sum(powers, axis=-1, keepdims=True)
    weights = (powers / totals).astype(jnp.bfloat16)
    mixed_heads = jnp.einsum(
        "bhqk,bkhd->bqhd", weights, value_part, preferred_element_type=jnp.float32
    )
    return (
        mixed_heads.reshape(packed.shape[0], -1).astype(jnp.bfloat16),
        highest + jnp.log(totals),
    )


def attend_backward(packed, logsum, grad_mixed):
    query_part, key_part, value_part = split_heads(packed)
    scale = HDIM ** (-0.5)
    scores = (
        jnp.einsum("bqhd,bkhd->bhqk", query_part, key_part, preferred_element_type=jnp.float32)
        * scale
    )
    probs_full = jnp.exp(scores - logsum)
    upstream = grad_mixed.reshape(query_part.shape)
    grad_probs = jnp.einsum(
        "bqhd,bkhd->bhqk", upstream, value_part, preferred_element_type=jnp.float32
    )
    grad_values = jnp.einsum(
        "bhqk,bqhd->bkhd",
        probs_full.astype(jnp.bfloat16),
        upstream,
        preferred_element_type=jnp.float32,
    )
    grad_scores = (
        probs_full * (grad_probs - jnp.sum(probs_full * grad_probs, axis=-1, keepdims=True))
    ).astype(jnp.bfloat16)
    grad_query = (
        jnp.einsum("bhqk,bkhd->bqhd", grad_scores, key_part, preferred_element_type=jnp.float32)
        * scale
    )
    grad_keys = (
        jnp.einsum("bhqk,bqhd->bkhd", grad_scores, query_part, preferred_element_type=jnp.float32)
        * scale
    )
    stacked = jnp.stack([grad_query, grad_keys, grad_values], axis=2)
    return stacked.reshape(packed.shape[0], -1).astype(jnp.bfloat16)


def attention_forward(stream, gain_row, shift_row, weight_qkv, weight_proj):
    normed, normal, inverse = norm_forward(stream, gain_row, shift_row)
    normed_all = gather_rows(normed.astype(jnp.bfloat16))
    packed = sum_halves(jnp.dot(normed_all, weight_qkv, preferred_element_type=jnp.float32)).astype(
        jnp.bfloat16
    )
    mixed_heads, logsum = attend_forward(packed)
    mixed_all = gather_halves(mixed_heads)
    branch = sum_rows(jnp.dot(mixed_all, weight_proj, preferred_element_type=jnp.float32))
    saved = {
        "normal": normal,
        "inverse": inverse,
        "normed_all": normed_all,
        "packed": packed,
        "logsum": logsum,
        "mixed_all": mixed_all,
    }
    return (stream + branch, saved)


def attention_backward(upstream, saved, weight_qkv, weight_proj):
    grad_all = gather_rows(upstream.astype(jnp.bfloat16))
    grad_mixed = sum_halves(
        jnp.einsum("te,de->td", grad_all, weight_proj, preferred_element_type=jnp.float32)
    ).astype(jnp.bfloat16)
    grad_w_proj = jnp.einsum(
        "td,te->de", saved["mixed_all"], grad_all, preferred_element_type=jnp.float32
    )
    grad_packed = attend_backward(saved["packed"], saved["logsum"], grad_mixed)
    grad_packed_all = gather_halves(grad_packed)
    grad_part = jnp.einsum(
        "tf,df->td", grad_packed_all, weight_qkv, preferred_element_type=jnp.float32
    )
    grad_w_qkv = jnp.einsum(
        "td,tf->df", saved["normed_all"], grad_packed_all, preferred_element_type=jnp.float32
    )
    return (sum_rows(grad_part), grad_w_qkv, grad_w_proj)


def second_product(active, buffer_shape, weight_out):
    active_all = gather_halves(active).reshape(buffer_shape[0], buffer_shape[1], -1)
    slot_out = jnp.einsum(
        "ecf,efd->ecd", active_all, weight_out, preferred_element_type=jnp.float32
    )
    return (active_all, slot_out.reshape(-1, slot_out.shape[2]))


def expert_forward(
    stream, gain_row, shift_row, choice_ids, slot_rows, weight_router, weight_in, weight_out
):
    normed, normal, inverse = norm_forward(stream, gain_row, shift_row)
    normed_all = gather_rows(normed.astype(jnp.bfloat16))
    row_count = normed_all.shape[0]
    expert_count = weight_in.shape[0]
    capacity = 2 * ((5 * row_count + 4 * expert_count - 1) // (4 * expert_count))
    logits = lax.psum(jnp.dot(normed_all, weight_router, preferred_element_type=jnp.float32), "col")
    router = softmax_rows(logits)
    onehot = (
        choice_ids[:, :, None] == lax.broadcasted_iota(jnp.int32, (1, 1, expert_count), 2)
    ).astype(jnp.float32)
    gate_values = jnp.sum(onehot * router[:, None, :], axis=2)
    flat_slots = choice_ids * capacity + slot_rows
    owners = jnp.broadcast_to(
        lax.broadcasted_iota(jnp.int32, (row_count, 1), 0), flat_slots.shape
    ).reshape(-1)
    slot_owner = (
        jnp.full((expert_count * capacity,), row_count, jnp.int32)
        .at[flat_slots.reshape(-1)]
        .set(owners)
    )
    slot_assign = (
        jnp.full((expert_count * capacity,), 2 * row_count, jnp.int32)
        .at[flat_slots.reshape(-1)]
        .set(lax.iota(jnp.int32, 2 * row_count))
    )
    padded = jnp.concatenate(
        [normed_all, jnp.zeros((1, normed_all.shape[1]), jnp.bfloat16)], axis=0
    )
    buffer = padded[slot_owner].reshape(expert_count, capacity, -1)
    hidden_part = jnp.einsum("ecd,edf->ecf", buffer, weight_in, preferred_element_type=jnp.float32)
    hidden = sum_halves(hidden_part.reshape(buffer.shape[0] * buffer.shape[1], -1))
    active = jax.nn.gelu(hidden).astype(jnp.bfloat16)
    active_all, slot_out = second_product(active, buffer.shape, weight_out)
    branch_part = jnp.sum(gate_values[:, :, None] * slot_out[flat_slots], axis=1)
    saved = {
        "normal": normal,
        "inverse": inverse,
        "normed_all": normed_all,
        "router": router,
        "onehot": onehot,
        "gate_values": gate_values,
        "flat_slots": flat_slots,
        "slot_owner": slot_owner,
        "slot_assign": slot_assign,
        "buffer": buffer,
        "hidden": hidden,
        "active": active,
    }
    saved["active_all"] = active_all
    saved["slot_out"] = slot_out
    return (stream + sum_rows(branch_part), saved)


def expert_backward(upstream, saved, weight_router, weight_in, weight_out):
    buffer = saved["buffer"]
    expert_count = weight_in.shape[0]
    capacity = saved["slot_owner"].shape[0] // expert_count
    active_all = saved["active_all"]
    slot_out = saved["slot_out"]
    flat_slots = saved["flat_slots"]
    grad_all = gather_rows(upstream.astype(jnp.bfloat16))
    gate_part = jnp.sum(grad_all.astype(jnp.float32)[:, None, :] * slot_out[flat_slots], axis=2)
    grad_gates = lax.psum(gate_part, ("row", "col"))
    padded_grad = jnp.concatenate(
        [grad_all, jnp.zeros((1, grad_all.shape[1]), jnp.bfloat16)], axis=0
    )
    slot_gate = jnp.concatenate([saved["gate_values"].reshape(-1), jnp.zeros((1,), jnp.float32)])[
        saved["slot_assign"]
    ]
    grad_slot = (
        (slot_gate[:, None] * padded_grad[saved["slot_owner"]])
        .astype(jnp.bfloat16)
        .reshape(expert_count, capacity, -1)
    )
    grad_active_part = jnp.einsum(
        "ecd,efd->ecf", grad_slot, weight_out, preferred_element_type=jnp.float32
    )
    grad_w_out = jnp.einsum(
        "ecf,ecd->efd", active_all, grad_slot, preferred_element_type=jnp.float32
    )
    grad_active = sum_halves(grad_active_part.reshape(buffer.shape[0] * buffer.shape[1], -1))
    gelu_pull = jax.vjp(jax.nn.gelu, saved["hidden"])[1]
    grad_hidden = gelu_pull(grad_active)[0].astype(jnp.bfloat16)
    grad_hidden_all = gather_halves(grad_hidden).reshape(buffer.shape[0], buffer.shape[1], -1)
    grad_buffer = jnp.einsum(
        "ecf,edf->ecd", grad_hidden_all, weight_in, preferred_element_type=jnp.float32
    )
    grad_w_in = jnp.einsum(
        "ecd,ecf->edf", buffer, grad_hidden_all, preferred_element_type=jnp.float32
    )
    grad_buffer = grad_buffer.reshape(expert_count * capacity, -1)
    router = saved["router"]
    grad_probs = jnp.sum(grad_gates[:, :, None] * saved["onehot"], axis=1)
    grad_logits = (
        router * (grad_probs - jnp.sum(router * grad_probs, axis=1, keepdims=True))
    ).astype(jnp.bfloat16)
    grad_w_router = jnp.einsum(
        "td,te->de", saved["normed_all"], grad_logits, preferred_element_type=jnp.float32
    )
    router_back = jnp.einsum(
        "te,de->td", grad_logits, weight_router, preferred_element_type=jnp.float32
    )
    leading = (lax.axis_index("row") == 0).astype(jnp.float32)
    grad_part = jnp.sum(grad_buffer[flat_slots], axis=1) + leading * router_back
    return (sum_rows(grad_part), grad_w_router, grad_w_in, grad_w_out)


def per_device(
    tokens,
    norm_gain,
    norm_shift,
    w_qkv,
    w_proj,
    w_router,
    w_in,
    w_out,
    expert_ids,
    slot_ids,
    cotangent,
):
    layer_count = w_qkv.shape[0]
    stream = tokens.astype(jnp.float32)
    attention_saved = []
    expert_saved = []
    for layer_index in range(layer_count):
        weight_qkv = w_qkv[layer_index].reshape(w_qkv.shape[1], -1)
        stream, kept_one = attention_forward(
            stream,
            norm_gain[layer_index, 0],
            norm_shift[layer_index, 0],
            weight_qkv,
            w_proj[layer_index],
        )
        stream, kept_two = expert_forward(
            stream,
            norm_gain[layer_index, 1],
            norm_shift[layer_index, 1],
            expert_ids[layer_index],
            slot_ids[layer_index],
            w_router[layer_index],
            w_in[layer_index],
            w_out[layer_index],
        )
        attention_saved.append(kept_one)
        expert_saved.append(kept_two)
    output = stream.astype(jnp.bfloat16)
    grad_stream = cotangent.astype(jnp.float32)
    qkv_grads = [None] * layer_count
    proj_grads = [None] * layer_count
    router_grads = [None] * layer_count
    in_grads = [None] * layer_count
    out_grads = [None] * layer_count
    gain_grads = [None] * layer_count
    shift_grads = [None] * layer_count
    for layer_index in reversed(range(layer_count)):
        weight_qkv = w_qkv[layer_index].reshape(w_qkv.shape[1], -1)
        kept_two = expert_saved[layer_index]
        grad_normed, router_grads[layer_index], grad_w_in, grad_w_out = expert_backward(
            grad_stream, kept_two, w_router[layer_index], w_in[layer_index], w_out[layer_index]
        )
        grad_w_in, grad_w_out = (
            lax.psum_scatter(grad_w_in, "dp", scatter_dimension=0, tiled=True),
            lax.psum_scatter(grad_w_out, "dp", scatter_dimension=0, tiled=True),
        )
        in_grads[layer_index] = grad_w_in
        out_grads[layer_index] = grad_w_out
        grad_inner, gain_two, shift_two = norm_backward(
            grad_normed, kept_two["normal"], kept_two["inverse"], norm_gain[layer_index, 1]
        )
        grad_stream = grad_stream + grad_inner
        kept_one = attention_saved[layer_index]
        grad_normed, grad_w_qkv, proj_grads[layer_index] = attention_backward(
            grad_stream, kept_one, weight_qkv, w_proj[layer_index]
        )
        qkv_grads[layer_index] = grad_w_qkv.reshape(w_qkv.shape[1:])
        grad_inner, gain_one, shift_one = norm_backward(
            grad_normed, kept_one["normal"], kept_one["inverse"], norm_gain[layer_index, 0]
        )
        grad_stream = grad_stream + grad_inner
        gain_grads[layer_index] = jnp.stack([gain_one, gain_two])
        shift_grads[layer_index] = jnp.stack([shift_one, shift_two])
    grad_qkv, grad_proj, grad_router = lax.psum(
        (jnp.stack(qkv_grads), jnp.stack(proj_grads), jnp.stack(router_grads)), "dp"
    )
    grad_gain, grad_shift = lax.psum((jnp.stack(gain_grads), jnp.stack(shift_grads)), ("dp", "row"))
    grad_in = jnp.stack(in_grads)
    grad_out = jnp.stack(out_grads)
    return (
        output,
        grad_stream,
        grad_qkv,
        grad_proj,
        grad_router,
        grad_in,
        grad_out,
        grad_gain,
        grad_shift,
    )


def exchange(values, axis, offset):
    count = lax.axis_size(axis)
    return lax.ppermute(values, axis, [(place, place ^ offset) for place in range(count)])


def contract(left, right, left_dim, right_dim):
    return lax.dot_general(
        left, right, (((left_dim,), (right_dim,)), ((), ())), preferred_element_type=jnp.float32
    )


def layer_norm_parts(values):
    center = jnp.mean(values, axis=1, keepdims=True)
    shifted = values - center
    spread = jnp.mean(shifted * shifted, axis=1, keepdims=True)
    inverse = lax.rsqrt(spread + EPSILON)
    return (shifted * inverse, inverse)


def layer_norm_pull(upstream, normal, inverse, gain_row):
    scaled = upstream * gain_row
    first = jnp.mean(scaled, axis=1, keepdims=True)
    second = jnp.mean(scaled * normal, axis=1, keepdims=True)
    return inverse * (scaled - first - normal * second)


def gelu_parts(values):
    factor = (2.0 / jnp.pi) ** 0.5
    squares = values * values
    curve = jnp.tanh(values * (factor + (factor * 0.044715) * squares))
    half = 0.5 + 0.5 * curve
    slope = half + (0.5 * values) * (1.0 - curve * curve) * (
        factor + (3.0 * factor * 0.044715) * squares
    )
    return (values * half, slope)


def head_probs(query_head, key_pair, valid):
    scores = contract(query_head, key_pair, 1, 1) * HDIM ** (-0.5)
    scores = jnp.where(valid, scores, -1e30)
    powers = jnp.exp(scores - jnp.max(scores, axis=1, keepdims=True))
    return powers / jnp.sum(powers, axis=1, keepdims=True)


def assemble_weights(place_ref, block_refs, full_ref, rows, features):
    half = features // 2
    strip = features // rows
    for position, block_ref in enumerate(block_refs):
        other, offset = divmod(position, rows)
        side = lax.bitwise_xor(place_ref[2], other)
        top = pl.multiple_of(side * half, half)
        for part in range(3):
            full_ref[pl.ds(top, half), pl.ds(part * features + offset * strip, strip)] = block_ref[
                :, pl.ds(part * strip, strip)
            ]
        for piece in range(half // strip):
            left = pl.multiple_of(3 * features + side * half + piece * strip, strip)
            full_ref[pl.ds(offset * strip, strip), pl.ds(left, strip)] = block_ref[
                pl.ds(piece * strip, strip), pl.ds(3 * strip, strip)
            ]


def attention_forward_kernel(rows, place_ref, *refs):
    block_refs = refs[: 2 * rows]
    norm_ref, stream_ref = refs[2 * rows : 2 * rows + 2]
    start_ref, middle_ref, first_ref, packed_ref, mixed_ref, second_ref, full_ref = refs[-7:]
    part_refs = refs[2 * rows + 2 : -7]
    features = stream_ref.shape[1]
    padded = stream_ref.shape[0]
    assemble_weights(place_ref, block_refs, full_ref, rows, features)
    send(full_ref)
    stream = stream_ref[...].astype(jnp.float32)
    for part_ref in part_refs:
        stream = stream + part_ref[...].astype(jnp.float32)
    start_ref[...] = stream
    send(start_ref)
    normal, _ = layer_norm_parts(stream)
    normed = (normal * norm_ref[0:1] + norm_ref[2:3]).astype(jnp.bfloat16)
    first_ref[...] = normed
    send(first_ref)
    for part in range(3):
        columns = pl.ds(part * features, features)
        packed_ref[:, columns] = contract(normed, full_ref[:, columns], 1, 0).astype(jnp.bfloat16)
    send(packed_ref)
    valid = lax.broadcasted_iota(jnp.int32, (padded, padded), 1) < SEQ
    lower = lax.broadcasted_iota(jnp.int32, (padded, 2 * HDIM), 1) < HDIM
    for pair in range(features // (2 * HDIM)):
        query = packed_ref[:, pl.ds(pair * 2 * HDIM, 2 * HDIM)]
        keys = packed_ref[:, pl.ds(features + pair * 2 * HDIM, 2 * HDIM)]
        values = packed_ref[:, pl.ds(2 * features + pair * 2 * HDIM, 2 * HDIM)]
        blank = jnp.zeros_like(query)
        results = []
        for query_head in (jnp.where(lower, query, blank), jnp.where(lower, blank, query)):
            probs = head_probs(query_head, keys, valid).astype(jnp.bfloat16)
            results.append(contract(probs, values, 1, 0))
        mixed_ref[:, pl.ds(pair * 2 * HDIM, 2 * HDIM)] = jnp.where(
            lower, results[0], results[1]
        ).astype(jnp.bfloat16)
    send(mixed_ref)
    stream = stream + contract(mixed_ref[...], full_ref[:, pl.ds(3 * features, features)], 1, 0)
    middle_ref[...] = stream
    send(middle_ref)
    normal, _ = layer_norm_parts(stream)
    second_ref[...] = (normal * norm_ref[1:2] + norm_ref[3:4]).astype(jnp.bfloat16)


def attention_backward_kernel(rows, place_ref, *refs):
    (
        full_ref,
        norm_ref,
        start_ref,
        middle_ref,
        first_ref,
        packed_ref,
        mixed_ref,
        grad_ref,
        router_ref,
    ) = refs[:9]
    part_refs = refs[9:-5]
    result_ref, branch_ref, blocks_ref, gpacked_ref, gmixed_ref = refs[-5:]
    features = start_ref.shape[1]
    padded = start_ref.shape[0]
    upstream = part_refs[0][...].astype(jnp.float32)
    for part_ref in part_refs[1:]:
        upstream = upstream + part_ref[...].astype(jnp.float32)
    normal, inverse = layer_norm_parts(middle_ref[...])
    gain_two = jnp.sum(upstream * normal, axis=0, keepdims=True)
    shift_two = jnp.sum(upstream, axis=0, keepdims=True)
    grad_middle = grad_ref[...].astype(jnp.float32) + layer_norm_pull(
        upstream, normal, inverse, norm_ref[1:2]
    )
    grad_attn = grad_middle.astype(jnp.bfloat16)
    gmixed_ref[...] = contract(
        grad_attn, full_ref[:, pl.ds(3 * features, features)], 1, 1
    ).astype(jnp.bfloat16)
    valid = lax.broadcasted_iota(jnp.int32, (padded, padded), 1) < SEQ
    lower = lax.broadcasted_iota(jnp.int32, (padded, 2 * HDIM), 1) < HDIM
    scale = HDIM ** (-0.5)
    for pair in range(features // (2 * HDIM)):
        spans = [pl.ds(part * features + pair * 2 * HDIM, 2 * HDIM) for part in range(3)]
        query, keys, values = [packed_ref[:, span] for span in spans]
        gmixed = gmixed_ref[:, spans[0]]
        blank = jnp.zeros_like(query)
        found = []
        for side in range(2):
            keep = lower if side == 0 else jnp.logical_not(lower)
            probs = head_probs(jnp.where(keep, query, blank), keys, valid)
            grad_probs = contract(jnp.where(keep, gmixed, blank), values, 1, 1)
            grad_values = contract(probs.astype(jnp.bfloat16), gmixed, 0, 0)
            grad_scores = (
                probs * (grad_probs - jnp.sum(probs * grad_probs, axis=1, keepdims=True))
            ).astype(jnp.bfloat16)
            grad_query = contract(grad_scores, keys, 1, 0) * scale
            grad_keys = contract(grad_scores, query, 0, 0) * scale
            found.append((grad_query, grad_keys, grad_values))
        for part in range(3):
            gpacked_ref[:, spans[part]] = jnp.where(lower, found[0][part], found[1][part]).astype(
                jnp.bfloat16
            )
    upstream = contract(gpacked_ref[...], full_ref[:, pl.ds(0, 3 * features)], 1, 1)
    normal, inverse = layer_norm_parts(start_ref[...])
    gain_one = jnp.sum(upstream * normal, axis=0, keepdims=True)
    shift_one = jnp.sum(upstream, axis=0, keepdims=True)
    result = grad_middle + layer_norm_pull(upstream, normal, inverse, norm_ref[0:1])
    result_ref[...] = result
    branch_ref[...] = result.astype(jnp.bfloat16)
    half = features // 2
    strip = features // rows
    extra = jnp.concatenate(
        [
            router_ref[...],
            gain_one,
            gain_two,
            shift_one,
            shift_two,
            jnp.zeros((blocks_ref.shape[2] - 4 * strip - router_ref.shape[0] - 4, features), jnp.float32),
        ],
        axis=0,
    ).astype(jnp.bfloat16)
    grad_proj = contract(mixed_ref[...], grad_attn, 0, 0).astype(jnp.bfloat16)
    for offset in range(rows):
        for side in range(2):
            columns = slice(side * half, (side + 1) * half)
            blocks_ref[side, offset, pl.ds(3 * strip, strip), :] = grad_proj[
                offset * strip : (offset + 1) * strip, columns
            ]
            blocks_ref[side, offset, pl.ds(4 * strip, extra.shape[0]), :] = extra[:, columns]
    for part in range(3):
        grad_part = contract(
            gpacked_ref[:, pl.ds(part * features, features)], first_ref[...], 0, 0
        ).astype(jnp.bfloat16)
        for offset in range(rows):
            for side in range(2):
                blocks_ref[side, offset, pl.ds(part * strip, strip), :] = grad_part[
                    offset * strip : (offset + 1) * strip, side * half : (side + 1) * half
                ]


def dispatch_kernel(room, codes_ref, *refs):
    groups = codes_ref.shape[1]
    block_refs, out_refs = refs[:-groups], refs[-groups:]
    padded = block_refs[0].shape[0]
    rows_of = lax.broadcasted_iota(jnp.int32, (room, padded), 0)
    for group in range(groups):
        total = jnp.zeros((room, block_refs[0].shape[1]), jnp.float32)
        for image, block_ref in enumerate(block_refs):
            picks = (codes_ref[image, group : group + 1, :] == rows_of).astype(jnp.float32)
            total = total + contract(picks.astype(jnp.bfloat16), block_ref[...], 1, 0)
        out_refs[group][...] = total.astype(jnp.bfloat16)


def combine_kernel(rows, codes_ref, *refs):
    slot_refs, out_refs = refs[: codes_ref.shape[1]], refs[codes_ref.shape[1] :]
    room = slot_refs[0].shape[0]
    padded = out_refs[0].shape[0]
    lanes = lax.broadcasted_iota(jnp.int32, (padded, room), 1)
    for image in range(rows):
        total = jnp.zeros(out_refs[0].shape, jnp.float32)
        for source, slot_ref in enumerate(slot_refs):
            codes = codes_ref[pl.ds(image * padded, padded), source : source + 1]
            picks = (codes == lanes).astype(jnp.float32)
            total = total + contract(picks.astype(jnp.bfloat16), slot_ref[...], 1, 0)
        out_refs[image][...] = total.astype(jnp.bfloat16)


def expert_router(place_ref, buffer, wrouter):
    router = softmax_rows(contract(buffer, wrouter, 1, 1))
    chosen = lax.broadcasted_iota(jnp.int32, router.shape, 1) == place_ref[3]
    gate = jnp.sum(jnp.where(chosen, router, 0.0), axis=1, keepdims=True)
    return (router, chosen, gate)


def expert_forward_kernel(groups, place_ref, wrouter_ref, win_ref, wout_ref, *refs):
    buffer = jnp.concatenate([ref[...] for ref in refs[:groups]], axis=0)
    room = refs[0].shape[0]
    half = buffer.shape[1] // 2
    _, _, gate = expert_router(place_ref, buffer, wrouter_ref[...])
    sums = [jnp.zeros((buffer.shape[0], half), jnp.float32) for _ in range(2)]
    for quarter in range(win_ref.shape[0] // 2):
        hidden = contract(buffer[:, :half], win_ref[2 * quarter], 1, 0) + contract(
            buffer[:, half:], win_ref[2 * quarter + 1], 1, 0
        )
        active = gelu_parts(hidden)[0].astype(jnp.bfloat16)
        for side in range(2):
            sums[side] = sums[side] + contract(active, wout_ref[2 * quarter + side], 1, 0)
    for group in range(groups):
        span = slice(group * room, (group + 1) * room)
        for side in range(2):
            refs[groups + group][:, pl.ds(side * half, half)] = (
                gate[span] * sums[side][span]
            ).astype(jnp.bfloat16)


def expert_full_kernel(groups, with_output, place_ref, wrouter_ref, win_ref, wout_ref, *refs):
    buffer = jnp.concatenate([ref[...] for ref in refs[:groups]], axis=0)
    grads = jnp.concatenate([ref[...] for ref in refs[groups : 2 * groups]], axis=0)
    back_refs = refs[2 * groups : 3 * groups]
    out_refs = refs[3 * groups : -3]
    gin_ref, gout_ref, grouter_ref = refs[-3:]
    room = refs[0].shape[0]
    half = buffer.shape[1] // 2
    router, chosen, gate = expert_router(place_ref, buffer, wrouter_ref[...])
    grad_slot = (gate * grads.astype(jnp.float32)).astype(jnp.bfloat16)
    flipped = buffer.T
    sums = [jnp.zeros((buffer.shape[0], half), jnp.float32) for _ in range(2)]
    backs = [jnp.zeros((buffer.shape[0], half), jnp.float32) for _ in range(2)]
    grad_gate = jnp.zeros((buffer.shape[0], 1), jnp.float32)
    for quarter in range(win_ref.shape[0] // 2):
        hidden = contract(buffer[:, :half], win_ref[2 * quarter], 1, 0) + contract(
            buffer[:, half:], win_ref[2 * quarter + 1], 1, 0
        )
        value, slope = gelu_parts(hidden)
        active = value.astype(jnp.bfloat16)
        if with_output:
            for side in range(2):
                sums[side] = sums[side] + contract(active, wout_ref[2 * quarter + side], 1, 0)
        pulled = contract(grads[:, :half], wout_ref[2 * quarter], 1, 1) + contract(
            grads[:, half:], wout_ref[2 * quarter + 1], 1, 1
        )
        grad_gate = grad_gate + jnp.sum(
            pulled * active.astype(jnp.float32), axis=1, keepdims=True
        )
        grad_hidden = (gate * pulled * slope).astype(jnp.bfloat16)
        turned = active.T
        for side in range(2):
            block = 2 * quarter + side
            span = slice(side * half, (side + 1) * half)
            backs[side] = backs[side] + contract(grad_hidden, win_ref[block], 1, 1)
            gin_ref[block] = contract(flipped[span], grad_hidden, 1, 0).astype(jnp.bfloat16)
            gout_ref[block] = contract(turned, grad_slot[:, span], 1, 0).astype(jnp.bfloat16)
    grad_logits = (
        router * (jnp.where(chosen, grad_gate, 0.0) - gate * grad_gate)
    ).astype(jnp.bfloat16)
    grouter_ref[...] = contract(grad_logits, buffer, 0, 0)
    router_back = contract(grad_logits, wrouter_ref[...], 1, 0)
    for group in range(groups):
        span = slice(group * room, (group + 1) * room)
        for side in range(2):
            columns = slice(side * half, (side + 1) * half)
            back_refs[group][:, columns] = (
                backs[side][span] + router_back[span, columns]
            ).astype(jnp.bfloat16)
            if with_output:
                out_refs[group][:, columns] = (gate[span] * sums[side][span]).astype(jnp.bfloat16)


SMALL = pl.BlockSpec(memory_space=pltpu.SMEM)
LOCAL = pl.BlockSpec(memory_space=pltpu.VMEM)
FAR = pl.BlockSpec(memory_space=pltpu.HBM)


def widen_kernel(narrow_ref, *refs):
    refs[-1][0, 0] = narrow_ref[0].astype(jnp.float32)


def widen_grads(layer, layer_count, narrow, previous):
    members, *block = narrow.shape
    anywhere = pl.BlockSpec(memory_space=pl.ANY)
    return pl.pallas_call(
        widen_kernel,
        name="widen",
        grid=(members,),
        in_specs=[pl.BlockSpec((1, *block), lambda step: (step, 0, 0))]
        + [anywhere] * len(previous),
        out_specs=pl.BlockSpec((1, 1, *block), lambda step: (layer, step, 0, 0)),
        out_shape=jax.ShapeDtypeStruct((layer_count, members, *block), jnp.float32),
        input_output_aliases={1: 0} if previous else {},
        compiler_params=pltpu.CompilerParams(vmem_limit_bytes=4 * 1024 * 1024),
    )(narrow, *previous)


class Staged:
    def __init__(self, ref, move=None):
        self.ref, self.move = ref, move
        self.shape, self.dtype = ref.shape, ref.dtype

    def wait(self):
        if self.move is not None:
            self.move.wait()
            self.move = None

    def __getitem__(self, index):
        self.wait()
        return self.ref[index]


class Sent:
    def __init__(self, ref, move):
        self.ref, self.move, self.moving = ref, move, False
        self.shape, self.dtype = ref.shape, ref.dtype

    def __getitem__(self, index):
        return self.ref[index]

    def __setitem__(self, index, values):
        self.ref[index] = values

    def send(self):
        if not self.moving:
            self.move.start()
            self.moving = True


def send(ref):
    if isinstance(ref, Sent):
        ref.send()


def staged_body(body, fixed_count, staged, far, *refs):
    fixed, refs = refs[:fixed_count], refs[fixed_count:]
    sources, refs = list(refs[: len(staged)]), refs[len(staged) :]
    targets, refs = list(refs[: len(far)]), refs[len(far) :]
    copies, refs = list(refs[: sum(staged)]), refs[sum(staged) :]
    made, refs = list(refs[: sum(far)]), refs[sum(far) :]
    marks, scratch = refs[0], refs[1:]
    for place, moved in enumerate(staged):
        if moved:
            copy = copies.pop(0)
            move = pltpu.make_async_copy(sources[place], copy, marks.at[place])
            move.start()
            sources[place] = Staged(copy, move)
    for place, apart in enumerate(far):
        if apart:
            source = made.pop(0)
            move = pltpu.make_async_copy(source, targets[place], marks.at[len(staged) + place])
            targets[place] = Sent(source, move)
    body(*fixed, *sources, *targets, *scratch)
    for source in sources:
        if isinstance(source, Staged):
            source.wait()
    for target in targets:
        send(target)
    for target in targets:
        if isinstance(target, Sent):
            target.move.wait()


def run_kernel(
    title, body, place, operands, results, work, scratch=(), room=16, near=(), far=()
):
    fixed = [] if place is None else [place]
    staged = [place not in near for place in range(len(operands))]
    arguments = fixed + [
        pltpu.with_memory_space_constraint(piece, pltpu.HBM) if moved else piece
        for moved, piece in zip(staged, operands)
    ]
    apart = [place in far for place in range(len(results))]
    return pl.pallas_call(
        functools.partial(staged_body, body, len(fixed), staged, apart),
        name=title,
        in_specs=[SMALL] * len(fixed) + [FAR if moved else LOCAL for moved in staged],
        out_specs=[FAR if away else LOCAL for away in apart],
        out_shape=[
            pltpu.HBM(shape, kind) if away else jax.ShapeDtypeStruct(shape, kind)
            for away, (shape, kind) in zip(apart, results)
        ],
        scratch_shapes=[
            pltpu.VMEM(piece.shape, piece.dtype) for moved, piece in zip(staged, operands) if moved
        ]
        + [pltpu.VMEM(shape, kind) for away, (shape, kind) in zip(apart, results) if away]
        + [pltpu.SemaphoreType.DMA((len(operands) + len(results),))]
        + list(scratch),
        compiler_params=pltpu.CompilerParams(vmem_limit_bytes=room * 1024 * 1024),
        cost_estimate=pl.CostEstimate(
            flops=work,
            bytes_accessed=sum(piece.size * piece.dtype.itemsize for piece in arguments),
            transcendentals=0,
        ),
    )(*arguments)


def after(values, *earlier):
    return lax.optimization_barrier((values, *earlier))[0]


def gather_group(values):
    near = [values]
    for offset in range(1, lax.axis_size("row")):
        near.append(exchange(values, "row", offset))
    return near + [exchange(piece, "col", 1) for piece in near]


def scatter_pieces(pieces, axis):
    return [
        piece if offset == 0 else exchange(piece, axis, offset)
        for offset, piece in enumerate(pieces)
    ]


def add_pieces(pieces):
    total = pieces[0].astype(jnp.float32)
    for piece in pieces[1:]:
        total = total + piece.astype(jnp.float32)
    return total


def sum_chip(blocks, at_col):
    mine = lax.dynamic_index_in_dim(blocks, at_col, 0, keepdims=False)
    other = exchange(lax.dynamic_index_in_dim(blocks, 1 - at_col, 0, keepdims=False), "col", 1)
    return add_pieces([mine, other]).astype(blocks.dtype)


def sum_groups(plane):
    groups, at_dp = lax.axis_size("dp"), lax.axis_index("dp")
    part = plane.shape[0] // groups
    pieces = [
        lax.dynamic_slice_in_dim(plane, (at_dp ^ offset) * part, part, 0)
        for offset in range(groups)
    ]
    owned = add_pieces(scatter_pieces(pieces, "dp")).astype(plane.dtype)
    result = jnp.zeros(plane.shape, jnp.float32)
    for offset in range(groups):
        piece = owned if offset == 0 else exchange(owned, "dp", offset)
        result = lax.dynamic_update_slice_in_dim(
            result, piece.astype(jnp.float32), (at_dp ^ offset) * part, 0
        )
    return result


def group_device(
    tokens,
    norm_gain,
    norm_shift,
    w_qkv,
    w_proj,
    w_router,
    w_in,
    w_out,
    expert_ids,
    slot_ids,
    cotangent,
):
    low = jnp.bfloat16
    groups, rows = lax.axis_size("dp"), lax.axis_size("row")
    members = 2 * rows
    at_dp, at_row, at_col = [lax.axis_index(name) for name in ("dp", "row", "col")]
    layer_count = w_qkv.shape[0]
    expert_count = w_in.shape[1]
    half = tokens.shape[1]
    features = 2 * half
    strip = features // rows
    padded = -(-SEQ // 16) * 16
    owner = at_dp * members + at_row * 2 + at_col
    place = jnp.stack([at_dp, at_row, at_col, owner]).astype(jnp.int32)

    def join(mine, other):
        return jnp.where(
            at_col == 0,
            jnp.concatenate([mine, other], axis=-1),
            jnp.concatenate([other, mine], axis=-1),
        )

    small = jnp.concatenate(
        [
            jnp.concatenate([norm_gain, norm_shift], axis=1).reshape(-1, half),
            w_router.transpose(0, 2, 1).reshape(-1, half).astype(jnp.float32),
        ],
        axis=0,
    )
    small = join(small, exchange(small, "col", 1))
    norms = small[: 4 * layer_count].reshape(layer_count, 4, features)
    routers = small[4 * layer_count :].reshape(layer_count, expert_count, features).astype(low)
    both = jnp.stack([tokens, cotangent]).reshape(2, 2, SEQ, half)
    mine = lax.dynamic_index_in_dim(both, at_col, 1, keepdims=False)
    other = exchange(lax.dynamic_index_in_dim(both, 1 - at_col, 1, keepdims=False), "col", 1)
    both = jnp.pad(join(mine, other), ((0, 0), (0, padded - SEQ), (0, 0)))

    def fetch_attention(layer, *earlier):
        block = jnp.concatenate(
            [
                w_qkv[layer].reshape(half, -1),
                jnp.concatenate(
                    [
                        w_proj[layer][:, piece * strip : (piece + 1) * strip]
                        for piece in range(half // strip)
                    ],
                    axis=0,
                ),
            ],
            axis=1,
        )
        return gather_group(after(block, *earlier) if earlier else block)

    def own_experts(layer, source):
        own = lax.dynamic_slice(
            source, (layer, at_dp * members, 0, 0), (1, members, *source.shape[2:])
        )
        return own[0]

    def fetch_weights(own, *earlier):
        return lax.all_to_all(
            after(own, *earlier), ("row", "col"), split_axis=0, concat_axis=0, tiled=True
        )

    capacity = 2 * ((5 * members * SEQ + 4 * expert_count - 1) // (4 * expert_count))
    room = -(-capacity // 16) * 16
    images = jnp.stack(
        [(at_row ^ offset) * 2 + (at_col ^ side) for side in range(2) for offset in range(rows)]
    )
    named = jnp.stack(
        [
            (at_dp ^ offset) * members + at_row * 2 + (at_col ^ side)
            for side in range(2)
            for offset in range(groups)
        ]
    )
    chosen = jnp.take(expert_ids.reshape(layer_count, members, SEQ, -1), images, axis=1)
    slots = jnp.take(slot_ids.reshape(layer_count, members, SEQ, -1), images, axis=1)
    codes = jnp.max(
        jnp.where(chosen[..., None] == named, slots[..., None], -1), axis=3
    )
    codes = jnp.pad(codes, ((0, 0), (0, 0), (0, padded - SEQ), (0, 0)), constant_values=-1)
    send_codes = codes[..., :groups].transpose(0, 1, 3, 2)
    back_codes = codes[:, :rows].reshape(layer_count, rows * padded, 2 * groups)

    token_block = ((padded, features), low)
    slot_block = ((room, features), low)

    def after_all(pieces, *earlier):
        return [after(piece, *earlier) for piece in pieces]

    def dispatch(layer, images):
        return run_kernel(
            "dispatch",
            functools.partial(dispatch_kernel, room),
            None,
            [send_codes[layer]] + images,
            [slot_block] * groups,
            2 * members * padded * groups * room * features,
            near=range(1, 1 + len(images)),
        )

    def bring_back(blocks, *earlier):
        blocks = after_all(scatter_pieces(blocks, "dp"), *earlier)
        return blocks + [exchange(piece, "col", 1) for piece in blocks]

    def combine(layer, blocks):
        return run_kernel(
            "combine",
            functools.partial(combine_kernel, rows),
            None,
            [back_codes[layer]] + blocks,
            [token_block] * rows,
            4 * rows * padded * groups * room * features,
        )

    def split(values):
        pieces = values[:SEQ].reshape(SEQ, 2, half)
        mine = lax.dynamic_index_in_dim(pieces, at_col, 1, keepdims=False)
        other = exchange(lax.dynamic_index_in_dim(pieces, 1 - at_col, 1, keepdims=False), "col", 1)
        return jnp.where(
            at_col == 0,
            jnp.concatenate([mine, other], axis=0),
            jnp.concatenate([other, mine], axis=0),
        )

    work = 4 * groups * room * members * half * w_in.shape[3]
    stream, parts = both[0], []
    kept, buffers, weights = [], [], []
    attention_blocks = fetch_attention(0)
    ready = attention_blocks[1:rows]
    for layer in range(layer_count):
        last = layer == layer_count - 1
        weight_in = fetch_weights(own_experts(layer, w_in), *ready)
        own_out = own_experts(layer, w_out)
        upstream = []
        if last:
            upstream = gather_group(after(both[1], *parts[1:]))
        saved = run_kernel(
            "attention_forward",
            functools.partial(attention_forward_kernel, rows),
            place,
            attention_blocks + [norms[layer], stream] + parts,
            [
                ((padded, features), jnp.float32),
                ((padded, features), jnp.float32),
                token_block,
                ((padded, 3 * features), low),
                token_block,
                token_block,
                ((features, 4 * features), low),
            ],
            16 * padded * features * features,
            far=(0, 1, 2, 3, 4, 6),
        )
        kept.append(saved)
        stream = saved[1]
        images = gather_group(saved[5])
        weight_out = fetch_weights(own_out, *images[1:rows], *upstream[1:rows])
        weights.append([weight_in, weight_out])
        if last:
            sent = dispatch(layer, upstream)
            branches = scatter_pieces(sent, "dp")
            images = after_all(images, sent[0])
        buffers.append(scatter_pieces(dispatch(layer, images), "dp"))
        if not last:
            result = run_kernel(
                "expert_forward",
                functools.partial(expert_forward_kernel, groups),
                place,
                [routers[layer]] + weights[layer] + buffers[layer],
                [slot_block] * groups,
                work,
            )
            ready = [result[0]]
            attention_blocks = fetch_attention(layer + 1, result[0])
            parts = scatter_pieces(combine(layer, bring_back(result)), "row")
    grad = both[1]
    shared = [None] * layer_count
    grad_in, grad_out = [], []
    for layer in reversed(range(layer_count)):
        last = layer == layer_count - 1
        found = run_kernel(
            "expert_full",
            functools.partial(expert_full_kernel, groups, last),
            place,
            [routers[layer]] + weights[layer] + buffers[layer] + branches,
            [slot_block] * (2 * groups if last else groups)
            + [
                (weights[layer][0].shape, low),
                (weights[layer][1].shape, low),
                ((expert_count, features), jnp.float32),
            ],
            3 * work,
            room=24,
        )
        if last:
            moved_in = fetch_weights(found[-3])
            blocks = bring_back(list(found[:groups]))
        else:
            moved_in = fetch_weights(found[-3], moved_out)
            moved_out = after(moved_out, found[0])
            grad_out = [widen_grads(layer + 1, layer_count, moved_out, grad_out)]
            blocks = bring_back(list(found[:groups]), *grad_out)
        pieces = combine(layer, blocks)
        if last:
            outputs = bring_back(after_all(list(found[groups : 2 * groups]), pieces[0]))
        grad_parts = scatter_pieces(after_all(pieces, moved_in), "row")
        if last:
            grad_parts[0] = after(grad_parts[0], *outputs[1:groups])
        else:
            outputs = scatter_pieces(after_all(outputs, *grad_parts[1:]), "row")
            arrived = scatter_pieces(after_all(chip, *grad_parts[1:]), "row")
            for part in outputs:
                stream = stream + part.astype(jnp.float32)
        saved = kept[layer]
        height = -(-(4 * strip + expert_count + 4) // (16 * groups)) * (16 * groups)
        grad, branch, blocks = run_kernel(
            "attention_backward",
            functools.partial(attention_backward_kernel, rows),
            place,
            [saved[6], norms[layer], saved[0], saved[1], saved[2], saved[3], saved[4], grad]
            + [found[-1]]
            + grad_parts,
            [
                ((padded, features), jnp.float32),
                token_block,
                ((2, rows, height, half), low),
            ],
            32 * padded * features * features,
            [pltpu.VMEM((padded, 3 * features), low), pltpu.VMEM((padded, features), low)],
        )
        chip = list(sum_chip(blocks, at_col))
        if layer > 0:
            images = gather_group(branch)
            moved_out = fetch_weights(found[-2], *images[1:rows])
            grad_in = [widen_grads(layer, layer_count, moved_in, grad_in)]
            branches = scatter_pieces(dispatch(layer - 1, images), "dp")
            if last:
                outputs = combine(layer, outputs)
            branches = after_all(branches, *grad_in, *outputs)
        else:
            earlier = add_pieces(arrived).astype(low)
            shared[layer + 1] = sum_groups(earlier)
            arrived = scatter_pieces(after_all(chip, earlier, *outputs[1:]), "row")
            moved_out = fetch_weights(found[-2], *arrived[1:])
            grad_in = [widen_grads(layer, layer_count, after(moved_in, chip[0]), grad_in)]
            output = split(stream.astype(low))
            arrived = after_all(arrived, *grad_in, *shared[1:], output)
            grad_out = [widen_grads(layer, layer_count, moved_out, grad_out)]
            shared[layer] = sum_groups(add_pieces(arrived).astype(low))
    grad_input = split(grad)
    shared = jnp.stack(shared)
    grad_qkv = (
        shared[:, : 3 * strip].reshape(layer_count, 3, strip, half).transpose(0, 3, 1, 2)
    )
    grad_proj = shared[:, 3 * strip : 4 * strip]
    grad_router = shared[:, 4 * strip : 4 * strip + expert_count].transpose(0, 2, 1)
    tail = shared[:, 4 * strip + expert_count : 4 * strip + expert_count + 4]
    return (
        output,
        grad_input,
        grad_qkv,
        grad_proj,
        grad_router,
        grad_in[0],
        grad_out[0],
        tail[:, :2],
        tail[:, 2:],
    )


def fits_groups(mesh, tokens, w_in):
    groups, rows, sides = mesh.shape["dp"], mesh.shape["row"], mesh.shape["col"]
    powers = all(size & (size - 1) == 0 for size in (groups, rows))
    return (
        sides == 2
        and powers
        and tokens.shape[0] == groups * rows * sides * SEQ
        and w_in.shape[1] == groups * rows * sides
    )


def solution(mesh):
    in_specs = (
        P(("dp", "row"), "col"),
        P(None, None, "col"),
        P(None, None, "col"),
        P(None, "col", None, "row"),
        P(None, "row", "col"),
        P(None, "col", None),
        P(None, None, "col", "row"),
        P(None, None, "row", "col"),
        P(None, "dp", None),
        P(None, "dp", None),
        P(("dp", "row"), "col"),
    )
    out_specs = (
        P(("dp", "row"), "col"),
        P(("dp", "row"), "col"),
        P(None, "col", None, "row"),
        P(None, "row", "col"),
        P(None, "col", None),
        P(None, "dp", "col", "row"),
        P(None, "dp", "row", "col"),
        P(None, None, "col"),
        P(None, None, "col"),
    )

    def program(*arguments):
        fits = fits_groups(mesh, arguments[0], arguments[6])
        return jax.shard_map(
            group_device if fits else per_device,
            mesh=mesh,
            in_specs=in_specs,
            out_specs=out_specs,
            check_vma=False,
        )(*arguments)

    return program
```

```python
import functools
import math

import jax
import jax.numpy as jnp
from jax import lax
from jax.experimental import pallas as pl
from jax.experimental.pallas import tpu as pltpu
from jax.sharding import PartitionSpec as P

HDIM = 64
SEQ = 197


EPSILON = 1e-06


def gather_rows(values):
    return lax.all_gather(values, "row", axis=0, tiled=True)


def sum_rows(values):
    return lax.psum_scatter(values, "row", scatter_dimension=0, tiled=True)


def gather_halves(values):
    return lax.all_gather(values, "col", axis=0, tiled=True)


def sum_halves(values):
    return lax.psum_scatter(values, "col", scatter_dimension=0, tiled=True)


def row_totals(first, second):
    return lax.psum((first, second), "col")


def softmax_rows(values):
    shifted = jnp.exp(values - jnp.max(values, axis=-1, keepdims=True))
    return shifted / jnp.sum(shifted, axis=-1, keepdims=True)


def norm_forward(stream, gain_row, shift_row):
    feature_count = stream.shape[1] * lax.axis_size("col")
    total, squares = row_totals(jnp.sum(stream, axis=1), jnp.sum(stream * stream, axis=1))
    center = total / feature_count
    inverse = lax.rsqrt(squares / feature_count - center * center + EPSILON)
    normal = (stream - center[:, None]) * inverse[:, None]
    return (normal * gain_row + shift_row, normal, inverse)


def norm_backward(upstream, normal, inverse, gain_row):
    feature_count = upstream.shape[1] * lax.axis_size("col")
    scaled = upstream * gain_row
    first, second = row_totals(jnp.sum(scaled, axis=1), jnp.sum(scaled * normal, axis=1))
    result_grad = inverse[:, None] * (
        scaled - first[:, None] / feature_count - normal * (second[:, None] / feature_count)
    )
    return (result_grad, jnp.sum(upstream * normal, axis=0), jnp.sum(upstream, axis=0))


def split_heads(packed):
    row_count = packed.shape[0]
    heads_here = packed.shape[1] // (3 * HDIM)
    parts = packed.reshape(row_count // SEQ, SEQ, 3, heads_here, HDIM)
    return (parts[:, :, 0], parts[:, :, 1], parts[:, :, 2])


def attend_forward(packed):
    query_part, key_part, value_part = split_heads(packed)
    scores = jnp.einsum(
        "bqhd,bkhd->bhqk", query_part, key_part, preferred_element_type=jnp.float32
    ) * HDIM ** (-0.5)
    highest = jnp.max(scores, axis=-1, keepdims=True)
    powers = jnp.exp(scores - highest)
    totals = jnp.sum(powers, axis=-1, keepdims=True)
    weights = (powers / totals).astype(jnp.bfloat16)
    mixed_heads = jnp.einsum(
        "bhqk,bkhd->bqhd", weights, value_part, preferred_element_type=jnp.float32
    )
    return (
        mixed_heads.reshape(packed.shape[0], -1).astype(jnp.bfloat16),
        highest + jnp.log(totals),
    )


def attend_backward(packed, logsum, grad_mixed):
    query_part, key_part, value_part = split_heads(packed)
    scale = HDIM ** (-0.5)
    scores = (
        jnp.einsum("bqhd,bkhd->bhqk", query_part, key_part, preferred_element_type=jnp.float32)
        * scale
    )
    probs_full = jnp.exp(scores - logsum)
    upstream = grad_mixed.reshape(query_part.shape)
    grad_probs = jnp.einsum(
        "bqhd,bkhd->bhqk", upstream, value_part, preferred_element_type=jnp.float32
    )
    grad_values = jnp.einsum(
        "bhqk,bqhd->bkhd",
        probs_full.astype(jnp.bfloat16),
        upstream,
        preferred_element_type=jnp.float32,
    )
    grad_scores = (
        probs_full * (grad_probs - jnp.sum(probs_full * grad_probs, axis=-1, keepdims=True))
    ).astype(jnp.bfloat16)
    grad_query = (
        jnp.einsum("bhqk,bkhd->bqhd", grad_scores, key_part, preferred_element_type=jnp.float32)
        * scale
    )
    grad_keys = (
        jnp.einsum("bhqk,bqhd->bkhd", grad_scores, query_part, preferred_element_type=jnp.float32)
        * scale
    )
    stacked = jnp.stack([grad_query, grad_keys, grad_values], axis=2)
    return stacked.reshape(packed.shape[0], -1).astype(jnp.bfloat16)


def attention_forward(stream, gain_row, shift_row, weight_qkv, weight_proj):
    normed, normal, inverse = norm_forward(stream, gain_row, shift_row)
    normed_all = gather_rows(normed.astype(jnp.bfloat16))
    packed = sum_halves(jnp.dot(normed_all, weight_qkv, preferred_element_type=jnp.float32)).astype(
        jnp.bfloat16
    )
    mixed_heads, logsum = attend_forward(packed)
    mixed_all = gather_halves(mixed_heads)
    branch = sum_rows(jnp.dot(mixed_all, weight_proj, preferred_element_type=jnp.float32))
    saved = {
        "normal": normal,
        "inverse": inverse,
        "normed_all": normed_all,
        "packed": packed,
        "logsum": logsum,
        "mixed_all": mixed_all,
    }
    return (stream + branch, saved)


def attention_backward(upstream, saved, weight_qkv, weight_proj):
    grad_all = gather_rows(upstream.astype(jnp.bfloat16))
    grad_mixed = sum_halves(
        jnp.einsum("te,de->td", grad_all, weight_proj, preferred_element_type=jnp.float32)
    ).astype(jnp.bfloat16)
    grad_w_proj = jnp.einsum(
        "td,te->de", saved["mixed_all"], grad_all, preferred_element_type=jnp.float32
    )
    grad_packed = attend_backward(saved["packed"], saved["logsum"], grad_mixed)
    grad_packed_all = gather_halves(grad_packed)
    grad_part = jnp.einsum(
        "tf,df->td", grad_packed_all, weight_qkv, preferred_element_type=jnp.float32
    )
    grad_w_qkv = jnp.einsum(
        "td,tf->df", saved["normed_all"], grad_packed_all, preferred_element_type=jnp.float32
    )
    return (sum_rows(grad_part), grad_w_qkv, grad_w_proj)


def second_product(active, buffer_shape, weight_out):
    active_all = gather_halves(active).reshape(buffer_shape[0], buffer_shape[1], -1)
    slot_out = jnp.einsum(
        "ecf,efd->ecd", active_all, weight_out, preferred_element_type=jnp.float32
    )
    return (active_all, slot_out.reshape(-1, slot_out.shape[2]))


def expert_forward(
    stream, gain_row, shift_row, choice_ids, slot_rows, weight_router, weight_in, weight_out
):
    normed, normal, inverse = norm_forward(stream, gain_row, shift_row)
    normed_all = gather_rows(normed.astype(jnp.bfloat16))
    row_count = normed_all.shape[0]
    expert_count = weight_in.shape[0]
    capacity = 2 * ((5 * row_count + 4 * expert_count - 1) // (4 * expert_count))
    logits = lax.psum(jnp.dot(normed_all, weight_router, preferred_element_type=jnp.float32), "col")
    router = softmax_rows(logits)
    onehot = (
        choice_ids[:, :, None] == lax.broadcasted_iota(jnp.int32, (1, 1, expert_count), 2)
    ).astype(jnp.float32)
    gate_values = jnp.sum(onehot * router[:, None, :], axis=2)
    flat_slots = choice_ids * capacity + slot_rows
    owners = jnp.broadcast_to(
        lax.broadcasted_iota(jnp.int32, (row_count, 1), 0), flat_slots.shape
    ).reshape(-1)
    slot_owner = (
        jnp.full((expert_count * capacity,), row_count, jnp.int32)
        .at[flat_slots.reshape(-1)]
        .set(owners)
    )
    slot_assign = (
        jnp.full((expert_count * capacity,), 2 * row_count, jnp.int32)
        .at[flat_slots.reshape(-1)]
        .set(lax.iota(jnp.int32, 2 * row_count))
    )
    padded = jnp.concatenate(
        [normed_all, jnp.zeros((1, normed_all.shape[1]), jnp.bfloat16)], axis=0
    )
    buffer = padded[slot_owner].reshape(expert_count, capacity, -1)
    hidden_part = jnp.einsum("ecd,edf->ecf", buffer, weight_in, preferred_element_type=jnp.float32)
    hidden = sum_halves(hidden_part.reshape(buffer.shape[0] * buffer.shape[1], -1))
    active = jax.nn.gelu(hidden).astype(jnp.bfloat16)
    active_all, slot_out = second_product(active, buffer.shape, weight_out)
    branch_part = jnp.sum(gate_values[:, :, None] * slot_out[flat_slots], axis=1)
    saved = {
        "normal": normal,
        "inverse": inverse,
        "normed_all": normed_all,
        "router": router,
        "onehot": onehot,
        "gate_values": gate_values,
        "flat_slots": flat_slots,
        "slot_owner": slot_owner,
        "slot_assign": slot_assign,
        "buffer": buffer,
        "hidden": hidden,
        "active": active,
    }
    saved["active_all"] = active_all
    saved["slot_out"] = slot_out
    return (stream + sum_rows(branch_part), saved)


def expert_backward(upstream, saved, weight_router, weight_in, weight_out):
    buffer = saved["buffer"]
    expert_count = weight_in.shape[0]
    capacity = saved["slot_owner"].shape[0] // expert_count
    active_all = saved["active_all"]
    slot_out = saved["slot_out"]
    flat_slots = saved["flat_slots"]
    grad_all = gather_rows(upstream.astype(jnp.bfloat16))
    gate_part = jnp.sum(grad_all.astype(jnp.float32)[:, None, :] * slot_out[flat_slots], axis=2)
    grad_gates = lax.psum(gate_part, ("row", "col"))
    padded_grad = jnp.concatenate(
        [grad_all, jnp.zeros((1, grad_all.shape[1]), jnp.bfloat16)], axis=0
    )
    slot_gate = jnp.concatenate([saved["gate_values"].reshape(-1), jnp.zeros((1,), jnp.float32)])[
        saved["slot_assign"]
    ]
    grad_slot = (
        (slot_gate[:, None] * padded_grad[saved["slot_owner"]])
        .astype(jnp.bfloat16)
        .reshape(expert_count, capacity, -1)
    )
    grad_active_part = jnp.einsum(
        "ecd,efd->ecf", grad_slot, weight_out, preferred_element_type=jnp.float32
    )
    grad_w_out = jnp.einsum(
        "ecf,ecd->efd", active_all, grad_slot, preferred_element_type=jnp.float32
    )
    grad_active = sum_halves(grad_active_part.reshape(buffer.shape[0] * buffer.shape[1], -1))
    gelu_pull = jax.vjp(jax.nn.gelu, saved["hidden"])[1]
    grad_hidden = gelu_pull(grad_active)[0].astype(jnp.bfloat16)
    grad_hidden_all = gather_halves(grad_hidden).reshape(buffer.shape[0], buffer.shape[1], -1)
    grad_buffer = jnp.einsum(
        "ecf,edf->ecd", grad_hidden_all, weight_in, preferred_element_type=jnp.float32
    )
    grad_w_in = jnp.einsum(
        "ecd,ecf->edf", buffer, grad_hidden_all, preferred_element_type=jnp.float32
    )
    grad_buffer = grad_buffer.reshape(expert_count * capacity, -1)
    router = saved["router"]
    grad_probs = jnp.sum(grad_gates[:, :, None] * saved["onehot"], axis=1)
    grad_logits = (
        router * (grad_probs - jnp.sum(router * grad_probs, axis=1, keepdims=True))
    ).astype(jnp.bfloat16)
    grad_w_router = jnp.einsum(
        "td,te->de", saved["normed_all"], grad_logits, preferred_element_type=jnp.float32
    )
    router_back = jnp.einsum(
        "te,de->td", grad_logits, weight_router, preferred_element_type=jnp.float32
    )
    leading = (lax.axis_index("row") == 0).astype(jnp.float32)
    grad_part = jnp.sum(grad_buffer[flat_slots], axis=1) + leading * router_back
    return (sum_rows(grad_part), grad_w_router, grad_w_in, grad_w_out)


def per_device(
    tokens,
    norm_gain,
    norm_shift,
    w_qkv,
    w_proj,
    w_router,
    w_in,
    w_out,
    expert_ids,
    slot_ids,
    cotangent,
):
    layer_count = w_qkv.shape[0]
    stream = tokens.astype(jnp.float32)
    attention_saved = []
    expert_saved = []
    for layer_index in range(layer_count):
        weight_qkv = w_qkv[layer_index].reshape(w_qkv.shape[1], -1)
        stream, kept_one = attention_forward(
            stream,
            norm_gain[layer_index, 0],
            norm_shift[layer_index, 0],
            weight_qkv,
            w_proj[layer_index],
        )
        stream, kept_two = expert_forward(
            stream,
            norm_gain[layer_index, 1],
            norm_shift[layer_index, 1],
            expert_ids[layer_index],
            slot_ids[layer_index],
            w_router[layer_index],
            w_in[layer_index],
            w_out[layer_index],
        )
        attention_saved.append(kept_one)
        expert_saved.append(kept_two)
    output = stream.astype(jnp.bfloat16)
    grad_stream = cotangent.astype(jnp.float32)
    qkv_grads = [None] * layer_count
    proj_grads = [None] * layer_count
    router_grads = [None] * layer_count
    in_grads = [None] * layer_count
    out_grads = [None] * layer_count
    gain_grads = [None] * layer_count
    shift_grads = [None] * layer_count
    for layer_index in reversed(range(layer_count)):
        weight_qkv = w_qkv[layer_index].reshape(w_qkv.shape[1], -1)
        kept_two = expert_saved[layer_index]
        grad_normed, router_grads[layer_index], grad_w_in, grad_w_out = expert_backward(
            grad_stream, kept_two, w_router[layer_index], w_in[layer_index], w_out[layer_index]
        )
        grad_w_in, grad_w_out = (
            lax.psum_scatter(grad_w_in, "dp", scatter_dimension=0, tiled=True),
            lax.psum_scatter(grad_w_out, "dp", scatter_dimension=0, tiled=True),
        )
        in_grads[layer_index] = grad_w_in
        out_grads[layer_index] = grad_w_out
        grad_inner, gain_two, shift_two = norm_backward(
            grad_normed, kept_two["normal"], kept_two["inverse"], norm_gain[layer_index, 1]
        )
        grad_stream = grad_stream + grad_inner
        kept_one = attention_saved[layer_index]
        grad_normed, grad_w_qkv, proj_grads[layer_index] = attention_backward(
            grad_stream, kept_one, weight_qkv, w_proj[layer_index]
        )
        qkv_grads[layer_index] = grad_w_qkv.reshape(w_qkv.shape[1:])
        grad_inner, gain_one, shift_one = norm_backward(
            grad_normed, kept_one["normal"], kept_one["inverse"], norm_gain[layer_index, 0]
        )
        grad_stream = grad_stream + grad_inner
        gain_grads[layer_index] = jnp.stack([gain_one, gain_two])
        shift_grads[layer_index] = jnp.stack([shift_one, shift_two])
    grad_qkv, grad_proj, grad_router = lax.psum(
        (jnp.stack(qkv_grads), jnp.stack(proj_grads), jnp.stack(router_grads)), "dp"
    )
    grad_gain, grad_shift = lax.psum((jnp.stack(gain_grads), jnp.stack(shift_grads)), ("dp", "row"))
    grad_in = jnp.stack(in_grads)
    grad_out = jnp.stack(out_grads)
    return (
        output,
        grad_stream,
        grad_qkv,
        grad_proj,
        grad_router,
        grad_in,
        grad_out,
        grad_gain,
        grad_shift,
    )


def exchange(values, axis, offset):
    count = lax.axis_size(axis)
    return lax.ppermute(values, axis, [(place, place ^ offset) for place in range(count)])


def contract(left, right, left_dim, right_dim):
    return lax.dot_general(
        left, right, (((left_dim,), (right_dim,)), ((), ())), preferred_element_type=jnp.float32
    )


def layer_norm_parts(values):
    center = jnp.mean(values, axis=1, keepdims=True)
    shifted = values - center
    spread = jnp.mean(shifted * shifted, axis=1, keepdims=True)
    inverse = lax.rsqrt(spread + EPSILON)
    return (shifted * inverse, inverse)


def layer_norm_pull(upstream, normal, inverse, gain_row):
    scaled = upstream * gain_row
    first = jnp.mean(scaled, axis=1, keepdims=True)
    second = jnp.mean(scaled * normal, axis=1, keepdims=True)
    return inverse * (scaled - first - normal * second)


def gelu_parts(values):
    factor = (2.0 / jnp.pi) ** 0.5
    squares = values * values
    curve = jnp.tanh(values * (factor + (factor * 0.044715) * squares))
    half = 0.5 + 0.5 * curve
    slope = half + (0.5 * values) * (1.0 - curve * curve) * (
        factor + (3.0 * factor * 0.044715) * squares
    )
    return (values * half, slope)


def head_probs(query_head, key_pair, valid):
    scores = contract(query_head, key_pair, 1, 1) * HDIM ** (-0.5)
    scores = jnp.where(valid, scores, -1e30)
    powers = jnp.exp(scores - jnp.max(scores, axis=1, keepdims=True))
    return powers / jnp.sum(powers, axis=1, keepdims=True)


def assemble_weights(place_ref, block_refs, full_ref, rows, features):
    half = features // 2
    strip = features // rows
    for position, block_ref in enumerate(block_refs):
        other, offset = divmod(position, rows)
        side = lax.bitwise_xor(place_ref[2], other)
        top = pl.multiple_of(side * half, half)
        for part in range(3):
            full_ref[pl.ds(top, half), pl.ds(part * features + offset * strip, strip)] = block_ref[
                :, pl.ds(part * strip, strip)
            ]
        for piece in range(half // strip):
            left = pl.multiple_of(3 * features + side * half + piece * strip, strip)
            full_ref[pl.ds(offset * strip, strip), pl.ds(left, strip)] = block_ref[
                pl.ds(piece * strip, strip), pl.ds(3 * strip, strip)
            ]


def attention_forward_kernel(rows, place_ref, *refs):
    block_refs = refs[: 2 * rows]
    norm_ref, stream_ref = refs[2 * rows : 2 * rows + 2]
    start_ref, middle_ref, first_ref, packed_ref, mixed_ref, second_ref, full_ref = refs[-7:]
    part_refs = refs[2 * rows + 2 : -7]
    features = stream_ref.shape[1]
    padded = stream_ref.shape[0]
    stream = stream_ref[...].astype(jnp.float32)
    for part_ref in part_refs:
        stream = stream + part_ref[...].astype(jnp.float32)
    start_ref[...] = stream
    send(start_ref)
    assemble_weights(place_ref, block_refs, full_ref, rows, features)
    send(full_ref)
    normal, _ = layer_norm_parts(stream)
    normed = (normal * norm_ref[0:1] + norm_ref[2:3]).astype(jnp.bfloat16)
    first_ref[...] = normed
    send(first_ref)
    for part in range(3):
        columns = pl.ds(part * features, features)
        packed_ref[:, columns] = contract(normed, full_ref[:, columns], 1, 0).astype(jnp.bfloat16)
    send(packed_ref)
    valid = lax.broadcasted_iota(jnp.int32, (padded, padded), 1) < SEQ
    lower = lax.broadcasted_iota(jnp.int32, (padded, 2 * HDIM), 1) < HDIM
    for pair in range(features // (2 * HDIM)):
        query = packed_ref[:, pl.ds(pair * 2 * HDIM, 2 * HDIM)]
        keys = packed_ref[:, pl.ds(features + pair * 2 * HDIM, 2 * HDIM)]
        values = packed_ref[:, pl.ds(2 * features + pair * 2 * HDIM, 2 * HDIM)]
        blank = jnp.zeros_like(query)
        results = []
        for query_head in (jnp.where(lower, query, blank), jnp.where(lower, blank, query)):
            probs = head_probs(query_head, keys, valid).astype(jnp.bfloat16)
            results.append(contract(probs, values, 1, 0))
        mixed_ref[:, pl.ds(pair * 2 * HDIM, 2 * HDIM)] = jnp.where(
            lower, results[0], results[1]
        ).astype(jnp.bfloat16)
    send(mixed_ref)
    stream = stream + contract(mixed_ref[...], full_ref[:, pl.ds(3 * features, features)], 1, 0)
    middle_ref[...] = stream
    send(middle_ref)
    normal, _ = layer_norm_parts(stream)
    second_ref[...] = (normal * norm_ref[1:2] + norm_ref[3:4]).astype(jnp.bfloat16)


def attention_backward_kernel(rows, place_ref, *refs):
    (
        full_ref,
        norm_ref,
        start_ref,
        middle_ref,
        first_ref,
        packed_ref,
        mixed_ref,
        grad_ref,
        router_ref,
    ) = refs[:9]
    part_refs = refs[9:-5]
    result_ref, branch_ref, blocks_ref, gpacked_ref, gmixed_ref = refs[-5:]
    features = start_ref.shape[1]
    padded = start_ref.shape[0]
    upstream = part_refs[0][...].astype(jnp.float32)
    for part_ref in part_refs[1:]:
        upstream = upstream + part_ref[...].astype(jnp.float32)
    normal, inverse = layer_norm_parts(middle_ref[...])
    gain_two = jnp.sum(upstream * normal, axis=0, keepdims=True)
    shift_two = jnp.sum(upstream, axis=0, keepdims=True)
    grad_middle = grad_ref[...].astype(jnp.float32) + layer_norm_pull(
        upstream, normal, inverse, norm_ref[1:2]
    )
    grad_attn = grad_middle.astype(jnp.bfloat16)
    gmixed_ref[...] = contract(
        grad_attn, full_ref[:, pl.ds(3 * features, features)], 1, 1
    ).astype(jnp.bfloat16)
    valid = lax.broadcasted_iota(jnp.int32, (padded, padded), 1) < SEQ
    lower = lax.broadcasted_iota(jnp.int32, (padded, 2 * HDIM), 1) < HDIM
    scale = HDIM ** (-0.5)
    for pair in range(features // (2 * HDIM)):
        spans = [pl.ds(part * features + pair * 2 * HDIM, 2 * HDIM) for part in range(3)]
        query, keys, values = [packed_ref[:, span] for span in spans]
        gmixed = gmixed_ref[:, spans[0]]
        blank = jnp.zeros_like(query)
        found = []
        for side in range(2):
            keep = lower if side == 0 else jnp.logical_not(lower)
            probs = head_probs(jnp.where(keep, query, blank), keys, valid)
            grad_probs = contract(jnp.where(keep, gmixed, blank), values, 1, 1)
            grad_values = contract(probs.astype(jnp.bfloat16), gmixed, 0, 0)
            grad_scores = (
                probs * (grad_probs - jnp.sum(probs * grad_probs, axis=1, keepdims=True))
            ).astype(jnp.bfloat16)
            grad_query = contract(grad_scores, keys, 1, 0) * scale
            grad_keys = contract(grad_scores, query, 0, 0) * scale
            found.append((grad_query, grad_keys, grad_values))
        for part in range(3):
            gpacked_ref[:, spans[part]] = jnp.where(lower, found[0][part], found[1][part]).astype(
                jnp.bfloat16
            )
    upstream = contract(gpacked_ref[...], full_ref[:, pl.ds(0, 3 * features)], 1, 1)
    normal, inverse = layer_norm_parts(start_ref[...])
    gain_one = jnp.sum(upstream * normal, axis=0, keepdims=True)
    shift_one = jnp.sum(upstream, axis=0, keepdims=True)
    result = grad_middle + layer_norm_pull(upstream, normal, inverse, norm_ref[0:1])
    result_ref[...] = result
    branch_ref[...] = result.astype(jnp.bfloat16)
    half = features // 2
    strip = features // rows
    extra = jnp.concatenate(
        [
            router_ref[...],
            gain_one,
            gain_two,
            shift_one,
            shift_two,
            jnp.zeros((blocks_ref.shape[2] - 4 * strip - router_ref.shape[0] - 4, features), jnp.float32),
        ],
        axis=0,
    ).astype(jnp.bfloat16)
    grad_proj = contract(mixed_ref[...], grad_attn, 0, 0).astype(jnp.bfloat16)
    for offset in range(rows):
        for side in range(2):
            columns = slice(side * half, (side + 1) * half)
            blocks_ref[side, offset, pl.ds(3 * strip, strip), :] = grad_proj[
                offset * strip : (offset + 1) * strip, columns
            ]
            blocks_ref[side, offset, pl.ds(4 * strip, extra.shape[0]), :] = extra[:, columns]
    for part in range(3):
        grad_part = contract(
            gpacked_ref[:, pl.ds(part * features, features)], first_ref[...], 0, 0
        ).astype(jnp.bfloat16)
        for offset in range(rows):
            for side in range(2):
                blocks_ref[side, offset, pl.ds(part * strip, strip), :] = grad_part[
                    offset * strip : (offset + 1) * strip, side * half : (side + 1) * half
                ]


def dispatch_kernel(room, codes_ref, *refs):
    groups = codes_ref.shape[1]
    block_refs, out_refs = refs[:-groups], refs[-groups:]
    padded = block_refs[0].shape[0]
    rows_of = lax.broadcasted_iota(jnp.int32, (room, padded), 0)
    for group in range(groups):
        total = jnp.zeros((room, block_refs[0].shape[1]), jnp.float32)
        for image, block_ref in enumerate(block_refs):
            picks = (codes_ref[image, group : group + 1, :] == rows_of).astype(jnp.float32)
            total = total + contract(picks.astype(jnp.bfloat16), block_ref[...], 1, 0)
        out_refs[group][...] = total.astype(jnp.bfloat16)


def combine_kernel(rows, codes_ref, *refs):
    slot_refs, out_refs = refs[: codes_ref.shape[1]], refs[codes_ref.shape[1] :]
    room = slot_refs[0].shape[0]
    padded = out_refs[0].shape[0]
    lanes = lax.broadcasted_iota(jnp.int32, (padded, room), 1)
    for image in range(rows):
        total = jnp.zeros(out_refs[0].shape, jnp.float32)
        for source, slot_ref in enumerate(slot_refs):
            codes = codes_ref[pl.ds(image * padded, padded), source : source + 1]
            picks = (codes == lanes).astype(jnp.float32)
            total = total + contract(picks.astype(jnp.bfloat16), slot_ref[...], 1, 0)
        out_refs[image][...] = total.astype(jnp.bfloat16)


def expert_router(place_ref, buffer, wrouter):
    router = softmax_rows(contract(buffer, wrouter, 1, 1))
    chosen = lax.broadcasted_iota(jnp.int32, router.shape, 1) == place_ref[3]
    gate = jnp.sum(jnp.where(chosen, router, 0.0), axis=1, keepdims=True)
    return (router, chosen, gate)


def expert_forward_kernel(groups, place_ref, wrouter_ref, win_ref, wout_ref, *refs):
    buffer = jnp.concatenate([ref[...] for ref in refs[:groups]], axis=0)
    room = refs[0].shape[0]
    half = buffer.shape[1] // 2
    _, _, gate = expert_router(place_ref, buffer, wrouter_ref[...])
    sums = [jnp.zeros((buffer.shape[0], half), jnp.float32) for _ in range(2)]
    for quarter in range(win_ref.shape[0] // 2):
        hidden = contract(buffer[:, :half], win_ref[2 * quarter], 1, 0) + contract(
            buffer[:, half:], win_ref[2 * quarter + 1], 1, 0
        )
        active = gelu_parts(hidden)[0].astype(jnp.bfloat16)
        for side in range(2):
            sums[side] = sums[side] + contract(active, wout_ref[2 * quarter + side], 1, 0)
    for group in range(groups):
        span = slice(group * room, (group + 1) * room)
        for side in range(2):
            refs[groups + group][:, pl.ds(side * half, half)] = (
                gate[span] * sums[side][span]
            ).astype(jnp.bfloat16)


def expert_full_kernel(groups, with_output, place_ref, wrouter_ref, win_ref, wout_ref, *refs):
    buffer = jnp.concatenate([ref[...] for ref in refs[:groups]], axis=0)
    grads = jnp.concatenate([ref[...] for ref in refs[groups : 2 * groups]], axis=0)
    back_refs = refs[2 * groups : 3 * groups]
    out_refs = refs[3 * groups : -3]
    gin_ref, gout_ref, grouter_ref = refs[-3:]
    room = refs[0].shape[0]
    half = buffer.shape[1] // 2
    router, chosen, gate = expert_router(place_ref, buffer, wrouter_ref[...])
    grad_slot = (gate * grads.astype(jnp.float32)).astype(jnp.bfloat16)
    flipped = buffer.T
    sums = [jnp.zeros((buffer.shape[0], half), jnp.float32) for _ in range(2)]
    backs = [jnp.zeros((buffer.shape[0], half), jnp.float32) for _ in range(2)]
    grad_gate = jnp.zeros((buffer.shape[0], 1), jnp.float32)
    for quarter in range(win_ref.shape[0] // 2):
        hidden = contract(buffer[:, :half], win_ref[2 * quarter], 1, 0) + contract(
            buffer[:, half:], win_ref[2 * quarter + 1], 1, 0
        )
        value, slope = gelu_parts(hidden)
        active = value.astype(jnp.bfloat16)
        if with_output:
            for side in range(2):
                sums[side] = sums[side] + contract(active, wout_ref[2 * quarter + side], 1, 0)
        pulled = contract(grads[:, :half], wout_ref[2 * quarter], 1, 1) + contract(
            grads[:, half:], wout_ref[2 * quarter + 1], 1, 1
        )
        grad_gate = grad_gate + jnp.sum(
            pulled * active.astype(jnp.float32), axis=1, keepdims=True
        )
        grad_hidden = (gate * pulled * slope).astype(jnp.bfloat16)
        turned = active.T
        for side in range(2):
            block = 2 * quarter + side
            span = slice(side * half, (side + 1) * half)
            backs[side] = backs[side] + contract(grad_hidden, win_ref[block], 1, 1)
            gin_ref[block] = contract(flipped[span], grad_hidden, 1, 0).astype(jnp.bfloat16)
            gout_ref[block] = contract(turned, grad_slot[:, span], 1, 0).astype(jnp.bfloat16)
    grad_logits = (
        router * (jnp.where(chosen, grad_gate, 0.0) - gate * grad_gate)
    ).astype(jnp.bfloat16)
    grouter_ref[...] = contract(grad_logits, buffer, 0, 0)
    router_back = contract(grad_logits, wrouter_ref[...], 1, 0)
    for group in range(groups):
        span = slice(group * room, (group + 1) * room)
        for side in range(2):
            columns = slice(side * half, (side + 1) * half)
            back_refs[group][:, columns] = (
                backs[side][span] + router_back[span, columns]
            ).astype(jnp.bfloat16)
            if with_output:
                out_refs[group][:, columns] = (gate[span] * sums[side][span]).astype(jnp.bfloat16)


SMALL = pl.BlockSpec(memory_space=pltpu.SMEM)
LOCAL = pl.BlockSpec(memory_space=pltpu.VMEM)
FAR = pl.BlockSpec(memory_space=pltpu.HBM)


def widen_kernel(narrow_ref, *refs):
    refs[-1][0, 0] = narrow_ref[0].astype(jnp.float32)


def widen_grads(layer, layer_count, narrow, previous):
    members, *block = narrow.shape
    anywhere = pl.BlockSpec(memory_space=pl.ANY)
    return pl.pallas_call(
        widen_kernel,
        name="widen",
        grid=(members,),
        in_specs=[pl.BlockSpec((1, *block), lambda step: (step, 0, 0))]
        + [anywhere] * len(previous),
        out_specs=pl.BlockSpec((1, 1, *block), lambda step: (layer, step, 0, 0)),
        out_shape=jax.ShapeDtypeStruct((layer_count, members, *block), jnp.float32),
        input_output_aliases={1: 0} if previous else {},
        compiler_params=pltpu.CompilerParams(vmem_limit_bytes=4 * 1024 * 1024),
    )(narrow, *previous)


class Staged:
    def __init__(self, ref, move=None):
        self.ref, self.move = ref, move
        self.shape, self.dtype = ref.shape, ref.dtype

    def wait(self):
        if self.move is not None:
            self.move.wait()
            self.move = None

    def __getitem__(self, index):
        self.wait()
        return self.ref[index]


class Sent:
    def __init__(self, ref, move):
        self.ref, self.move, self.moving = ref, move, False
        self.shape, self.dtype = ref.shape, ref.dtype

    def __getitem__(self, index):
        return self.ref[index]

    def __setitem__(self, index, values):
        self.ref[index] = values

    def send(self):
        if not self.moving:
            self.move.start()
            self.moving = True


def send(ref):
    if isinstance(ref, Sent):
        ref.send()


def staged_body(body, fixed_count, staged, far, *refs):
    fixed, refs = refs[:fixed_count], refs[fixed_count:]
    sources, refs = list(refs[: len(staged)]), refs[len(staged) :]
    targets, refs = list(refs[: len(far)]), refs[len(far) :]
    copies, refs = list(refs[: sum(staged)]), refs[sum(staged) :]
    made, refs = list(refs[: sum(far)]), refs[sum(far) :]
    marks, scratch = refs[0], refs[1:]
    for place, moved in enumerate(staged):
        if moved:
            copy = copies.pop(0)
            move = pltpu.make_async_copy(sources[place], copy, marks.at[place])
            sources[place] = Staged(copy, move)
    waiting = [source for source in sources if isinstance(source, Staged)]
    for source in sorted(waiting, key=lambda source: math.prod(source.shape)):
        source.move.start()
    for place, apart in enumerate(far):
        if apart:
            source = made.pop(0)
            move = pltpu.make_async_copy(source, targets[place], marks.at[len(staged) + place])
            targets[place] = Sent(source, move)
    body(*fixed, *sources, *targets, *scratch)
    for source in sources:
        if isinstance(source, Staged):
            source.wait()
    for target in targets:
        send(target)
    for target in targets:
        if isinstance(target, Sent):
            target.move.wait()


def run_kernel(
    title, body, place, operands, results, work, scratch=(), room=16, near=(), far=()
):
    fixed = [] if place is None else [place]
    staged = [place not in near for place in range(len(operands))]
    arguments = fixed + [
        pltpu.with_memory_space_constraint(piece, pltpu.HBM) if moved else piece
        for moved, piece in zip(staged, operands)
    ]
    apart = [place in far for place in range(len(results))]
    return pl.pallas_call(
        functools.partial(staged_body, body, len(fixed), staged, apart),
        name=title,
        in_specs=[SMALL] * len(fixed) + [FAR if moved else LOCAL for moved in staged],
        out_specs=[FAR if away else LOCAL for away in apart],
        out_shape=[
            pltpu.HBM(shape, kind) if away else jax.ShapeDtypeStruct(shape, kind)
            for away, (shape, kind) in zip(apart, results)
        ],
        scratch_shapes=[
            pltpu.VMEM(piece.shape, piece.dtype) for moved, piece in zip(staged, operands) if moved
        ]
        + [pltpu.VMEM(shape, kind) for away, (shape, kind) in zip(apart, results) if away]
        + [pltpu.SemaphoreType.DMA((len(operands) + len(results),))]
        + list(scratch),
        compiler_params=pltpu.CompilerParams(vmem_limit_bytes=room * 1024 * 1024),
        cost_estimate=pl.CostEstimate(
            flops=work,
            bytes_accessed=sum(piece.size * piece.dtype.itemsize for piece in arguments),
            transcendentals=0,
        ),
    )(*arguments)


def after(values, *earlier):
    return lax.optimization_barrier((values, *earlier))[0]


def gather_group(values):
    near = [values]
    for offset in range(1, lax.axis_size("row")):
        near.append(exchange(values, "row", offset))
    return near + [exchange(piece, "col", 1) for piece in near]


def scatter_pieces(pieces, axis):
    return [
        piece if offset == 0 else exchange(piece, axis, offset)
        for offset, piece in enumerate(pieces)
    ]


def add_pieces(pieces):
    total = pieces[0].astype(jnp.float32)
    for piece in pieces[1:]:
        total = total + piece.astype(jnp.float32)
    return total


def sum_chip(blocks, at_col):
    mine = lax.dynamic_index_in_dim(blocks, at_col, 0, keepdims=False)
    other = exchange(lax.dynamic_index_in_dim(blocks, 1 - at_col, 0, keepdims=False), "col", 1)
    return add_pieces([mine, other]).astype(blocks.dtype)


def sum_groups(plane):
    groups, at_dp = lax.axis_size("dp"), lax.axis_index("dp")
    part = plane.shape[0] // groups
    pieces = [
        lax.dynamic_slice_in_dim(plane, (at_dp ^ offset) * part, part, 0)
        for offset in range(groups)
    ]
    owned = add_pieces(scatter_pieces(pieces, "dp")).astype(plane.dtype)
    result = jnp.zeros(plane.shape, jnp.float32)
    for offset in range(groups):
        piece = owned if offset == 0 else exchange(owned, "dp", offset)
        result = lax.dynamic_update_slice_in_dim(
            result, piece.astype(jnp.float32), (at_dp ^ offset) * part, 0
        )
    return result


def group_device(
    tokens,
    norm_gain,
    norm_shift,
    w_qkv,
    w_proj,
    w_router,
    w_in,
    w_out,
    expert_ids,
    slot_ids,
    cotangent,
):
    low = jnp.bfloat16
    groups, rows = lax.axis_size("dp"), lax.axis_size("row")
    members = 2 * rows
    at_dp, at_row, at_col = [lax.axis_index(name) for name in ("dp", "row", "col")]
    layer_count = w_qkv.shape[0]
    expert_count = w_in.shape[1]
    half = tokens.shape[1]
    features = 2 * half
    strip = features // rows
    padded = -(-SEQ // 16) * 16
    owner = at_dp * members + at_row * 2 + at_col
    place = jnp.stack([at_dp, at_row, at_col, owner]).astype(jnp.int32)

    def join(mine, other):
        return jnp.where(
            at_col == 0,
            jnp.concatenate([mine, other], axis=-1),
            jnp.concatenate([other, mine], axis=-1),
        )

    small = jnp.concatenate(
        [
            jnp.concatenate([norm_gain, norm_shift], axis=1).reshape(-1, half),
            w_router.transpose(0, 2, 1).reshape(-1, half).astype(jnp.float32),
        ],
        axis=0,
    )
    small = join(small, exchange(small, "col", 1))
    norms = small[: 4 * layer_count].reshape(layer_count, 4, features)
    routers = small[4 * layer_count :].reshape(layer_count, expert_count, features).astype(low)
    both = jnp.stack([tokens, cotangent]).reshape(2, 2, SEQ, half)
    mine = lax.dynamic_index_in_dim(both, at_col, 1, keepdims=False)
    other = exchange(lax.dynamic_index_in_dim(both, 1 - at_col, 1, keepdims=False), "col", 1)
    both = jnp.pad(join(mine, other), ((0, 0), (0, padded - SEQ), (0, 0)))

    def fetch_attention(layer, *earlier):
        block = jnp.concatenate(
            [
                w_qkv[layer].reshape(half, -1),
                jnp.concatenate(
                    [
                        w_proj[layer][:, piece * strip : (piece + 1) * strip]
                        for piece in range(half // strip)
                    ],
                    axis=0,
                ),
            ],
            axis=1,
        )
        return gather_group(after(block, *earlier) if earlier else block)

    def own_experts(layer, source):
        own = lax.dynamic_slice(
            source, (layer, at_dp * members, 0, 0), (1, members, *source.shape[2:])
        )
        return own[0]

    def fetch_weights(own, *earlier):
        return lax.all_to_all(
            after(own, *earlier), ("row", "col"), split_axis=0, concat_axis=0, tiled=True
        )

    capacity = 2 * ((5 * members * SEQ + 4 * expert_count - 1) // (4 * expert_count))
    room = -(-capacity // 16) * 16
    images = jnp.stack(
        [(at_row ^ offset) * 2 + (at_col ^ side) for side in range(2) for offset in range(rows)]
    )
    named = jnp.stack(
        [
            (at_dp ^ offset) * members + at_row * 2 + (at_col ^ side)
            for side in range(2)
            for offset in range(groups)
        ]
    )
    chosen = jnp.take(expert_ids.reshape(layer_count, members, SEQ, -1), images, axis=1)
    slots = jnp.take(slot_ids.reshape(layer_count, members, SEQ, -1), images, axis=1)
    codes = jnp.max(
        jnp.where(chosen[..., None] == named, slots[..., None], -1), axis=3
    )
    codes = jnp.pad(codes, ((0, 0), (0, 0), (0, padded - SEQ), (0, 0)), constant_values=-1)
    send_codes = codes[..., :groups].transpose(0, 1, 3, 2)
    back_codes = codes[:, :rows].reshape(layer_count, rows * padded, 2 * groups)

    token_block = ((padded, features), low)
    slot_block = ((room, features), low)

    def after_all(pieces, *earlier):
        return [after(piece, *earlier) for piece in pieces]

    def dispatch(layer, images):
        return run_kernel(
            "dispatch",
            functools.partial(dispatch_kernel, room),
            None,
            [send_codes[layer]] + images,
            [slot_block] * groups,
            2 * members * padded * groups * room * features,
            near=range(1, 1 + len(images)),
        )

    def bring_back(blocks, *earlier):
        blocks = after_all(scatter_pieces(blocks, "dp"), *earlier)
        return blocks + [exchange(piece, "col", 1) for piece in blocks]

    def combine(layer, blocks):
        return run_kernel(
            "combine",
            functools.partial(combine_kernel, rows),
            None,
            [back_codes[layer]] + blocks,
            [token_block] * rows,
            4 * rows * padded * groups * room * features,
        )

    def split(values):
        pieces = values[:SEQ].reshape(SEQ, 2, half)
        mine = lax.dynamic_index_in_dim(pieces, at_col, 1, keepdims=False)
        other = exchange(lax.dynamic_index_in_dim(pieces, 1 - at_col, 1, keepdims=False), "col", 1)
        return jnp.where(
            at_col == 0,
            jnp.concatenate([mine, other], axis=0),
            jnp.concatenate([other, mine], axis=0),
        )

    work = 4 * groups * room * members * half * w_in.shape[3]
    stream, parts = both[0], []
    kept, buffers, weights = [], [], []
    attention_blocks = fetch_attention(0)
    ready = attention_blocks[1:rows]
    for layer in range(layer_count):
        last = layer == layer_count - 1
        weight_in = fetch_weights(own_experts(layer, w_in), *ready)
        own_out = own_experts(layer, w_out)
        upstream = []
        if last:
            upstream = gather_group(after(both[1], *parts[1:]))
        saved = run_kernel(
            "attention_forward",
            functools.partial(attention_forward_kernel, rows),
            place,
            attention_blocks + [norms[layer], stream] + parts,
            [
                ((padded, features), jnp.float32),
                ((padded, features), jnp.float32),
                token_block,
                ((padded, 3 * features), low),
                token_block,
                token_block,
                ((features, 4 * features), low),
            ],
            16 * padded * features * features,
            far=(0, 1, 2, 3, 4, 6),
        )
        kept.append(saved)
        stream = saved[1]
        images = gather_group(saved[5])
        weight_out = fetch_weights(own_out, *images[1:rows], *upstream[1:rows])
        weights.append([weight_in, weight_out])
        if last:
            sent = dispatch(layer, upstream)
            branches = scatter_pieces(sent, "dp")
            images = after_all(images, sent[0])
        buffers.append(scatter_pieces(dispatch(layer, images), "dp"))
        if not last:
            result = run_kernel(
                "expert_forward",
                functools.partial(expert_forward_kernel, groups),
                place,
                [routers[layer]] + weights[layer] + buffers[layer],
                [slot_block] * groups,
                work,
            )
            ready = [result[0]]
            attention_blocks = fetch_attention(layer + 1, result[0])
            parts = scatter_pieces(combine(layer, bring_back(result)), "row")
    grad = both[1]
    shared = [None] * layer_count
    grad_in, grad_out = [], []
    for layer in reversed(range(layer_count)):
        last = layer == layer_count - 1
        found = run_kernel(
            "expert_full",
            functools.partial(expert_full_kernel, groups, last),
            place,
            [routers[layer]] + weights[layer] + buffers[layer] + branches,
            [slot_block] * (2 * groups if last else groups)
            + [
                (weights[layer][0].shape, low),
                (weights[layer][1].shape, low),
                ((expert_count, features), jnp.float32),
            ],
            3 * work,
            room=24,
        )
        if last:
            moved_in = fetch_weights(found[-3])
            blocks = bring_back(list(found[:groups]))
        else:
            arrived = scatter_pieces(chip, "row")
            moved_in = fetch_weights(found[-3], moved_out, *arrived[1:])
            moved_out = after(moved_out, found[0])
            grad_out = [widen_grads(layer + 1, layer_count, moved_out, grad_out)]
            blocks = bring_back(list(found[:groups]), *grad_out)
            earlier = add_pieces(arrived).astype(low)
        pieces = combine(layer, blocks)
        if last:
            outputs = bring_back(after_all(list(found[groups : 2 * groups]), pieces[0]))
        grad_parts = scatter_pieces(after_all(pieces, moved_in), "row")
        if last:
            grad_parts[0] = after(grad_parts[0], *outputs[1:groups])
        saved = kept[layer]
        height = -(-(4 * strip + expert_count + 4) // (16 * groups)) * (16 * groups)
        grad, branch, blocks = run_kernel(
            "attention_backward",
            functools.partial(attention_backward_kernel, rows),
            place,
            [saved[6], norms[layer], saved[0], saved[1], saved[2], saved[3], saved[4], grad]
            + [found[-1]]
            + grad_parts,
            [
                ((padded, features), jnp.float32),
                token_block,
                ((2, rows, height, half), low),
            ],
            32 * padded * features * features,
            [pltpu.VMEM((padded, 3 * features), low), pltpu.VMEM((padded, features), low)],
        )
        chip = list(sum_chip(blocks, at_col))
        if layer > 0:
            images = gather_group(branch)
            moved_out = fetch_weights(found[-2], *images[1:rows])
            sent = dispatch(layer - 1, images)
            branches = scatter_pieces(sent, "dp")
            moved_in = after(moved_in, sent[0])
            grad_in = [widen_grads(layer, layer_count, moved_in, grad_in)]
            if last:
                outputs = combine(layer, after_all(outputs, sent[0]))
            branches = after_all(branches, *grad_in, *outputs, *chip)
        else:
            arrived = scatter_pieces(chip, "row")
            moved_out = fetch_weights(found[-2], *arrived[1:])
            grad_in = [widen_grads(layer, layer_count, after(moved_in, chip[0]), grad_in)]
            outputs = scatter_pieces(after_all(outputs, chip[0]), "row")
            for part in outputs:
                stream = stream + part.astype(jnp.float32)
            output = split(stream.astype(low))
            arrived = after_all(arrived, *grad_in)
            grad_out = [widen_grads(layer, layer_count, moved_out, grad_out)]
            both_sums = jnp.concatenate([add_pieces(arrived).astype(low), earlier], axis=1)
            both_sums = sum_groups(both_sums)
            shared = [both_sums[:, :half], both_sums[:, half:]]
    grad_input = split(grad)
    shared = jnp.stack(shared)
    grad_qkv = (
        shared[:, : 3 * strip].reshape(layer_count, 3, strip, half).transpose(0, 3, 1, 2)
    )
    grad_proj = shared[:, 3 * strip : 4 * strip]
    grad_router = shared[:, 4 * strip : 4 * strip + expert_count].transpose(0, 2, 1)
    tail = shared[:, 4 * strip + expert_count : 4 * strip + expert_count + 4]
    return (
        output,
        grad_input,
        grad_qkv,
        grad_proj,
        grad_router,
        grad_in[0],
        grad_out[0],
        tail[:, :2],
        tail[:, 2:],
    )


def fits_groups(mesh, tokens, w_in):
    groups, rows, sides = mesh.shape["dp"], mesh.shape["row"], mesh.shape["col"]
    powers = all(size & (size - 1) == 0 for size in (groups, rows))
    return (
        sides == 2
        and powers
        and tokens.shape[0] == groups * rows * sides * SEQ
        and w_in.shape[1] == groups * rows * sides
    )


def solution(mesh):
    in_specs = (
        P(("dp", "row"), "col"),
        P(None, None, "col"),
        P(None, None, "col"),
        P(None, "col", None, "row"),
        P(None, "row", "col"),
        P(None, "col", None),
        P(None, None, "col", "row"),
        P(None, None, "row", "col"),
        P(None, "dp", None),
        P(None, "dp", None),
        P(("dp", "row"), "col"),
    )
    out_specs = (
        P(("dp", "row"), "col"),
        P(("dp", "row"), "col"),
        P(None, "col", None, "row"),
        P(None, "row", "col"),
        P(None, "col", None),
        P(None, "dp", "col", "row"),
        P(None, "dp", "row", "col"),
        P(None, None, "col"),
        P(None, None, "col"),
    )

    def program(*arguments):
        fits = fits_groups(mesh, arguments[0], arguments[6])
        return jax.shard_map(
            group_device if fits else per_device,
            mesh=mesh,
            in_specs=in_specs,
            out_specs=out_specs,
            check_vma=False,
        )(*arguments)

    return program
```

```python
import functools
import math

import jax
import jax.numpy as jnp
from jax import lax
from jax.experimental import pallas as pl
from jax.experimental.pallas import tpu as pltpu
from jax.sharding import PartitionSpec as P

HDIM = 64
SEQ = 197


EPSILON = 1e-06


def gather_rows(values):
    return lax.all_gather(values, "row", axis=0, tiled=True)


def sum_rows(values):
    return lax.psum_scatter(values, "row", scatter_dimension=0, tiled=True)


def gather_halves(values):
    return lax.all_gather(values, "col", axis=0, tiled=True)


def sum_halves(values):
    return lax.psum_scatter(values, "col", scatter_dimension=0, tiled=True)


def row_totals(first, second):
    return lax.psum((first, second), "col")


def softmax_rows(values):
    shifted = jnp.exp(values - jnp.max(values, axis=-1, keepdims=True))
    return shifted / jnp.sum(shifted, axis=-1, keepdims=True)


def norm_forward(stream, gain_row, shift_row):
    feature_count = stream.shape[1] * lax.axis_size("col")
    total, squares = row_totals(jnp.sum(stream, axis=1), jnp.sum(stream * stream, axis=1))
    center = total / feature_count
    inverse = lax.rsqrt(squares / feature_count - center * center + EPSILON)
    normal = (stream - center[:, None]) * inverse[:, None]
    return (normal * gain_row + shift_row, normal, inverse)


def norm_backward(upstream, normal, inverse, gain_row):
    feature_count = upstream.shape[1] * lax.axis_size("col")
    scaled = upstream * gain_row
    first, second = row_totals(jnp.sum(scaled, axis=1), jnp.sum(scaled * normal, axis=1))
    result_grad = inverse[:, None] * (
        scaled - first[:, None] / feature_count - normal * (second[:, None] / feature_count)
    )
    return (result_grad, jnp.sum(upstream * normal, axis=0), jnp.sum(upstream, axis=0))


def split_heads(packed):
    row_count = packed.shape[0]
    heads_here = packed.shape[1] // (3 * HDIM)
    parts = packed.reshape(row_count // SEQ, SEQ, 3, heads_here, HDIM)
    return (parts[:, :, 0], parts[:, :, 1], parts[:, :, 2])


def attend_forward(packed):
    query_part, key_part, value_part = split_heads(packed)
    scores = jnp.einsum(
        "bqhd,bkhd->bhqk", query_part, key_part, preferred_element_type=jnp.float32
    ) * HDIM ** (-0.5)
    highest = jnp.max(scores, axis=-1, keepdims=True)
    powers = jnp.exp(scores - highest)
    totals = jnp.sum(powers, axis=-1, keepdims=True)
    weights = (powers / totals).astype(jnp.bfloat16)
    mixed_heads = jnp.einsum(
        "bhqk,bkhd->bqhd", weights, value_part, preferred_element_type=jnp.float32
    )
    return (
        mixed_heads.reshape(packed.shape[0], -1).astype(jnp.bfloat16),
        highest + jnp.log(totals),
    )


def attend_backward(packed, logsum, grad_mixed):
    query_part, key_part, value_part = split_heads(packed)
    scale = HDIM ** (-0.5)
    scores = (
        jnp.einsum("bqhd,bkhd->bhqk", query_part, key_part, preferred_element_type=jnp.float32)
        * scale
    )
    probs_full = jnp.exp(scores - logsum)
    upstream = grad_mixed.reshape(query_part.shape)
    grad_probs = jnp.einsum(
        "bqhd,bkhd->bhqk", upstream, value_part, preferred_element_type=jnp.float32
    )
    grad_values = jnp.einsum(
        "bhqk,bqhd->bkhd",
        probs_full.astype(jnp.bfloat16),
        upstream,
        preferred_element_type=jnp.float32,
    )
    grad_scores = (
        probs_full * (grad_probs - jnp.sum(probs_full * grad_probs, axis=-1, keepdims=True))
    ).astype(jnp.bfloat16)
    grad_query = (
        jnp.einsum("bhqk,bkhd->bqhd", grad_scores, key_part, preferred_element_type=jnp.float32)
        * scale
    )
    grad_keys = (
        jnp.einsum("bhqk,bqhd->bkhd", grad_scores, query_part, preferred_element_type=jnp.float32)
        * scale
    )
    stacked = jnp.stack([grad_query, grad_keys, grad_values], axis=2)
    return stacked.reshape(packed.shape[0], -1).astype(jnp.bfloat16)


def attention_forward(stream, gain_row, shift_row, weight_qkv, weight_proj):
    normed, normal, inverse = norm_forward(stream, gain_row, shift_row)
    normed_all = gather_rows(normed.astype(jnp.bfloat16))
    packed = sum_halves(jnp.dot(normed_all, weight_qkv, preferred_element_type=jnp.float32)).astype(
        jnp.bfloat16
    )
    mixed_heads, logsum = attend_forward(packed)
    mixed_all = gather_halves(mixed_heads)
    branch = sum_rows(jnp.dot(mixed_all, weight_proj, preferred_element_type=jnp.float32))
    saved = {
        "normal": normal,
        "inverse": inverse,
        "normed_all": normed_all,
        "packed": packed,
        "logsum": logsum,
        "mixed_all": mixed_all,
    }
    return (stream + branch, saved)


def attention_backward(upstream, saved, weight_qkv, weight_proj):
    grad_all = gather_rows(upstream.astype(jnp.bfloat16))
    grad_mixed = sum_halves(
        jnp.einsum("te,de->td", grad_all, weight_proj, preferred_element_type=jnp.float32)
    ).astype(jnp.bfloat16)
    grad_w_proj = jnp.einsum(
        "td,te->de", saved["mixed_all"], grad_all, preferred_element_type=jnp.float32
    )
    grad_packed = attend_backward(saved["packed"], saved["logsum"], grad_mixed)
    grad_packed_all = gather_halves(grad_packed)
    grad_part = jnp.einsum(
        "tf,df->td", grad_packed_all, weight_qkv, preferred_element_type=jnp.float32
    )
    grad_w_qkv = jnp.einsum(
        "td,tf->df", saved["normed_all"], grad_packed_all, preferred_element_type=jnp.float32
    )
    return (sum_rows(grad_part), grad_w_qkv, grad_w_proj)


def second_product(active, buffer_shape, weight_out):
    active_all = gather_halves(active).reshape(buffer_shape[0], buffer_shape[1], -1)
    slot_out = jnp.einsum(
        "ecf,efd->ecd", active_all, weight_out, preferred_element_type=jnp.float32
    )
    return (active_all, slot_out.reshape(-1, slot_out.shape[2]))


def expert_forward(
    stream, gain_row, shift_row, choice_ids, slot_rows, weight_router, weight_in, weight_out
):
    normed, normal, inverse = norm_forward(stream, gain_row, shift_row)
    normed_all = gather_rows(normed.astype(jnp.bfloat16))
    row_count = normed_all.shape[0]
    expert_count = weight_in.shape[0]
    capacity = 2 * ((5 * row_count + 4 * expert_count - 1) // (4 * expert_count))
    logits = lax.psum(jnp.dot(normed_all, weight_router, preferred_element_type=jnp.float32), "col")
    router = softmax_rows(logits)
    onehot = (
        choice_ids[:, :, None] == lax.broadcasted_iota(jnp.int32, (1, 1, expert_count), 2)
    ).astype(jnp.float32)
    gate_values = jnp.sum(onehot * router[:, None, :], axis=2)
    flat_slots = choice_ids * capacity + slot_rows
    owners = jnp.broadcast_to(
        lax.broadcasted_iota(jnp.int32, (row_count, 1), 0), flat_slots.shape
    ).reshape(-1)
    slot_owner = (
        jnp.full((expert_count * capacity,), row_count, jnp.int32)
        .at[flat_slots.reshape(-1)]
        .set(owners)
    )
    slot_assign = (
        jnp.full((expert_count * capacity,), 2 * row_count, jnp.int32)
        .at[flat_slots.reshape(-1)]
        .set(lax.iota(jnp.int32, 2 * row_count))
    )
    padded = jnp.concatenate(
        [normed_all, jnp.zeros((1, normed_all.shape[1]), jnp.bfloat16)], axis=0
    )
    buffer = padded[slot_owner].reshape(expert_count, capacity, -1)
    hidden_part = jnp.einsum("ecd,edf->ecf", buffer, weight_in, preferred_element_type=jnp.float32)
    hidden = sum_halves(hidden_part.reshape(buffer.shape[0] * buffer.shape[1], -1))
    active = jax.nn.gelu(hidden).astype(jnp.bfloat16)
    active_all, slot_out = second_product(active, buffer.shape, weight_out)
    branch_part = jnp.sum(gate_values[:, :, None] * slot_out[flat_slots], axis=1)
    saved = {
        "normal": normal,
        "inverse": inverse,
        "normed_all": normed_all,
        "router": router,
        "onehot": onehot,
        "gate_values": gate_values,
        "flat_slots": flat_slots,
        "slot_owner": slot_owner,
        "slot_assign": slot_assign,
        "buffer": buffer,
        "hidden": hidden,
        "active": active,
    }
    saved["active_all"] = active_all
    saved["slot_out"] = slot_out
    return (stream + sum_rows(branch_part), saved)


def expert_backward(upstream, saved, weight_router, weight_in, weight_out):
    buffer = saved["buffer"]
    expert_count = weight_in.shape[0]
    capacity = saved["slot_owner"].shape[0] // expert_count
    active_all = saved["active_all"]
    slot_out = saved["slot_out"]
    flat_slots = saved["flat_slots"]
    grad_all = gather_rows(upstream.astype(jnp.bfloat16))
    gate_part = jnp.sum(grad_all.astype(jnp.float32)[:, None, :] * slot_out[flat_slots], axis=2)
    grad_gates = lax.psum(gate_part, ("row", "col"))
    padded_grad = jnp.concatenate(
        [grad_all, jnp.zeros((1, grad_all.shape[1]), jnp.bfloat16)], axis=0
    )
    slot_gate = jnp.concatenate([saved["gate_values"].reshape(-1), jnp.zeros((1,), jnp.float32)])[
        saved["slot_assign"]
    ]
    grad_slot = (
        (slot_gate[:, None] * padded_grad[saved["slot_owner"]])
        .astype(jnp.bfloat16)
        .reshape(expert_count, capacity, -1)
    )
    grad_active_part = jnp.einsum(
        "ecd,efd->ecf", grad_slot, weight_out, preferred_element_type=jnp.float32
    )
    grad_w_out = jnp.einsum(
        "ecf,ecd->efd", active_all, grad_slot, preferred_element_type=jnp.float32
    )
    grad_active = sum_halves(grad_active_part.reshape(buffer.shape[0] * buffer.shape[1], -1))
    gelu_pull = jax.vjp(jax.nn.gelu, saved["hidden"])[1]
    grad_hidden = gelu_pull(grad_active)[0].astype(jnp.bfloat16)
    grad_hidden_all = gather_halves(grad_hidden).reshape(buffer.shape[0], buffer.shape[1], -1)
    grad_buffer = jnp.einsum(
        "ecf,edf->ecd", grad_hidden_all, weight_in, preferred_element_type=jnp.float32
    )
    grad_w_in = jnp.einsum(
        "ecd,ecf->edf", buffer, grad_hidden_all, preferred_element_type=jnp.float32
    )
    grad_buffer = grad_buffer.reshape(expert_count * capacity, -1)
    router = saved["router"]
    grad_probs = jnp.sum(grad_gates[:, :, None] * saved["onehot"], axis=1)
    grad_logits = (
        router * (grad_probs - jnp.sum(router * grad_probs, axis=1, keepdims=True))
    ).astype(jnp.bfloat16)
    grad_w_router = jnp.einsum(
        "td,te->de", saved["normed_all"], grad_logits, preferred_element_type=jnp.float32
    )
    router_back = jnp.einsum(
        "te,de->td", grad_logits, weight_router, preferred_element_type=jnp.float32
    )
    leading = (lax.axis_index("row") == 0).astype(jnp.float32)
    grad_part = jnp.sum(grad_buffer[flat_slots], axis=1) + leading * router_back
    return (sum_rows(grad_part), grad_w_router, grad_w_in, grad_w_out)


def per_device(
    tokens,
    norm_gain,
    norm_shift,
    w_qkv,
    w_proj,
    w_router,
    w_in,
    w_out,
    expert_ids,
    slot_ids,
    cotangent,
):
    layer_count = w_qkv.shape[0]
    stream = tokens.astype(jnp.float32)
    attention_saved = []
    expert_saved = []
    for layer_index in range(layer_count):
        weight_qkv = w_qkv[layer_index].reshape(w_qkv.shape[1], -1)
        stream, kept_one = attention_forward(
            stream,
            norm_gain[layer_index, 0],
            norm_shift[layer_index, 0],
            weight_qkv,
            w_proj[layer_index],
        )
        stream, kept_two = expert_forward(
            stream,
            norm_gain[layer_index, 1],
            norm_shift[layer_index, 1],
            expert_ids[layer_index],
            slot_ids[layer_index],
            w_router[layer_index],
            w_in[layer_index],
            w_out[layer_index],
        )
        attention_saved.append(kept_one)
        expert_saved.append(kept_two)
    output = stream.astype(jnp.bfloat16)
    grad_stream = cotangent.astype(jnp.float32)
    qkv_grads = [None] * layer_count
    proj_grads = [None] * layer_count
    router_grads = [None] * layer_count
    in_grads = [None] * layer_count
    out_grads = [None] * layer_count
    gain_grads = [None] * layer_count
    shift_grads = [None] * layer_count
    for layer_index in reversed(range(layer_count)):
        weight_qkv = w_qkv[layer_index].reshape(w_qkv.shape[1], -1)
        kept_two = expert_saved[layer_index]
        grad_normed, router_grads[layer_index], grad_w_in, grad_w_out = expert_backward(
            grad_stream, kept_two, w_router[layer_index], w_in[layer_index], w_out[layer_index]
        )
        grad_w_in, grad_w_out = (
            lax.psum_scatter(grad_w_in, "dp", scatter_dimension=0, tiled=True),
            lax.psum_scatter(grad_w_out, "dp", scatter_dimension=0, tiled=True),
        )
        in_grads[layer_index] = grad_w_in
        out_grads[layer_index] = grad_w_out
        grad_inner, gain_two, shift_two = norm_backward(
            grad_normed, kept_two["normal"], kept_two["inverse"], norm_gain[layer_index, 1]
        )
        grad_stream = grad_stream + grad_inner
        kept_one = attention_saved[layer_index]
        grad_normed, grad_w_qkv, proj_grads[layer_index] = attention_backward(
            grad_stream, kept_one, weight_qkv, w_proj[layer_index]
        )
        qkv_grads[layer_index] = grad_w_qkv.reshape(w_qkv.shape[1:])
        grad_inner, gain_one, shift_one = norm_backward(
            grad_normed, kept_one["normal"], kept_one["inverse"], norm_gain[layer_index, 0]
        )
        grad_stream = grad_stream + grad_inner
        gain_grads[layer_index] = jnp.stack([gain_one, gain_two])
        shift_grads[layer_index] = jnp.stack([shift_one, shift_two])
    grad_qkv, grad_proj, grad_router = lax.psum(
        (jnp.stack(qkv_grads), jnp.stack(proj_grads), jnp.stack(router_grads)), "dp"
    )
    grad_gain, grad_shift = lax.psum((jnp.stack(gain_grads), jnp.stack(shift_grads)), ("dp", "row"))
    grad_in = jnp.stack(in_grads)
    grad_out = jnp.stack(out_grads)
    return (
        output,
        grad_stream,
        grad_qkv,
        grad_proj,
        grad_router,
        grad_in,
        grad_out,
        grad_gain,
        grad_shift,
    )


def exchange(values, axis, offset):
    count = lax.axis_size(axis)
    return lax.ppermute(values, axis, [(place, place ^ offset) for place in range(count)])


def contract(left, right, left_dim, right_dim):
    return lax.dot_general(
        left, right, (((left_dim,), (right_dim,)), ((), ())), preferred_element_type=jnp.float32
    )


def layer_norm_parts(values):
    center = jnp.mean(values, axis=1, keepdims=True)
    shifted = values - center
    spread = jnp.mean(shifted * shifted, axis=1, keepdims=True)
    inverse = lax.rsqrt(spread + EPSILON)
    return (shifted * inverse, inverse)


def layer_norm_pull(upstream, normal, inverse, gain_row):
    scaled = upstream * gain_row
    first = jnp.mean(scaled, axis=1, keepdims=True)
    second = jnp.mean(scaled * normal, axis=1, keepdims=True)
    return inverse * (scaled - first - normal * second)


def gelu_parts(values):
    factor = (2.0 / jnp.pi) ** 0.5
    squares = values * values
    curve = jnp.tanh(values * (factor + (factor * 0.044715) * squares))
    half = 0.5 + 0.5 * curve
    slope = half + (0.5 * values) * (1.0 - curve * curve) * (
        factor + (3.0 * factor * 0.044715) * squares
    )
    return (values * half, slope)


def head_probs(query_head, key_pair, valid):
    scores = contract(query_head, key_pair, 1, 1) * HDIM ** (-0.5)
    scores = jnp.where(valid, scores, -1e30)
    powers = jnp.exp(scores - jnp.max(scores, axis=1, keepdims=True))
    return powers / jnp.sum(powers, axis=1, keepdims=True)


def assemble_weights(place_ref, block_refs, full_ref, rows, features):
    half = features // 2
    strip = features // rows
    for position, block_ref in enumerate(block_refs):
        other, offset = divmod(position, rows)
        side = lax.bitwise_xor(place_ref[2], other)
        top = pl.multiple_of(side * half, half)
        for part in range(3):
            full_ref[pl.ds(top, half), pl.ds(part * features + offset * strip, strip)] = block_ref[
                :, pl.ds(part * strip, strip)
            ]
        for piece in range(half // strip):
            left = pl.multiple_of(3 * features + side * half + piece * strip, strip)
            full_ref[pl.ds(offset * strip, strip), pl.ds(left, strip)] = block_ref[
                pl.ds(piece * strip, strip), pl.ds(3 * strip, strip)
            ]


def attention_forward_kernel(rows, place_ref, *refs):
    block_refs = refs[: 2 * rows]
    norm_ref, stream_ref = refs[2 * rows : 2 * rows + 2]
    start_ref, middle_ref, first_ref, packed_ref, mixed_ref, second_ref, full_ref = refs[-7:]
    part_refs = refs[2 * rows + 2 : -7]
    features = stream_ref.shape[1]
    padded = stream_ref.shape[0]
    stream = stream_ref[...].astype(jnp.float32)
    for part_ref in part_refs:
        stream = stream + part_ref[...].astype(jnp.float32)
    start_ref[...] = stream
    send(start_ref)
    assemble_weights(place_ref, block_refs, full_ref, rows, features)
    send(full_ref)
    normal, _ = layer_norm_parts(stream)
    normed = (normal * norm_ref[0:1] + norm_ref[2:3]).astype(jnp.bfloat16)
    first_ref[...] = normed
    send(first_ref)
    for part in range(3):
        columns = pl.ds(part * features, features)
        packed_ref[:, columns] = contract(normed, full_ref[:, columns], 1, 0).astype(jnp.bfloat16)
    send(packed_ref)
    valid = lax.broadcasted_iota(jnp.int32, (padded, padded), 1) < SEQ
    lower = lax.broadcasted_iota(jnp.int32, (padded, 2 * HDIM), 1) < HDIM
    for pair in range(features // (2 * HDIM)):
        query = packed_ref[:, pl.ds(pair * 2 * HDIM, 2 * HDIM)]
        keys = packed_ref[:, pl.ds(features + pair * 2 * HDIM, 2 * HDIM)]
        values = packed_ref[:, pl.ds(2 * features + pair * 2 * HDIM, 2 * HDIM)]
        blank = jnp.zeros_like(query)
        results = []
        for query_head in (jnp.where(lower, query, blank), jnp.where(lower, blank, query)):
            probs = head_probs(query_head, keys, valid).astype(jnp.bfloat16)
            results.append(contract(probs, values, 1, 0))
        mixed_ref[:, pl.ds(pair * 2 * HDIM, 2 * HDIM)] = jnp.where(
            lower, results[0], results[1]
        ).astype(jnp.bfloat16)
    send(mixed_ref)
    stream = stream + contract(mixed_ref[...], full_ref[:, pl.ds(3 * features, features)], 1, 0)
    middle_ref[...] = stream
    send(middle_ref)
    normal, _ = layer_norm_parts(stream)
    second_ref[...] = (normal * norm_ref[1:2] + norm_ref[3:4]).astype(jnp.bfloat16)


def attention_backward_kernel(rows, place_ref, *refs):
    (
        full_ref,
        norm_ref,
        start_ref,
        middle_ref,
        first_ref,
        packed_ref,
        mixed_ref,
        grad_ref,
        router_ref,
    ) = refs[:9]
    part_refs = refs[9:-5]
    result_ref, branch_ref, blocks_ref, gpacked_ref, gmixed_ref = refs[-5:]
    features = start_ref.shape[1]
    padded = start_ref.shape[0]
    upstream = part_refs[0][...].astype(jnp.float32)
    for part_ref in part_refs[1:]:
        upstream = upstream + part_ref[...].astype(jnp.float32)
    normal, inverse = layer_norm_parts(middle_ref[...])
    gain_two = jnp.sum(upstream * normal, axis=0, keepdims=True)
    shift_two = jnp.sum(upstream, axis=0, keepdims=True)
    grad_middle = grad_ref[...].astype(jnp.float32) + layer_norm_pull(
        upstream, normal, inverse, norm_ref[1:2]
    )
    grad_attn = grad_middle.astype(jnp.bfloat16)
    gmixed_ref[...] = contract(
        grad_attn, full_ref[:, pl.ds(3 * features, features)], 1, 1
    ).astype(jnp.bfloat16)
    valid = lax.broadcasted_iota(jnp.int32, (padded, padded), 1) < SEQ
    lower = lax.broadcasted_iota(jnp.int32, (padded, 2 * HDIM), 1) < HDIM
    scale = HDIM ** (-0.5)
    for pair in range(features // (2 * HDIM)):
        spans = [pl.ds(part * features + pair * 2 * HDIM, 2 * HDIM) for part in range(3)]
        query, keys, values = [packed_ref[:, span] for span in spans]
        gmixed = gmixed_ref[:, spans[0]]
        blank = jnp.zeros_like(query)
        found = []
        for side in range(2):
            keep = lower if side == 0 else jnp.logical_not(lower)
            probs = head_probs(jnp.where(keep, query, blank), keys, valid)
            grad_probs = contract(jnp.where(keep, gmixed, blank), values, 1, 1)
            grad_values = contract(probs.astype(jnp.bfloat16), gmixed, 0, 0)
            grad_scores = (
                probs * (grad_probs - jnp.sum(probs * grad_probs, axis=1, keepdims=True))
            ).astype(jnp.bfloat16)
            grad_query = contract(grad_scores, keys, 1, 0) * scale
            grad_keys = contract(grad_scores, query, 0, 0) * scale
            found.append((grad_query, grad_keys, grad_values))
        for part in range(3):
            gpacked_ref[:, spans[part]] = jnp.where(lower, found[0][part], found[1][part]).astype(
                jnp.bfloat16
            )
    upstream = contract(gpacked_ref[...], full_ref[:, pl.ds(0, 3 * features)], 1, 1)
    normal, inverse = layer_norm_parts(start_ref[...])
    gain_one = jnp.sum(upstream * normal, axis=0, keepdims=True)
    shift_one = jnp.sum(upstream, axis=0, keepdims=True)
    result = grad_middle + layer_norm_pull(upstream, normal, inverse, norm_ref[0:1])
    result_ref[...] = result
    branch_ref[...] = result.astype(jnp.bfloat16)
    half = features // 2
    strip = features // rows
    extra = jnp.concatenate(
        [
            router_ref[...],
            gain_one,
            gain_two,
            shift_one,
            shift_two,
            jnp.zeros((blocks_ref.shape[2] - 4 * strip - router_ref.shape[0] - 4, features), jnp.float32),
        ],
        axis=0,
    ).astype(jnp.bfloat16)
    grad_proj = contract(mixed_ref[...], grad_attn, 0, 0).astype(jnp.bfloat16)
    for offset in range(rows):
        for side in range(2):
            columns = slice(side * half, (side + 1) * half)
            blocks_ref[side, offset, pl.ds(3 * strip, strip), :] = grad_proj[
                offset * strip : (offset + 1) * strip, columns
            ]
            blocks_ref[side, offset, pl.ds(4 * strip, extra.shape[0]), :] = extra[:, columns]
    for part in range(3):
        grad_part = contract(
            gpacked_ref[:, pl.ds(part * features, features)], first_ref[...], 0, 0
        ).astype(jnp.bfloat16)
        for offset in range(rows):
            for side in range(2):
                blocks_ref[side, offset, pl.ds(part * strip, strip), :] = grad_part[
                    offset * strip : (offset + 1) * strip, side * half : (side + 1) * half
                ]


def dispatch_kernel(room, codes_ref, *refs):
    groups = codes_ref.shape[1]
    block_refs, out_refs = refs[:-groups], refs[-groups:]
    padded = block_refs[0].shape[0]
    rows_of = lax.broadcasted_iota(jnp.int32, (room, padded), 0)
    for group in range(groups):
        total = jnp.zeros((room, block_refs[0].shape[1]), jnp.float32)
        for image, block_ref in enumerate(block_refs):
            picks = (codes_ref[image, group : group + 1, :] == rows_of).astype(jnp.float32)
            total = total + contract(picks.astype(jnp.bfloat16), block_ref[...], 1, 0)
        out_refs[group][...] = total.astype(jnp.bfloat16)


def combine_kernel(rows, codes_ref, *refs):
    slot_refs, out_refs = refs[: codes_ref.shape[1]], refs[codes_ref.shape[1] :]
    room = slot_refs[0].shape[0]
    padded = out_refs[0].shape[0]
    lanes = lax.broadcasted_iota(jnp.int32, (padded, room), 1)
    for image in range(rows):
        total = jnp.zeros(out_refs[0].shape, jnp.float32)
        for source, slot_ref in enumerate(slot_refs):
            codes = codes_ref[pl.ds(image * padded, padded), source : source + 1]
            picks = (codes == lanes).astype(jnp.float32)
            total = total + contract(picks.astype(jnp.bfloat16), slot_ref[...], 1, 0)
        out_refs[image][...] = total.astype(jnp.bfloat16)


def expert_router(place_ref, buffer, wrouter):
    router = softmax_rows(contract(buffer, wrouter, 1, 1))
    chosen = lax.broadcasted_iota(jnp.int32, router.shape, 1) == place_ref[3]
    gate = jnp.sum(jnp.where(chosen, router, 0.0), axis=1, keepdims=True)
    return (router, chosen, gate)


def expert_forward_kernel(groups, place_ref, wrouter_ref, win_ref, wout_ref, *refs):
    buffer = jnp.concatenate([ref[...] for ref in refs[:groups]], axis=0)
    room = refs[0].shape[0]
    half = buffer.shape[1] // 2
    _, _, gate = expert_router(place_ref, buffer, wrouter_ref[...])
    sums = [jnp.zeros((buffer.shape[0], half), jnp.float32) for _ in range(2)]
    for quarter in range(win_ref.shape[0] // 2):
        hidden = contract(buffer[:, :half], win_ref[2 * quarter], 1, 0) + contract(
            buffer[:, half:], win_ref[2 * quarter + 1], 1, 0
        )
        active = gelu_parts(hidden)[0].astype(jnp.bfloat16)
        for side in range(2):
            sums[side] = sums[side] + contract(active, wout_ref[2 * quarter + side], 1, 0)
    for group in range(groups):
        span = slice(group * room, (group + 1) * room)
        for side in range(2):
            refs[groups + group][:, pl.ds(side * half, half)] = (
                gate[span] * sums[side][span]
            ).astype(jnp.bfloat16)


def expert_full_kernel(groups, with_output, place_ref, wrouter_ref, win_ref, wout_ref, *refs):
    buffer = jnp.concatenate([ref[...] for ref in refs[:groups]], axis=0)
    grads = jnp.concatenate([ref[...] for ref in refs[groups : 2 * groups]], axis=0)
    back_refs = refs[2 * groups : 3 * groups]
    out_refs = refs[3 * groups : -3]
    gin_ref, gout_ref, grouter_ref = refs[-3:]
    room = refs[0].shape[0]
    half = buffer.shape[1] // 2
    router, chosen, gate = expert_router(place_ref, buffer, wrouter_ref[...])
    grad_slot = (gate * grads.astype(jnp.float32)).astype(jnp.bfloat16)
    flipped = buffer.T
    sums = [jnp.zeros((buffer.shape[0], half), jnp.float32) for _ in range(2)]
    backs = [jnp.zeros((buffer.shape[0], half), jnp.float32) for _ in range(2)]
    grad_gate = jnp.zeros((buffer.shape[0], 1), jnp.float32)
    for quarter in range(win_ref.shape[0] // 2):
        hidden = contract(buffer[:, :half], win_ref[2 * quarter], 1, 0) + contract(
            buffer[:, half:], win_ref[2 * quarter + 1], 1, 0
        )
        value, slope = gelu_parts(hidden)
        active = value.astype(jnp.bfloat16)
        if with_output:
            for side in range(2):
                sums[side] = sums[side] + contract(active, wout_ref[2 * quarter + side], 1, 0)
        pulled = contract(grads[:, :half], wout_ref[2 * quarter], 1, 1) + contract(
            grads[:, half:], wout_ref[2 * quarter + 1], 1, 1
        )
        grad_gate = grad_gate + jnp.sum(
            pulled * active.astype(jnp.float32), axis=1, keepdims=True
        )
        grad_hidden = (gate * pulled * slope).astype(jnp.bfloat16)
        turned = active.T
        for side in range(2):
            block = 2 * quarter + side
            span = slice(side * half, (side + 1) * half)
            backs[side] = backs[side] + contract(grad_hidden, win_ref[block], 1, 1)
            gin_ref[block] = contract(flipped[span], grad_hidden, 1, 0).astype(jnp.bfloat16)
            gout_ref[block] = contract(turned, grad_slot[:, span], 1, 0).astype(jnp.bfloat16)
    grad_logits = (
        router * (jnp.where(chosen, grad_gate, 0.0) - gate * grad_gate)
    ).astype(jnp.bfloat16)
    grouter_ref[...] = contract(grad_logits, buffer, 0, 0)
    router_back = contract(grad_logits, wrouter_ref[...], 1, 0)
    for group in range(groups):
        span = slice(group * room, (group + 1) * room)
        for side in range(2):
            columns = slice(side * half, (side + 1) * half)
            back_refs[group][:, columns] = (
                backs[side][span] + router_back[span, columns]
            ).astype(jnp.bfloat16)
            if with_output:
                out_refs[group][:, columns] = (gate[span] * sums[side][span]).astype(jnp.bfloat16)


SMALL = pl.BlockSpec(memory_space=pltpu.SMEM)
LOCAL = pl.BlockSpec(memory_space=pltpu.VMEM)
FAR = pl.BlockSpec(memory_space=pltpu.HBM)


def widen_kernel(narrow_ref, *refs):
    refs[-1][0, 0] = narrow_ref[0].astype(jnp.float32)


def widen_grads(layer, layer_count, narrow, previous):
    members, *block = narrow.shape
    anywhere = pl.BlockSpec(memory_space=pl.ANY)
    return pl.pallas_call(
        widen_kernel,
        name="widen",
        grid=(members,),
        in_specs=[pl.BlockSpec((1, *block), lambda step: (step, 0, 0))]
        + [anywhere] * len(previous),
        out_specs=pl.BlockSpec((1, 1, *block), lambda step: (layer, step, 0, 0)),
        out_shape=jax.ShapeDtypeStruct((layer_count, members, *block), jnp.float32),
        input_output_aliases={1: 0} if previous else {},
        compiler_params=pltpu.CompilerParams(vmem_limit_bytes=4 * 1024 * 1024),
    )(narrow, *previous)


class Staged:
    def __init__(self, ref, move=None):
        self.ref, self.move = ref, move
        self.shape, self.dtype = ref.shape, ref.dtype

    def wait(self):
        if self.move is not None:
            self.move.wait()
            self.move = None

    def __getitem__(self, index):
        self.wait()
        return self.ref[index]


class Sent:
    def __init__(self, ref, move):
        self.ref, self.move, self.moving = ref, move, False
        self.shape, self.dtype = ref.shape, ref.dtype

    def __getitem__(self, index):
        return self.ref[index]

    def __setitem__(self, index, values):
        self.ref[index] = values

    def send(self):
        if not self.moving:
            self.move.start()
            self.moving = True


def send(ref):
    if isinstance(ref, Sent):
        ref.send()


def staged_body(body, fixed_count, staged, far, *refs):
    fixed, refs = refs[:fixed_count], refs[fixed_count:]
    sources, refs = list(refs[: len(staged)]), refs[len(staged) :]
    targets, refs = list(refs[: len(far)]), refs[len(far) :]
    copies, refs = list(refs[: sum(staged)]), refs[sum(staged) :]
    made, refs = list(refs[: sum(far)]), refs[sum(far) :]
    marks, scratch = refs[0], refs[1:]
    for place, moved in enumerate(staged):
        if moved:
            copy = copies.pop(0)
            move = pltpu.make_async_copy(sources[place], copy, marks.at[place])
            sources[place] = Staged(copy, move)
    waiting = [source for source in sources if isinstance(source, Staged)]
    for source in sorted(waiting, key=lambda source: math.prod(source.shape)):
        source.move.start()
    for place, apart in enumerate(far):
        if apart:
            source = made.pop(0)
            move = pltpu.make_async_copy(source, targets[place], marks.at[len(staged) + place])
            targets[place] = Sent(source, move)
    body(*fixed, *sources, *targets, *scratch)
    for source in sources:
        if isinstance(source, Staged):
            source.wait()
    for target in targets:
        send(target)
    for target in targets:
        if isinstance(target, Sent):
            target.move.wait()


def run_kernel(
    title, body, place, operands, results, work, scratch=(), room=16, near=(), far=()
):
    fixed = [] if place is None else [place]
    staged = [place not in near for place in range(len(operands))]
    arguments = fixed + [
        pltpu.with_memory_space_constraint(piece, pltpu.HBM) if moved else piece
        for moved, piece in zip(staged, operands)
    ]
    apart = [place in far for place in range(len(results))]
    return pl.pallas_call(
        functools.partial(staged_body, body, len(fixed), staged, apart),
        name=title,
        in_specs=[SMALL] * len(fixed) + [FAR if moved else LOCAL for moved in staged],
        out_specs=[FAR if away else LOCAL for away in apart],
        out_shape=[
            pltpu.HBM(shape, kind) if away else jax.ShapeDtypeStruct(shape, kind)
            for away, (shape, kind) in zip(apart, results)
        ],
        scratch_shapes=[
            pltpu.VMEM(piece.shape, piece.dtype) for moved, piece in zip(staged, operands) if moved
        ]
        + [pltpu.VMEM(shape, kind) for away, (shape, kind) in zip(apart, results) if away]
        + [pltpu.SemaphoreType.DMA((len(operands) + len(results),))]
        + list(scratch),
        compiler_params=pltpu.CompilerParams(vmem_limit_bytes=room * 1024 * 1024),
        cost_estimate=pl.CostEstimate(
            flops=work // 4,
            bytes_accessed=sum(piece.size * piece.dtype.itemsize for piece in arguments),
            transcendentals=0,
        ),
    )(*arguments)


def after(values, *earlier):
    return lax.optimization_barrier((values, *earlier))[0]


def gather_group(values):
    near = [values]
    for offset in range(1, lax.axis_size("row")):
        near.append(exchange(values, "row", offset))
    return near + [exchange(piece, "col", 1) for piece in near]


def scatter_pieces(pieces, axis):
    return [
        piece if offset == 0 else exchange(piece, axis, offset)
        for offset, piece in enumerate(pieces)
    ]


def add_pieces(pieces):
    total = pieces[0].astype(jnp.float32)
    for piece in pieces[1:]:
        total = total + piece.astype(jnp.float32)
    return total


def sum_chip(blocks, at_col):
    mine = lax.dynamic_index_in_dim(blocks, at_col, 0, keepdims=False)
    other = exchange(lax.dynamic_index_in_dim(blocks, 1 - at_col, 0, keepdims=False), "col", 1)
    return add_pieces([mine, other]).astype(blocks.dtype)


def sum_groups(plane):
    groups, at_dp = lax.axis_size("dp"), lax.axis_index("dp")
    part = plane.shape[0] // groups
    pieces = [
        lax.dynamic_slice_in_dim(plane, (at_dp ^ offset) * part, part, 0)
        for offset in range(groups)
    ]
    owned = add_pieces(scatter_pieces(pieces, "dp")).astype(plane.dtype)
    result = jnp.zeros(plane.shape, jnp.float32)
    for offset in range(groups):
        piece = owned if offset == 0 else exchange(owned, "dp", offset)
        result = lax.dynamic_update_slice_in_dim(
            result, piece.astype(jnp.float32), (at_dp ^ offset) * part, 0
        )
    return result


def group_device(
    tokens,
    norm_gain,
    norm_shift,
    w_qkv,
    w_proj,
    w_router,
    w_in,
    w_out,
    expert_ids,
    slot_ids,
    cotangent,
):
    low = jnp.bfloat16
    groups, rows = lax.axis_size("dp"), lax.axis_size("row")
    members = 2 * rows
    at_dp, at_row, at_col = [lax.axis_index(name) for name in ("dp", "row", "col")]
    layer_count = w_qkv.shape[0]
    expert_count = w_in.shape[1]
    half = tokens.shape[1]
    features = 2 * half
    strip = features // rows
    padded = -(-SEQ // 16) * 16
    owner = at_dp * members + at_row * 2 + at_col
    place = jnp.stack([at_dp, at_row, at_col, owner]).astype(jnp.int32)

    def join(mine, other):
        return jnp.where(
            at_col == 0,
            jnp.concatenate([mine, other], axis=-1),
            jnp.concatenate([other, mine], axis=-1),
        )

    small = jnp.concatenate(
        [
            jnp.concatenate([norm_gain, norm_shift], axis=1).reshape(-1, half),
            w_router.transpose(0, 2, 1).reshape(-1, half).astype(jnp.float32),
        ],
        axis=0,
    )
    small = join(small, exchange(small, "col", 1))
    norms = small[: 4 * layer_count].reshape(layer_count, 4, features)
    routers = small[4 * layer_count :].reshape(layer_count, expert_count, features).astype(low)
    both = jnp.stack([tokens, cotangent]).reshape(2, 2, SEQ, half)
    mine = lax.dynamic_index_in_dim(both, at_col, 1, keepdims=False)
    other = exchange(lax.dynamic_index_in_dim(both, 1 - at_col, 1, keepdims=False), "col", 1)
    both = jnp.pad(join(mine, other), ((0, 0), (0, padded - SEQ), (0, 0)))

    def fetch_attention(layer, *earlier):
        block = jnp.concatenate(
            [
                w_qkv[layer].reshape(half, -1),
                jnp.concatenate(
                    [
                        w_proj[layer][:, piece * strip : (piece + 1) * strip]
                        for piece in range(half // strip)
                    ],
                    axis=0,
                ),
            ],
            axis=1,
        )
        return gather_group(after(block, *earlier) if earlier else block)

    def own_experts(layer, source):
        own = lax.dynamic_slice(
            source, (layer, at_dp * members, 0, 0), (1, members, *source.shape[2:])
        )
        return own[0]

    def fetch_weights(own, *earlier):
        return lax.all_to_all(
            after(own, *earlier), ("row", "col"), split_axis=0, concat_axis=0, tiled=True
        )

    capacity = 2 * ((5 * members * SEQ + 4 * expert_count - 1) // (4 * expert_count))
    room = -(-capacity // 16) * 16
    images = jnp.stack(
        [(at_row ^ offset) * 2 + (at_col ^ side) for side in range(2) for offset in range(rows)]
    )
    named = jnp.stack(
        [
            (at_dp ^ offset) * members + at_row * 2 + (at_col ^ side)
            for side in range(2)
            for offset in range(groups)
        ]
    )
    chosen = jnp.take(expert_ids.reshape(layer_count, members, SEQ, -1), images, axis=1)
    slots = jnp.take(slot_ids.reshape(layer_count, members, SEQ, -1), images, axis=1)
    codes = jnp.max(
        jnp.where(chosen[..., None] == named, slots[..., None], -1), axis=3
    )
    codes = jnp.pad(codes, ((0, 0), (0, 0), (0, padded - SEQ), (0, 0)), constant_values=-1)
    send_codes = codes[..., :groups].transpose(0, 1, 3, 2)
    back_codes = codes[:, :rows].reshape(layer_count, rows * padded, 2 * groups)

    token_block = ((padded, features), low)
    slot_block = ((room, features), low)

    def after_all(pieces, *earlier):
        return [after(piece, *earlier) for piece in pieces]

    def dispatch(layer, images):
        return run_kernel(
            "dispatch",
            functools.partial(dispatch_kernel, room),
            None,
            [send_codes[layer]] + images,
            [slot_block] * groups,
            2 * members * padded * groups * room * features,
            near=range(1, 1 + len(images)),
        )

    def bring_back(blocks, *earlier):
        blocks = after_all(scatter_pieces(blocks, "dp"), *earlier)
        return blocks + [exchange(piece, "col", 1) for piece in blocks]

    def combine(layer, blocks):
        return run_kernel(
            "combine",
            functools.partial(combine_kernel, rows),
            None,
            [back_codes[layer]] + blocks,
            [token_block] * rows,
            4 * rows * padded * groups * room * features,
        )

    def split(values):
        pieces = values[:SEQ].reshape(SEQ, 2, half)
        mine = lax.dynamic_index_in_dim(pieces, at_col, 1, keepdims=False)
        other = exchange(lax.dynamic_index_in_dim(pieces, 1 - at_col, 1, keepdims=False), "col", 1)
        return jnp.where(
            at_col == 0,
            jnp.concatenate([mine, other], axis=0),
            jnp.concatenate([other, mine], axis=0),
        )

    work = 4 * groups * room * members * half * w_in.shape[3]
    stream, parts = both[0], []
    kept, buffers, weights = [], [], []
    attention_blocks = fetch_attention(0)
    ready = attention_blocks[1:rows]
    for layer in range(layer_count):
        last = layer == layer_count - 1
        weight_in = fetch_weights(own_experts(layer, w_in), *ready)
        own_out = own_experts(layer, w_out)
        upstream = []
        if last:
            upstream = gather_group(after(both[1], *parts[1:]))
        saved = run_kernel(
            "attention_forward",
            functools.partial(attention_forward_kernel, rows),
            place,
            attention_blocks + [norms[layer], stream] + parts,
            [
                ((padded, features), jnp.float32),
                ((padded, features), jnp.float32),
                token_block,
                ((padded, 3 * features), low),
                token_block,
                token_block,
                ((features, 4 * features), low),
            ],
            16 * padded * features * features,
            far=(0, 1, 2, 3, 4, 6),
        )
        kept.append(saved)
        stream = saved[1]
        images = gather_group(saved[5])
        weight_out = fetch_weights(own_out, *images[1:rows], *upstream[1:rows])
        weights.append([weight_in, weight_out])
        if last:
            sent = dispatch(layer, upstream)
            branches = scatter_pieces(sent, "dp")
            images = after_all(images, sent[0])
        buffers.append(scatter_pieces(dispatch(layer, images), "dp"))
        if not last:
            result = run_kernel(
                "expert_forward",
                functools.partial(expert_forward_kernel, groups),
                place,
                [routers[layer]] + weights[layer] + buffers[layer],
                [slot_block] * groups,
                work,
            )
            ready = [result[0]]
            attention_blocks = fetch_attention(layer + 1, result[0])
            parts = scatter_pieces(combine(layer, bring_back(result)), "row")
    grad = both[1]
    shared = [None] * layer_count
    grad_in, grad_out = [], []
    for layer in reversed(range(layer_count)):
        last = layer == layer_count - 1
        found = run_kernel(
            "expert_full",
            functools.partial(expert_full_kernel, groups, last),
            place,
            [routers[layer]] + weights[layer] + buffers[layer] + branches,
            [slot_block] * (2 * groups if last else groups)
            + [
                (weights[layer][0].shape, low),
                (weights[layer][1].shape, low),
                ((expert_count, features), jnp.float32),
            ],
            3 * work,
            room=24,
        )
        if last:
            moved_in = fetch_weights(found[-3])
            blocks = bring_back(list(found[:groups]))
        else:
            arrived = scatter_pieces(chip, "row")
            moved_in = fetch_weights(found[-3], moved_out, *arrived[1:])
            moved_out = after(moved_out, found[0])
            grad_out = [widen_grads(layer + 1, layer_count, moved_out, grad_out)]
            blocks = bring_back(list(found[:groups]), *grad_out)
            earlier = add_pieces(arrived).astype(low)
        pieces = combine(layer, blocks)
        if last:
            outputs = bring_back(after_all(list(found[groups : 2 * groups]), pieces[0]))
        grad_parts = scatter_pieces(after_all(pieces, moved_in), "row")
        if last:
            grad_parts[0] = after(grad_parts[0], *outputs[1:groups])
        saved = kept[layer]
        height = -(-(4 * strip + expert_count + 4) // (16 * groups)) * (16 * groups)
        grad, branch, blocks = run_kernel(
            "attention_backward",
            functools.partial(attention_backward_kernel, rows),
            place,
            [saved[6], norms[layer], saved[0], saved[1], saved[2], saved[3], saved[4], grad]
            + [found[-1]]
            + grad_parts,
            [
                ((padded, features), jnp.float32),
                token_block,
                ((2, rows, height, half), low),
            ],
            32 * padded * features * features,
            [pltpu.VMEM((padded, 3 * features), low), pltpu.VMEM((padded, features), low)],
        )
        chip = list(sum_chip(blocks, at_col))
        if layer > 0:
            images = gather_group(branch)
            moved_out = fetch_weights(found[-2], *images[1:rows])
            sent = dispatch(layer - 1, images)
            branches = scatter_pieces(sent, "dp")
            moved_in = after(moved_in, sent[0])
            grad_in = [widen_grads(layer, layer_count, moved_in, grad_in)]
            if last:
                outputs = combine(layer, after_all(outputs, sent[0]))
            branches = after_all(branches, *grad_in, *outputs, *chip)
        else:
            arrived = scatter_pieces(chip, "row")
            moved_out = fetch_weights(found[-2], *arrived[1:])
            grad_in = [widen_grads(layer, layer_count, after(moved_in, chip[0]), grad_in)]
            outputs = scatter_pieces(after_all(outputs, chip[0]), "row")
            for part in outputs:
                stream = stream + part.astype(jnp.float32)
            output = split(stream.astype(low))
            arrived = after_all(arrived, *grad_in)
            grad_out = [widen_grads(layer, layer_count, moved_out, grad_out)]
            both_sums = jnp.concatenate([add_pieces(arrived).astype(low), earlier], axis=1)
            both_sums = sum_groups(both_sums)
            shared = [both_sums[:, :half], both_sums[:, half:]]
    grad_input = split(grad)
    shared = jnp.stack(shared)
    grad_qkv = (
        shared[:, : 3 * strip].reshape(layer_count, 3, strip, half).transpose(0, 3, 1, 2)
    )
    grad_proj = shared[:, 3 * strip : 4 * strip]
    grad_router = shared[:, 4 * strip : 4 * strip + expert_count].transpose(0, 2, 1)
    tail = shared[:, 4 * strip + expert_count : 4 * strip + expert_count + 4]
    return (
        output,
        grad_input,
        grad_qkv,
        grad_proj,
        grad_router,
        grad_in[0],
        grad_out[0],
        tail[:, :2],
        tail[:, 2:],
    )


def fits_groups(mesh, tokens, w_in):
    groups, rows, sides = mesh.shape["dp"], mesh.shape["row"], mesh.shape["col"]
    powers = all(size & (size - 1) == 0 for size in (groups, rows))
    return (
        sides == 2
        and powers
        and tokens.shape[0] == groups * rows * sides * SEQ
        and w_in.shape[1] == groups * rows * sides
    )


def solution(mesh):
    in_specs = (
        P(("dp", "row"), "col"),
        P(None, None, "col"),
        P(None, None, "col"),
        P(None, "col", None, "row"),
        P(None, "row", "col"),
        P(None, "col", None),
        P(None, None, "col", "row"),
        P(None, None, "row", "col"),
        P(None, "dp", None),
        P(None, "dp", None),
        P(("dp", "row"), "col"),
    )
    out_specs = (
        P(("dp", "row"), "col"),
        P(("dp", "row"), "col"),
        P(None, "col", None, "row"),
        P(None, "row", "col"),
        P(None, "col", None),
        P(None, "dp", "col", "row"),
        P(None, "dp", "row", "col"),
        P(None, None, "col"),
        P(None, None, "col"),
    )

    def program(*arguments):
        fits = fits_groups(mesh, arguments[0], arguments[6])
        return jax.shard_map(
            group_device if fits else per_device,
            mesh=mesh,
            in_specs=in_specs,
            out_specs=out_specs,
            check_vma=False,
        )(*arguments)

    return program
```
